32 devices in a mesh: tensor: 2 (over core), dp: 4 (over z), ctx: 4 (over y, x).
Axes of the slice: x: 2, y: 2, z: 4, core: 2. Of those that a mesh axis runs over, the one named last changes fastest.
Arguments:
- tokens: bfloat16 [4, 1024, 2560], P('dp', 'ctx'), may hold values from -6 to 6
- segments: int32 [4, 1024], P('dp'), may hold values from 0 to 2, as said below
- gain_attn: bfloat16 [2560], replicated, may hold values from 0.5 to 1.5
- w_qa: bfloat16 [2560, 768], replicated, may hold values from -0.125 to 0.125
- gain_q: bfloat16 [768], replicated, may hold values from 0.5 to 1.5
- w_kva: bfloat16 [2560, 288], replicated, may hold values from -0.125 to 0.125
- gain_kv: bfloat16 [256], replicated, may hold values from 0.5 to 1.5
- w_qb: bfloat16 [768, 3840], P(None, 'tensor'), may hold values from -0.3125 to 0.3125
- w_kvb: bfloat16 [256, 5120], P(None, 'tensor'), may hold values from -0.375 to 0.375
- w_o: bfloat16 [2560, 2560], P(('dp', 'ctx'), 'tensor'), may hold values from -3 to 3
- gain_mlp: bfloat16 [2560], replicated, may hold values from 0.5 to 1.5
- w_gate: bfloat16 [2560, 6400], P(('dp', 'ctx'), 'tensor'), may hold values from -0.125 to 0.125
- w_up: bfloat16 [2560, 6400], P(('dp', 'ctx'), 'tensor'), may hold values from -0.125 to 0.125
- w_down: bfloat16 [2560, 6400], P(('dp', 'ctx'), 'tensor'), may hold values from -0.625 to 0.625
- cotangent: bfloat16 [4, 1024, 2560], P('dp', 'ctx'), may hold values from -6 to 6
Outputs:
- layer_out: bfloat16 [4, 1024, 2560], P('dp', 'ctx')
- grad_tokens: bfloat16 [4, 1024, 2560], P('dp', 'ctx')
- grad_gain_attn: float32 [2560], replicated
- grad_w_qa: float32 [2560, 768], P(('dp', 'ctx'))
- grad_gain_q: float32 [768], replicated
- grad_w_kva: float32 [2560, 288], P(('dp', 'ctx'))
- grad_gain_kv: float32 [256], replicated
- grad_w_qb: float32 [768, 3840], P(None, 'tensor')
- grad_w_kvb: float32 [256, 5120], P(None, 'tensor')
- grad_w_o: float32 [2560, 2560], P(('dp', 'ctx'), 'tensor')
- grad_gain_mlp: float32 [2560], replicated
- grad_w_gate: float32 [2560, 6400], P(('dp', 'ctx'), 'tensor')
- grad_w_up: float32 [2560, 6400], P(('dp', 'ctx'), 'tensor')
- grad_w_down: float32 [2560, 6400], P(('dp', 'ctx'), 'tensor')
The draws below stay inside these ranges and needn't reach their ends.
Inputs may be any that keep to these rules, and one draw needn't show every extreme that they name: `segments`: in each sequence the segment numbers start at 0, never fall, rise by at most one from a token to the next, and the last token has number 2.
All inputs are finite; a program needn't handle non-finite values.
Results may differ from the reference program's by a relative error of at most 0.02.
Values may be sent and summed in bfloat16 or wider, within the bound.
No kernel may reach another device: no remote copies, remote signals or barrier semaphores. Data moves between devices by JAX's collectives and lax.ppermute only.
A program may use at most 640 MiB of HBM per device.

```python
import math
import jax
import jax.numpy as jnp
from jax import lax

D = 2560
HEADS = 40
NOPE = 64
ROPE = 32
VDIM = 64
QRANK = 768
KVRANK = 256
FF = 6400
SPAN = 256
SEQ_LEN = 1024
SEQS = 4


def draw_segments(key, part):
    key = jax.random.fold_in(key, 11)
    key_long, key_first = jax.random.split(key, 2)
    longest = jax.random.randint(key_long, (SEQS,), SEQ_LEN - SPAN + 2, SEQ_LEN - 1)
    first = jax.random.randint(key_first, (SEQS,), 1, SEQ_LEN - longest)
    index = jnp.arange(SEQ_LEN, dtype=jnp.int32)[None, :]
    ending = (first + longest)[:, None]
    breaks = (index == first[:, None]) | (index == ending)
    return jnp.cumsum(breaks.astype(jnp.int32), axis=1)


def shard_levels(own_key, dims, shards, least, largest):
    gain = 1.0
    for dim, shards_of in shards:
        heights = jax.random.uniform(jax.random.fold_in(jax.random.fold_in(own_key, 6), dim), (shards_of,), jnp.float32, least / len(shards), largest / len(shards))
        gain = gain * jnp.repeat(jnp.exp(heights), dims[dim] // shards_of).reshape((-1,) + (1,) * (len(dims) - 1 - dim))
    return gain


def scatter_about(rng, dims, scale, limit, cuts=(), held_as=jnp.bfloat16):
    loudness = shard_levels(rng, dims, cuts, -0.22, 0.18) if cuts else 1.0
    values = jax.random.normal(rng, dims, jnp.float32) * scale * loudness
    return jnp.minimum(jnp.maximum(values, -limit), limit).astype(held_as)


def setup_inputs(seed: int = 0) -> dict:
    arg_keys = jax.random.split(jax.random.key(seed), 16)
    return {
        "tokens": scatter_about(arg_keys[0], (SEQS, SEQ_LEN, D), 1.0, 6.0, ((0, 4), (1, 4))),
        "segments": draw_segments(jax.random.fold_in(arg_keys[15], 71), 0),
        "gain_attn": jnp.clip(1.0 + 0.1 * jax.random.normal(arg_keys[2], (D,), jnp.float32), 0.5, 1.5).astype(jnp.bfloat16),
        "w_qa": scatter_about(arg_keys[3], (D, QRANK), D ** -0.5, 0.125),
        "gain_q": jnp.clip(1.0 + 0.1 * jax.random.normal(arg_keys[4], (QRANK,), jnp.float32), 0.5, 1.5).astype(jnp.bfloat16),
        "w_kva": scatter_about(arg_keys[5], (D, KVRANK + ROPE), D ** -0.5, 0.125),
        "gain_kv": jnp.clip(1.0 + 0.1 * jax.random.normal(arg_keys[6], (KVRANK,), jnp.float32), 0.5, 1.5).astype(jnp.bfloat16),
        "w_qb": scatter_about(arg_keys[7], (QRANK, HEADS * (NOPE + ROPE)), (QRANK // 2) ** -0.5, 0.3125, ((1, 2),)),
        "w_kvb": scatter_about(arg_keys[8], (KVRANK, HEADS * (NOPE + VDIM)), KVRANK ** -0.5, 0.375, ((1, 2),)),
        "w_o": scatter_about(arg_keys[9], (D, HEADS * VDIM), (max(2, HEADS * VDIM // 640)) ** -0.5, 3.0, ((0, 16), (1, 2))),
        "gain_mlp": jnp.clip(1.0 + 0.1 * jax.random.normal(arg_keys[10], (D,), jnp.float32), 0.5, 1.5).astype(jnp.bfloat16),
        "w_gate": scatter_about(arg_keys[11], (D, FF), D ** -0.5, 0.125, ((0, 16), (1, 2))),
        "w_up": scatter_about(arg_keys[12], (D, FF), D ** -0.5, 0.125, ((0, 16), (1, 2))),
        "w_down": scatter_about(arg_keys[13], (D, FF), (FF // 64) ** -0.5, 0.625, ((0, 16), (1, 2))),
        "cotangent": scatter_about(arg_keys[14], (SEQS, SEQ_LEN, D), 1.0, 6.0, ((0, 4), (1, 4))),
    }


@jax.custom_vjp
def low(v):
    return lax.optimization_barrier(v.astype(jnp.bfloat16)).astype(jnp.float32)

@jax.custom_vjp
def low_back(v):
    return v

def low_keep(v):
    return (low(v), None)

def low_pass(kept, grad):
    return (grad,)

def back_keep(v):
    return (v, None)

def back_low(kept, grad):
    return (low(grad),)
low.defvjp(low_keep, low_pass)
low_back.defvjp(back_keep, back_low)
eps_norm = 1e-05
res_scale = 1.4 / math.sqrt(62.0)
rope_base = 10000.0
masked_score = -1e+30
precise = lax.Precision.HIGHEST

def rms_scale(values):
    return values * lax.rsqrt(lax.optimization_barrier(jnp.mean(values * values, axis=-1, keepdims=True)) + eps_norm)

def rotate(values, cosine, sine):
    half = values.shape[-1] // 2
    turned = jnp.concatenate([-values[..., half:], values[..., :half]], axis=-1)
    return values * cosine + turned * sine

def rotary_tables(positions):
    freqs = rope_base ** (-jnp.arange(0, ROPE, 2).astype(jnp.float32) / ROPE)
    angles = positions.astype(jnp.float32)[:, None] * freqs[None, :]
    angles = jnp.concatenate([angles, angles], axis=1)
    return (jnp.cos(angles), jnp.sin(angles))

def matmul_high(left, right):
    return jnp.dot(left, right, precision=precise, preferred_element_type=jnp.float32)

def layer_one(hidden_in, segment_ids, gain_attn, w_qa, gain_q, w_kva, gain_kv, w_qb, w_kvb, w_o, gain_mlp, w_gate, w_up, w_down):
    length = hidden_in.shape[0]
    index = jnp.arange(length, dtype=jnp.int32)
    doc_start = lax.optimization_barrier(jnp.sum((segment_ids[None, :] < segment_ids[:, None]).astype(jnp.int32), axis=1))
    cosine, sine = rotary_tables(index - doc_start)
    allowed = (segment_ids[:, None] == segment_ids[None, :]) & (index[None, :] <= index[:, None])
    scaled_in = rms_scale(hidden_in)
    normed_in = low(scaled_in * gain_attn)
    q_latent = low_back(matmul_high(normed_in, w_qa))
    q_normed = low(rms_scale(q_latent) * gain_q)
    kv_latent = low_back(matmul_high(normed_in, w_kva))
    c_round = low(rms_scale(kv_latent[:, :KVRANK]))
    c_normed = low(c_round * gain_kv)
    key_rope = low(rotate(kv_latent[:, KVRANK:], cosine, sine))
    q_raw = low_back(matmul_high(q_normed, w_qb)).reshape(length, HEADS, NOPE + ROPE)
    q_rot = low(jnp.concatenate([q_raw[..., :NOPE], rotate(q_raw[..., NOPE:], cosine[:, None, :], sine[:, None, :])], axis=-1))
    kv_heads = low(matmul_high(c_normed, w_kvb)).reshape(length, HEADS, NOPE + VDIM)
    keys = jnp.concatenate([kv_heads[..., :NOPE], jnp.broadcast_to(key_rope[:, None, :], (length, HEADS, ROPE))], axis=-1)
    value_heads = kv_heads[..., NOPE:]
    group = math.gcd(HEADS, 8)
    count_groups = HEADS // group
    score_scale = 1.0 / math.sqrt(NOPE + ROPE)

    def by_group(array):
        return array.reshape(length, count_groups, group, array.shape[2]).transpose(1, 0, 2, 3)

    def attend(parts):
        q_block, k_block, v_block = parts
        scores = low_back(jnp.einsum('qhd,khd->hqk', q_block, k_block, precision=precise) * score_scale)
        scores = jnp.where(allowed[None], scores, masked_score)
        highest = lax.optimization_barrier(jnp.max(scores, axis=-1, keepdims=True))
        weights = jnp.exp(scores - highest)
        probs = weights / lax.optimization_barrier(jnp.sum(weights, axis=-1, keepdims=True))
        return jnp.einsum('hqk,khd->qhd', low(probs), v_block, precision=precise)
    mixed = lax.map(jax.checkpoint(attend), (by_group(q_rot), by_group(keys), by_group(value_heads)))
    heads_out = low(low_back(mixed.transpose(1, 0, 2, 3).reshape(length, HEADS * VDIM)))
    attn = low_back(matmul_high(heads_out, w_o.T))
    resid = hidden_in + res_scale * attn
    normed_mid = low(rms_scale(resid) * gain_mlp)
    gate = low_back(matmul_high(normed_mid, w_gate))
    up_proj = low_back(matmul_high(normed_mid, w_up))
    hidden_mid = low(gate * jax.nn.sigmoid(gate) * up_proj)
    mlp = low_back(matmul_high(hidden_mid, w_down.T))
    return resid + res_scale * mlp

def reference(tokens, segments, gain_attn, w_qa, gain_q, w_kva, gain_kv, w_qb, w_kvb, w_o, gain_mlp, w_gate, w_up, w_down, cotangent):
    floats = tuple((array.astype(jnp.float32) for array in (tokens, gain_attn, w_qa, gain_q, w_kva, gain_kv, w_qb, w_kvb, w_o, gain_mlp, w_gate, w_up, w_down)))

    def forward(hidden_all, *weights):

        def one_sequence(pair):
            return layer_one(pair[0], pair[1], *weights)
        return lax.map(one_sequence, (hidden_all, segments))
    result, pullback = jax.vjp(forward, *floats)
    grads = pullback(cotangent.astype(jnp.float32))
    return (result.astype(jnp.bfloat16), grads[0].astype(jnp.bfloat16), grads[1], grads[2], grads[3], grads[4], grads[5], grads[6], grads[7], grads[8], grads[9], grads[10], grads[11], grads[12])
```

```python
import functools
import math

import jax
import jax.numpy as jnp
import numpy as np
from jax import lax
from jax.experimental import pallas as pl
from jax.experimental.pallas import tpu as pltpu
from jax.sharding import PartitionSpec as P

NOPE = 64
ROPE = 32
VDIM = 64
KVRANK = 256
LANES = 128
QUERY_BLOCK = 256

eps_norm = 1e-05
res_scale = 1.4 / math.sqrt(62.0)
rope_base = 10000.0
masked_score = -1e30
score_scale = 1.0 / math.sqrt(NOPE + ROPE)
exponent = score_scale * math.log2(math.e)

f32 = jnp.float32
bf16 = jnp.bfloat16


def rms_scale(values):
    return values * lax.rsqrt(jnp.mean(values * values, axis=-1, keepdims=True) + eps_norm)


def rms_back(values, grad):
    return jax.vjp(rms_scale, values)[1](grad)[0]


def rotate(values, cosine, sine):
    half = values.shape[-1] // 2
    turned = jnp.concatenate([-values[..., half:], values[..., :half]], axis=-1)
    return values * cosine + turned * sine


def rotate_back(grad, cosine, sine):
    half = grad.shape[-1] // 2
    scaled = grad * sine
    turned = jnp.concatenate([scaled[..., half:], -scaled[..., :half]], axis=-1)
    return grad * cosine + turned


def dot(left, right, contract):
    return lax.dot_general(left, right, (contract, ((), ())), preferred_element_type=f32)


NN = ((1,), (0,))
NT = ((1,), (1,))
TN = ((0,), (0,))


def exchange(value, axis, step, size):
    return lax.ppermute(value, axis, [(i, i ^ step) for i in range(size)])


def pick(stacked, index):
    return lax.dynamic_index_in_dim(stacked, index, axis=0, keepdims=False)


def spread_queries(heads):
    out = np.zeros((heads, NOPE + ROPE, heads, 2, LANES), np.float32)
    half = ROPE // 2
    for h in range(heads):
        for j in range(NOPE + ROPE):
            out[h, j, h, 0, j] = 1.0
        for j in range(half):
            out[h, NOPE + half + j, h, 1, NOPE + j] = -1.0
            out[h, NOPE + j, h, 1, NOPE + half + j] = 1.0
    return out.reshape(heads * (NOPE + ROPE), heads * 2 * LANES)


def spread_keys(heads):
    out = np.zeros((heads, NOPE + VDIM, heads, 2, LANES), np.float32)
    for h in range(heads):
        for j in range(NOPE):
            out[h, j, h, 0, j] = 1.0
        for j in range(VDIM):
            out[h, NOPE + j, h, 1, j] = 1.0
    return out.reshape(heads * (NOPE + VDIM), heads * 2 * LANES)


def spread_rope(heads):
    out = np.zeros((ROPE, heads, 2, LANES), np.float32)
    for j in range(ROPE):
        out[j, :, 0, NOPE + j] = 1.0
    return out.reshape(ROPE, heads * 2 * LANES)


def spread_values(heads):
    out = np.zeros((heads, VDIM, heads, LANES), np.float32)
    for h in range(heads):
        for j in range(VDIM):
            out[h, j, h, j] = 1.0
    return out.reshape(heads * VDIM, heads * LANES)


def split_low(value):
    first = value.astype(bf16).astype(f32)
    second = (value - first).astype(bf16).astype(f32)
    third = (value - first - second).astype(bf16).astype(f32)
    return first, second, third


def forward_kernel(
    qn_ref, kvn_ref, wq_ref, wkv_ref, cos_ref, sin_ref, qtab_ref, ktab_ref, o_ref, q_ref, k_ref, v_ref
):
    length = qn_ref.shape[0]
    block = min(QUERY_BLOCK, length)
    raw = jnp.dot(qn_ref[...], wq_ref[...], preferred_element_type=f32)
    query = raw[:, :LANES] * cos_ref[...] + raw[:, LANES:] * sin_ref[...] + qtab_ref[...]
    q_ref[...] = query.astype(bf16)
    both = jnp.dot(kvn_ref[...], wkv_ref[...], preferred_element_type=f32)
    k_ref[...] = (both[:, :LANES] + ktab_ref[...]).astype(bf16)
    lane = lax.broadcasted_iota(jnp.int32, (length, LANES), 1)
    ones = (lane >= VDIM) & (lane < VDIM + 3)
    v_ref[...] = jnp.where(ones, 1.0, both[:, LANES:]).astype(bf16)
    lane = lax.broadcasted_iota(jnp.int32, (block, LANES), 1)
    after = lax.broadcasted_iota(jnp.int32, (block, block), 1) > lax.broadcasted_iota(
        jnp.int32, (block, block), 0
    )
    for i in range(length // block):
        here = pl.ds(i * block, block)
        query = q_ref[here, :]
        own = dot(query, k_ref[here, :], NT)
        own = jnp.where(after, masked_score, own)
        highest = jnp.max(own, axis=1, keepdims=True)
        if i:
            before = pl.ds(0, i * block)
            past = dot(query, k_ref[before, :], NT)
            highest = jnp.maximum(highest, jnp.max(past, axis=1, keepdims=True))
        weights = jnp.exp2((own - highest) * exponent).astype(bf16)
        mixed = dot(weights, v_ref[here, :], NN)
        if i:
            weights = jnp.exp2((past - highest) * exponent).astype(bf16)
            mixed = mixed + dot(weights, v_ref[before, :], NN)
        total = mixed[:, VDIM : VDIM + 1]
        o_ref[here, :] = jnp.where(lane < VDIM, mixed / total, 0.0).astype(bf16)
        first, second, third = split_low(-(highest + jnp.log2(total) / exponent))
        at = NOPE + ROPE
        kept = jnp.where(
            lane == at,
            first,
            jnp.where(
                lane == at + 1, second, jnp.where(lane == at + 2, third, query.astype(f32))
            ),
        )
        q_ref[here, :] = kept.astype(bf16)


def backward_kernel(
    q_ref, k_ref, v_ref, o_ref, g_ref, cos_ref, sin_ref, dq_ref, dkv_ref, grad_ref, dk_acc, dv_acc
):
    length = q_ref.shape[0]
    block = min(QUERY_BLOCK, length)
    grad = g_ref[...].astype(f32)
    inner = jnp.sum(grad * o_ref[...].astype(f32), axis=1, keepdims=True)
    first, second, third = split_low(-inner)
    lane = lax.broadcasted_iota(jnp.int32, (length, LANES), 1)
    grad = jnp.where(
        lane == VDIM,
        first,
        jnp.where(lane == VDIM + 1, second, jnp.where(lane == VDIM + 2, third, grad)),
    )
    grad_ref[...] = grad.astype(bf16)
    after = lax.broadcasted_iota(jnp.int32, (block, block), 0) > lax.broadcasted_iota(
        jnp.int32, (block, block), 1
    )
    for i in reversed(range(length // block)):
        here = pl.ds(i * block, block)
        query, grad = q_ref[here, :], grad_ref[here, :]

        def part(span, masked):
            keys = k_ref[span, :]
            scores = dot(keys, query, NT)
            if masked:
                scores = jnp.where(after, masked_score, scores)
            probs = jnp.exp2(scores * exponent)
            inward = dot(v_ref[span, :], grad, NT)
            low = (probs * inward).astype(bf16)
            dv = dot(probs.astype(bf16), grad, NN)
            dk = dot(low, query, NN)
            if i == length // block - 1:
                dv_acc[span, :] = dv
                dk_acc[span, :] = dk
            else:
                dv_acc[span, :] += dv
                dk_acc[span, :] += dk
            return dot(low, keys, TN)

        dq = part(here, True)
        if i:
            dq = dq + part(pl.ds(0, i * block), False)
        dq = dq * score_scale
        dq_ref[here, :LANES] = (dq * cos_ref[here, :]).astype(bf16)
        dq_ref[here, LANES:] = (dq * sin_ref[here, :]).astype(bf16)
    dkv_ref[:, :LANES] = jnp.where(lane < NOPE + ROPE, dk_acc[...] * score_scale, 0.0).astype(bf16)
    dkv_ref[:, LANES:] = jnp.where(lane < VDIM, dv_acc[...], 0.0).astype(bf16)


def kernel_params():
    return pltpu.CompilerParams(
        dimension_semantics=("arbitrary",), vmem_limit_bytes=48 * 1024 * 1024
    )


def attend(qn, kvn, wq, wkv, cosine, sine, qtab, ktab):
    length = qn.shape[0]
    heads = wq.shape[1] // (2 * LANES)
    whole = lambda a: pl.BlockSpec(a.shape, lambda h: (0, 0))
    column = lambda rows, width: pl.BlockSpec((rows, width), lambda h: (0, h))
    out = jax.ShapeDtypeStruct((length, heads * LANES), bf16)
    scores = heads * length * length
    return pl.pallas_call(
        forward_kernel,
        grid=(heads,),
        in_specs=[
            whole(qn),
            whole(kvn),
            column(wq.shape[0], 2 * LANES),
            column(wkv.shape[0], 2 * LANES),
            whole(cosine),
            whole(sine),
            whole(qtab),
            whole(ktab),
        ],
        out_specs=[column(length, LANES)] * 4,
        out_shape=[out] * 4,
        compiler_params=kernel_params(),
        cost_estimate=pl.CostEstimate(
            flops=4 * scores * LANES, bytes_accessed=16 * length * heads * LANES, transcendentals=scores
        ),
    )(qn, kvn, wq, wkv, cosine, sine, qtab, ktab)


def attend_back(q, k, v, o, g, cosine, sine):
    length = q.shape[0]
    heads = q.shape[1] // LANES
    whole = lambda a: pl.BlockSpec(a.shape, lambda h: (0, 0))
    column = lambda width: pl.BlockSpec((length, width), lambda h: (0, h))
    out = jax.ShapeDtypeStruct((length, heads * 2 * LANES), bf16)
    scores = heads * length * length
    return pl.pallas_call(
        backward_kernel,
        grid=(heads,),
        in_specs=[column(LANES)] * 5 + [whole(cosine), whole(sine)],
        out_specs=[column(2 * LANES)] * 2,
        out_shape=[out] * 2,
        scratch_shapes=[
            pltpu.VMEM((length, LANES), bf16),
            pltpu.VMEM((length, LANES), f32),
            pltpu.VMEM((length, LANES), f32),
        ],
        compiler_params=kernel_params(),
        cost_estimate=pl.CostEstimate(
            flops=10 * scores * LANES, bytes_accessed=24 * length * heads * LANES, transcendentals=scores
        ),
    )(q, k, v, o, g, cosine, sine)


def body(
    sizes,
    tokens,
    segments,
    gain_attn,
    w_qa,
    gain_q,
    w_kva,
    gain_kv,
    w_qb,
    w_kvb,
    w_o,
    gain_mlp,
    w_gate,
    w_up,
    w_down,
    cotangent,
):
    nt, nz, nc = sizes
    t, z, c = lax.axis_index("tensor"), lax.axis_index("dp"), lax.axis_index("ctx")
    rows, width = tokens.shape[1:]
    half = rows // nt
    block = w_o.shape[0]
    length = nc * rows
    heads = w_qb.shape[1] // (NOPE + ROPE) // nc
    ff = w_gate.shape[1] // nz
    qrank = w_qa.shape[1]

    def turn(value):
        lead = value.shape[:-1]
        return jnp.swapaxes(value.reshape(lead + (nz, nc, block)), -3, -2).reshape(lead + (width,))

    def turn_back(value):
        lead = value.shape[:-1]
        return jnp.swapaxes(value.reshape(lead + (nc, nz, block)), -3, -2).reshape(lead + (width,))

    def swap(value):
        return exchange(value, "tensor", 1, nt)

    def both_halves(value):
        other = swap(value)
        first = jnp.where(t == 0, value, other)
        second = jnp.where(t == 0, other, value)
        return first, second

    def gather_ctx(value):
        pieces = [value] + [exchange(value, "ctx", k, nc) for k in range(1, nc)]
        first, second = both_halves(jnp.stack(pieces))
        return jnp.concatenate(
            [part for j in range(nc) for part in (pick(first, c ^ j), pick(second, c ^ j))], axis=0
        )

    def scatter_ctx(value):
        parts = value.reshape(nc, nt, half, value.shape[1])
        keep = jnp.where(t == 0, parts[:, 0], parts[:, 1])
        give = jnp.where(t == 0, parts[:, 1], parts[:, 0]).astype(bf16)
        parts = (keep + swap(give).astype(f32)).astype(bf16)
        total = pick(parts, c).astype(f32)
        for k in range(1, nc):
            total = total + exchange(pick(parts, c ^ k), "ctx", k, nc).astype(f32)
        return total

    def gather_dp(value):
        pieces = []
        for k in range(nz):
            piece = exchange(value, "dp", k, nz) if k else value
            pieces += [piece, swap(piece)]
        return jnp.concatenate(pieces, axis=0)

    def scatter_dp(value):
        parts = value.reshape(nz, nt, half, value.shape[1])
        total = None
        for k in range(nz):
            piece = parts[k, 0] + swap(parts[k, 1].astype(bf16)).astype(f32)
            if k:
                piece = exchange(piece.astype(bf16), "dp", k, nz).astype(f32)
            total = piece if total is None else total + piece
        return total

    def spread_dp(value):
        parts = jnp.swapaxes(value.reshape(block, nz, -1), 0, 1)
        pieces = [pick(parts, z)]
        for k in range(1, nz):
            pieces.append(exchange(pick(parts, z ^ k), "dp", k, nz))
        pieces = jnp.stack(pieces)
        return jnp.concatenate([pick(pieces, z ^ j)[None] for j in range(nz)], axis=0)

    def spread_dp_back(parts):
        pieces = [pick(parts, z)]
        for k in range(1, nz):
            pieces.append(exchange(pick(parts, z ^ k), "dp", k, nz))
        pieces = jnp.stack(pieces)
        return jnp.concatenate([pick(pieces, z ^ j) for j in range(nz)], axis=1)

    def gather_weight(value):
        parts = spread_dp(value).reshape(nz * block, ff)
        return lax.all_gather(parts, "ctx", axis=0, tiled=True)

    def scatter_weight(value):
        parts = lax.psum_scatter(value.astype(bf16), "ctx", scatter_dimension=0, tiled=True)
        return spread_dp_back(parts.reshape(nz, block, ff)).astype(f32)

    full_down = gather_weight(w_down)
    full_gate = gather_weight(w_gate)
    full_up = gather_weight(w_up)

    out_parts = jnp.swapaxes(w_o.reshape(block, nc, heads * VDIM), 0, 1)
    pieces = [pick(out_parts, c)]
    for k in range(1, nc):
        pieces.append(exchange(pick(out_parts, c ^ k), "ctx", k, nc))
    pieces = jnp.stack(pieces)
    own_out = jnp.concatenate([pick(pieces, c ^ j)[None] for j in range(nc)], axis=0)
    pieces = [own_out] + [exchange(own_out, "dp", k, nz) for k in range(1, nz)]
    pieces = jnp.stack(pieces)
    full_out = jnp.concatenate([pick(pieces, z ^ j)[:, None] for j in range(nz)], axis=1)
    spread_v = jnp.asarray(spread_values(heads), bf16)
    full_out = dot(full_out.reshape(width, heads * VDIM), spread_v, NN).astype(bf16)

    spread_q = jnp.asarray(spread_queries(heads), bf16)
    spread_k = jnp.asarray(spread_keys(heads), bf16)
    own_qb = lax.dynamic_slice_in_dim(w_qb, c * heads * (NOPE + ROPE), heads * (NOPE + ROPE), axis=1)
    own_kvb = lax.dynamic_slice_in_dim(w_kvb, c * heads * (NOPE + VDIM), heads * (NOPE + VDIM), axis=1)
    wide_qb = dot(own_qb, spread_q, NN).astype(bf16)
    wide_kvb = jnp.concatenate(
        [dot(own_kvb, spread_k, NN).astype(bf16), jnp.asarray(spread_rope(heads), bf16)], axis=0
    )

    segment_all = segments[0]
    doc_start = jnp.sum((segment_all[None, :] < segment_all[:, None]).astype(jnp.int32), axis=1)
    positions = (jnp.arange(length, dtype=jnp.int32) - doc_start).astype(f32)
    freqs = rope_base ** (-jnp.arange(0, ROPE, 2).astype(f32) / ROPE)
    angles = positions[:, None] * freqs[None, :]
    angles = jnp.concatenate([angles, angles], axis=1)
    cosine, sine = jnp.cos(angles), jnp.sin(angles)
    fill = lambda width, value: jnp.full((length, width), value, f32)
    tail = LANES - NOPE - ROPE
    cos_table = jnp.concatenate([fill(NOPE, 1.0), cosine, fill(tail, 0.0)], axis=1)
    sin_table = jnp.concatenate([fill(NOPE, 0.0), sine, fill(tail, 0.0)], axis=1)
    same = (segment_all[:, None] == jnp.arange(3, dtype=jnp.int32)[None, :]).astype(f32)
    query_table = jnp.concatenate(
        [fill(NOPE + ROPE + 3, 0.0), same * masked_score, fill(tail - 6, 0.0)], axis=1
    )
    key_table = jnp.concatenate(
        [fill(NOPE + ROPE, 0.0), fill(3, 1.0), 1.0 - same, fill(tail - 6, 0.0)], axis=1
    )
    first_row = c * rows + t * half
    own_cos = lax.dynamic_slice_in_dim(cosine, first_row, half)
    own_sin = lax.dynamic_slice_in_dim(sine, first_row, half)

    gain_in = gain_attn.astype(f32)
    gain_query = gain_q.astype(f32)
    gain_latent = gain_kv.astype(f32)
    gain_middle = turn(gain_mlp.astype(f32))
    own_tokens = lax.dynamic_slice_in_dim(tokens[0], t * half, half)
    own_cotangent = turn(lax.dynamic_slice_in_dim(cotangent[0], t * half, half))
    hidden_in = own_tokens.astype(f32)
    scaled_in = rms_scale(hidden_in)
    normed_in = (scaled_in * gain_in).astype(bf16)
    q_latent = dot(normed_in, w_qa, NN)
    kv_latent = dot(normed_in, w_kva, NN)
    q_scaled = rms_scale(q_latent)
    q_normed = (q_scaled * gain_query).astype(bf16)
    c_round = rms_scale(kv_latent[:, :KVRANK]).astype(bf16).astype(f32)
    c_normed = (c_round * gain_latent).astype(bf16)
    key_rope = rotate(kv_latent[:, KVRANK:], own_cos, own_sin).astype(bf16)
    latents = gather_ctx(jnp.concatenate([q_normed, c_normed, key_rope], axis=1))
    qn, kvn = latents[:, :qrank], latents[:, qrank:]
    heads_out, q_rot, keys, values = attend(
        qn, kvn, wide_qb, wide_kvb, cos_table, sin_table, query_table, key_table
    )
    attn = scatter_ctx(dot(heads_out, full_out, NT))
    resid = turn(own_tokens).astype(f32) + res_scale * attn
    resid_scaled = rms_scale(resid)
    normed_mid = gather_dp((resid_scaled * gain_middle).astype(bf16))
    gate = dot(normed_mid, full_gate, NN)
    up_proj = dot(normed_mid, full_up, NN)
    sigma = jax.nn.sigmoid(gate)
    silu_gate = gate * sigma
    hidden_mid = (silu_gate * up_proj).astype(bf16)
    mlp = scatter_dp(dot(hidden_mid, full_down, NT))
    layer_out = (resid + res_scale * mlp).astype(bf16)
    layer_out = turn_back(jnp.concatenate(both_halves(layer_out), axis=0))[None]

    grad_out = own_cotangent.astype(f32)
    grad_mlp = gather_dp((res_scale * grad_out).astype(bf16))
    grad_hidden = dot(grad_mlp, full_down, NN)
    grad_gate = (grad_hidden * up_proj * sigma * (1.0 + gate * (1.0 - sigma))).astype(bf16)
    grad_up = (grad_hidden * silu_gate).astype(bf16)
    grad_normed_mid = scatter_dp(dot(grad_gate, full_gate, NT) + dot(grad_up, full_up, NT))
    grad_w_down = scatter_weight(dot(grad_mlp, hidden_mid, TN))
    grad_w_gate = scatter_weight(dot(normed_mid, grad_gate, TN))
    grad_w_up = scatter_weight(dot(normed_mid, grad_up, TN))
    grad_gain_mlp = jnp.sum(grad_normed_mid * resid_scaled, axis=0)
    grad_resid = grad_out + rms_back(resid, grad_normed_mid * gain_middle)

    grad_attn = gather_ctx((res_scale * grad_resid).astype(bf16))
    grad_heads = dot(grad_attn, full_out, NN).astype(bf16)
    grad_out_part = dot(dot(grad_attn, heads_out, TN).astype(bf16), spread_v, NT).astype(bf16)
    grad_out_part = jnp.swapaxes(grad_out_part.reshape(nc, nz, block, heads * VDIM), 0, 1)
    total = pick(grad_out_part, z).astype(f32)
    for k in range(1, nz):
        total = total + exchange(pick(grad_out_part, z ^ k), "dp", k, nz).astype(f32)
    total = total.astype(bf16)
    pieces = [pick(total, c)]
    for k in range(1, nc):
        pieces.append(exchange(pick(total, c ^ k), "ctx", k, nc))
    pieces = jnp.stack(pieces)
    grad_w_o = jnp.concatenate([pick(pieces, c ^ j) for j in range(nc)], axis=1).astype(f32)

    grad_q, grad_kv = attend_back(q_rot, keys, values, heads_out, grad_heads, cos_table, sin_table)
    grad_latents = scatter_ctx(
        jnp.concatenate([dot(grad_q, wide_qb, NT), dot(grad_kv, wide_kvb, NT)], axis=1)
    )
    grad_wide_qb = dot(dot(qn, grad_q, TN).astype(bf16), spread_q, NT)
    grad_wide_qb = jnp.pad(
        grad_wide_qb.astype(bf16), ((0, 0), (0, heads * (VDIM - ROPE)))
    )
    grad_wide_kvb = dot(dot(kvn[:, :KVRANK], grad_kv, TN).astype(bf16), spread_k, NT).astype(bf16)
    grad_ups = jnp.concatenate([grad_wide_qb, grad_wide_kvb], axis=0)
    grad_ups = lax.psum_scatter(grad_ups, "dp", scatter_dimension=0, tiled=True)
    grad_ups = lax.all_gather(grad_ups, ("dp", "ctx"), axis=0, tiled=False)
    grad_ups = grad_ups.reshape(nz, nc, -1, heads * (NOPE + VDIM))
    grad_ups = jnp.swapaxes(grad_ups, 0, 1).reshape(nc, qrank + KVRANK, heads * (NOPE + VDIM))
    grad_w_qb = jnp.swapaxes(grad_ups[:, :qrank, : heads * (NOPE + ROPE)], 0, 1)
    grad_w_qb = grad_w_qb.reshape(qrank, -1).astype(f32)
    grad_w_kvb = jnp.swapaxes(grad_ups[:, qrank:], 0, 1).reshape(KVRANK, -1).astype(f32)

    grad_q_normed = grad_latents[:, :qrank]
    grad_c_normed = grad_latents[:, qrank : qrank + KVRANK]
    grad_key_rope = grad_latents[:, qrank + KVRANK :]
    grad_gain_q = jnp.sum(grad_q_normed * q_scaled, axis=0)
    grad_gain_kv = jnp.sum(grad_c_normed * c_round, axis=0)
    grad_q_latent = rms_back(q_latent, grad_q_normed * gain_query).astype(bf16)
    grad_c_latent = rms_back(kv_latent[:, :KVRANK], grad_c_normed * gain_latent)
    grad_kv_latent = jnp.concatenate(
        [grad_c_latent, rotate_back(grad_key_rope, own_cos, own_sin)], axis=1
    ).astype(bf16)
    grad_normed_in = dot(grad_q_latent, w_qa, NT) + dot(grad_kv_latent, w_kva, NT)
    grad_gain_attn = jnp.sum(grad_normed_in * scaled_in, axis=0)
    grad_tokens = turn_back(grad_resid) + rms_back(hidden_in, grad_normed_in * gain_in)
    grad_tokens = jnp.concatenate(both_halves(grad_tokens.astype(bf16)), axis=0)[None]

    lat_width = qrank + w_kva.shape[1]
    grad_lat = jnp.concatenate(
        [dot(normed_in, grad_q_latent, TN), dot(normed_in, grad_kv_latent, TN)], axis=1
    )
    grad_lat = jnp.stack([grad_lat[:, : lat_width // 2], grad_lat[:, lat_width // 2 :]])
    keep, give = pick(grad_lat, t), pick(grad_lat, 1 - t).astype(bf16)
    parts = (keep + swap(give).astype(f32)).astype(bf16)
    parts = jnp.swapaxes(parts.reshape(nz, nc, block, lat_width // 2), 0, 1)
    total = pick(parts, c).astype(f32)
    for k in range(1, nc):
        total = total + exchange(pick(parts, c ^ k), "ctx", k, nc).astype(f32)
    parts = total.astype(bf16)
    total = pick(parts, z).astype(f32)
    for k in range(1, nz):
        total = total + exchange(pick(parts, z ^ k), "dp", k, nz).astype(f32)
    grad_lat = jnp.concatenate(both_halves(total.astype(bf16)), axis=1).astype(f32)
    grad_w_qa, grad_w_kva = grad_lat[:, :qrank], grad_lat[:, qrank:]

    gains = jnp.concatenate([grad_gain_attn, grad_gain_q, grad_gain_kv, turn_back(grad_gain_mlp)])
    gains = gains.reshape(-1, LANES)
    for axis, size in (("tensor", nt), ("ctx", nc), ("dp", nz)):
        step = 1
        while step < size:
            gains = gains + exchange(gains, axis, step, size)
            step *= 2
    gains = gains.reshape(-1)
    ends = np.cumsum([width, qrank, KVRANK])
    grad_gain_attn, grad_gain_q, grad_gain_kv, grad_gain_mlp = jnp.split(gains, ends)
    return (
        layer_out,
        grad_tokens,
        grad_gain_attn,
        grad_w_qa,
        grad_gain_q,
        grad_w_kva,
        grad_gain_kv,
        grad_w_qb,
        grad_w_kvb,
        grad_w_o,
        grad_gain_mlp,
        grad_w_gate,
        grad_w_up,
        grad_w_down,
    )


def solution(mesh):
    placed = (
        P("dp", "ctx", None),
        P("dp", None),
        P(),
        P(),
        P(),
        P(),
        P(),
        P(None, "tensor"),
        P(None, "tensor"),
        P(("dp", "ctx"), "tensor"),
        P(),
        P(("dp", "ctx"), "tensor"),
        P(("dp", "ctx"), "tensor"),
        P(("dp", "ctx"), "tensor"),
        P("dp", "ctx", None),
    )
    sizes = tuple(mesh.shape[name] for name in ("tensor", "dp", "ctx"))
    return jax.shard_map(
        functools.partial(body, sizes),
        mesh=mesh,
        in_specs=placed,
        out_specs=(
            P("dp", "ctx", None),
            P("dp", "ctx", None),
            P(),
            P(("dp", "ctx"), None),
            P(),
            P(("dp", "ctx"), None),
            P(),
            P(None, "tensor"),
            P(None, "tensor"),
            P(("dp", "ctx"), "tensor"),
            P(),
            P(("dp", "ctx"), "tensor"),
            P(("dp", "ctx"), "tensor"),
            P(("dp", "ctx"), "tensor"),
        ),
        check_vma=False,
    )
```

```python
import functools
import math

import jax
import jax.numpy as jnp
import numpy as np
from jax import lax
from jax.experimental import pallas as pl
from jax.experimental.pallas import tpu as pltpu
from jax.sharding import PartitionSpec as P

NOPE = 64
ROPE = 32
VDIM = 64
KVRANK = 256
LANES = 128
QUERY_BLOCK = 256

eps_norm = 1e-05
res_scale = 1.4 / math.sqrt(62.0)
rope_base = 10000.0
masked_score = -1e30
score_scale = 1.0 / math.sqrt(NOPE + ROPE)
exponent = score_scale * math.log2(math.e)

f32 = jnp.float32
bf16 = jnp.bfloat16


def rms_scale(values):
    return values * lax.rsqrt(jnp.mean(values * values, axis=-1, keepdims=True) + eps_norm)


def dot(left, right, contract):
    return lax.dot_general(left, right, (contract, ((), ())), preferred_element_type=f32)


NN = ((1,), (0,))
NT = ((1,), (1,))
TN = ((0,), (0,))


def exchange(value, axis, step, size):
    return lax.ppermute(value, axis, [(i, i ^ step) for i in range(size)])


def after(value, *done):
    return lax.optimization_barrier((value,) + done)[0]


def pick(stacked, index):
    return lax.dynamic_index_in_dim(stacked, index, axis=0, keepdims=False)


def spread_queries(heads):
    out = np.zeros((heads, NOPE + ROPE, heads, 2, LANES), np.float32)
    half = ROPE // 2
    for h in range(heads):
        for j in range(NOPE + ROPE):
            out[h, j, h, 0, j] = 1.0
        for j in range(half):
            out[h, NOPE + half + j, h, 1, NOPE + j] = -1.0
            out[h, NOPE + j, h, 1, NOPE + half + j] = 1.0
    return out.reshape(heads * (NOPE + ROPE), heads * 2 * LANES)


def spread_keys(heads):
    out = np.zeros((heads, NOPE + VDIM, heads, 2, LANES), np.float32)
    for h in range(heads):
        for j in range(NOPE):
            out[h, j, h, 0, j] = 1.0
        for j in range(VDIM):
            out[h, NOPE + j, h, 1, j] = 1.0
    return out.reshape(heads * (NOPE + VDIM), heads * 2 * LANES)


def spread_rope(heads):
    out = np.zeros((ROPE, heads, 2, LANES), np.float32)
    for j in range(ROPE):
        out[j, :, 0, NOPE + j] = 1.0
    return out.reshape(ROPE, heads * 2 * LANES)


def spread_values(heads):
    out = np.zeros((heads, VDIM, heads, LANES), np.float32)
    for h in range(heads):
        for j in range(VDIM):
            out[h, j, h, j] = 1.0
    return out.reshape(heads * VDIM, heads * LANES)


def split_low(value):
    first = value.astype(bf16).astype(f32)
    second = (value - first).astype(bf16).astype(f32)
    third = (value - first - second).astype(bf16).astype(f32)
    return first, second, third


def rms_back(values, grad):
    inverse = lax.rsqrt(jnp.mean(values * values, axis=-1, keepdims=True) + eps_norm)
    scaled = values * inverse
    return (grad - scaled * jnp.mean(grad * scaled, axis=-1, keepdims=True)) * inverse


def turn_matrix():
    half = ROPE // 2
    out = np.zeros((ROPE, ROPE), np.float32)
    for j in range(half):
        out[half + j, j] = -1.0
        out[j, half + j] = 1.0
    return out


def total_of(refs):
    total = refs[0][...].astype(f32)
    for ref in refs[1:]:
        total = total + ref[...].astype(f32)
    return total


def move_blocks(source, target, outer, inner, block, cast=None):
    for i in range(outer):
        for j in range(inner):
            value = source[:, (i * inner + j) * block : (i * inner + j + 1) * block]
            target[:, (j * outer + i) * block : (j * outer + i + 1) * block] = (
                value if cast is None else cast(value)
            )


SCALARS = pl.BlockSpec(memory_space=pltpu.SMEM)
LOCAL = pl.BlockSpec(memory_space=pltpu.VMEM)


def params(megabytes=48):
    return pltpu.CompilerParams(vmem_limit_bytes=megabytes * 1024 * 1024)


def grid_params(megabytes=48):
    return pltpu.CompilerParams(
        dimension_semantics=("arbitrary",), vmem_limit_bytes=megabytes * 1024 * 1024
    )


def cost(flops=0, moved=0, special=0):
    return pl.CostEstimate(
        flops=flops // 10, bytes_accessed=moved // 10, transcendentals=special // 10
    )


def plain(kernel, ids, operands, outs, scratch=(), flops=0, megabytes=48):
    moved = sum(a.size * a.dtype.itemsize for a in operands)
    moved += sum(math.prod(s) * jnp.dtype(d).itemsize for s, d in outs)
    return pl.pallas_call(
        kernel,
        in_specs=[SCALARS] + [LOCAL] * len(operands),
        out_specs=[LOCAL] * len(outs),
        out_shape=[jax.ShapeDtypeStruct(s, d) for s, d in outs],
        scratch_shapes=list(scratch),
        compiler_params=params(megabytes),
        cost_estimate=cost(flops, moved),
    )(ids, *operands)


def enter_kernel(
    sizes, block, ids, tok, cot, gain_in, gain_query, gain_latent, w_qa, w_kva, cosine, sine, turned,
    normed_ref, lat_ref, q_ref, kv_ref, x_ref, cot_ref, gm_ref, *rest
):
    nt, nz, nc = sizes
    pieces, (inner, plain_ref) = rest[:nc], rest[nc:]
    half = normed_ref.shape[0]
    qrank = w_qa.shape[1]
    here = pl.ds(pl.multiple_of(ids[0] * half, half), half)
    own = tok[here, :]
    hidden = own.astype(f32)
    normed = (rms_scale(hidden) * gain_in[...]).astype(bf16)
    normed_ref[...] = normed
    q_latent = dot(normed, w_qa[...], NN)
    kv_latent = dot(normed, w_kva[...], NT)
    q_ref[...] = q_latent
    kv_ref[...] = kv_latent
    lat_ref[:, :qrank] = (rms_scale(q_latent) * gain_query[...]).astype(bf16)
    c_round = rms_scale(kv_latent[:, :KVRANK]).astype(bf16).astype(f32)
    lat_ref[:, qrank : qrank + KVRANK] = (c_round * gain_latent[...]).astype(bf16)
    rope = kv_latent[:, KVRANK:]
    other = jnp.dot(rope, turned[...], precision=lax.Precision.HIGHEST, preferred_element_type=f32)
    end = qrank + KVRANK + ROPE
    lat_ref[:, qrank + KVRANK : end] = (rope * cosine[...] + other * sine[...]).astype(bf16)
    lat_ref[:, end:] = jnp.zeros((half, lat_ref.shape[1] - end), bf16)
    move_blocks(normed_ref, inner, nz, nc, block)
    span = nz * block
    for k in range(nc):
        start = pl.multiple_of((ids[2] ^ k) * span, span)
        pieces[k][...] = inner[:, pl.ds(start, span)]
    plain_ref[...] = own
    move_blocks(plain_ref, x_ref, nz, nc, block)
    plain_ref[...] = cot[here, :]
    move_blocks(plain_ref, cot_ref, nz, nc, block)
    gm_ref[...] = (res_scale * cot_ref[...].astype(f32)).astype(bf16)


def forward_kernel(
    nt, ids, own_ref, oth_ref, wq_ref, wkv_ref, cos_ref, sin_ref, qtab_ref, ktab_ref,
    oown_ref, ooth_ref, q_ref, k_ref, v_ref, qn_ref, kvn_ref
):
    t, c = ids[0], ids[2]
    nc, half = own_ref.shape[0], own_ref.shape[1]
    length, qrank = qn_ref.shape
    block = nt * half

    @pl.when(pl.program_id(0) == 0)
    def _():
        for j in range(nc):
            for i in range(nt):
                rows = pl.ds((j * nt + i) * half, half)
                value = jnp.where(t == i, own_ref[c ^ j], oth_ref[c ^ j])
                qn_ref[rows, :] = value[:, :qrank]
                kvn_ref[rows, :] = value[:, qrank:]

    raw = jnp.dot(qn_ref[...], wq_ref[...], preferred_element_type=f32)
    query = raw[:, :LANES] * cos_ref[...] + raw[:, LANES:] * sin_ref[...] + qtab_ref[...]
    q_ref[...] = query.astype(bf16)
    both = jnp.dot(kvn_ref[...], wkv_ref[...], preferred_element_type=f32)
    k_ref[...] = (both[:, :LANES] + ktab_ref[...]).astype(bf16)
    lane = lax.broadcasted_iota(jnp.int32, (length, LANES), 1)
    ones = (lane >= VDIM) & (lane < VDIM + 3)
    v_ref[...] = jnp.where(ones, 1.0, both[:, LANES:]).astype(bf16)
    lane = lax.broadcasted_iota(jnp.int32, (block, LANES), 1)
    after = lax.broadcasted_iota(jnp.int32, (block, block), 1) > lax.broadcasted_iota(
        jnp.int32, (block, block), 0
    )
    for i in range(nc):
        here = pl.ds(i * block, block)
        query = q_ref[here, :]
        own = dot(query, k_ref[here, :], NT)
        own = jnp.where(after, masked_score, own)
        highest = jnp.max(own, axis=1, keepdims=True)
        if i:
            before = pl.ds(0, i * block)
            past = dot(query, k_ref[before, :], NT)
            highest = jnp.maximum(highest, jnp.max(past, axis=1, keepdims=True))
        weights = jnp.exp2((own - highest) * exponent).astype(bf16)
        mixed = dot(weights, v_ref[here, :], NN)
        if i:
            weights = jnp.exp2((past - highest) * exponent).astype(bf16)
            mixed = mixed + dot(weights, v_ref[before, :], NN)
        total = mixed[:, VDIM : VDIM + 1]
        out = jnp.where(lane < VDIM, mixed / total, 0.0).astype(bf16)
        for j in range(nt):
            part = out[j * half : (j + 1) * half]

            @pl.when(t == j)
            def _():
                oown_ref[c ^ i] = part

            @pl.when(t != j)
            def _():
                ooth_ref[c ^ i] = part

        first, second, third = split_low(-(highest + jnp.log2(total) / exponent))
        at = NOPE + ROPE
        kept = jnp.where(
            lane == at,
            first,
            jnp.where(lane == at + 1, second, jnp.where(lane == at + 2, third, query.astype(f32))),
        )
        q_ref[here, :] = kept.astype(bf16)


def backward_kernel(
    nt, ids, q_ref, k_ref, v_ref, oown_ref, ooth_ref, gown_ref, goth_ref, cos_ref, sin_ref,
    dq_ref, dkv_ref, grad_ref, dk_acc, dv_acc
):
    t, c = ids[0], ids[2]
    nc, half = gown_ref.shape[0], gown_ref.shape[1]
    length = q_ref.shape[0]
    block = nt * half
    lane = lax.broadcasted_iota(jnp.int32, (half, LANES), 1)
    for j in range(nc):
        for i in range(nt):
            grad = jnp.where(t == i, gown_ref[c ^ j], goth_ref[c ^ j]).astype(f32)
            out = jnp.where(t == i, oown_ref[c ^ j], ooth_ref[c ^ j]).astype(f32)
            first, second, third = split_low(-jnp.sum(grad * out, axis=1, keepdims=True))
            grad = jnp.where(
                lane == VDIM,
                first,
                jnp.where(lane == VDIM + 1, second, jnp.where(lane == VDIM + 2, third, grad)),
            )
            grad_ref[pl.ds((j * nt + i) * half, half), :] = grad.astype(bf16)
    after = lax.broadcasted_iota(jnp.int32, (block, block), 0) > lax.broadcasted_iota(
        jnp.int32, (block, block), 1
    )
    for i in reversed(range(nc)):
        here = pl.ds(i * block, block)
        query, grad = q_ref[here, :], grad_ref[here, :]

        def part(span, masked):
            keys = k_ref[span, :]
            scores = dot(keys, query, NT)
            if masked:
                scores = jnp.where(after, masked_score, scores)
            probs = jnp.exp2(scores * exponent)
            inward = dot(v_ref[span, :], grad, NT)
            low = (probs * inward).astype(bf16)
            dv = dot(probs.astype(bf16), grad, NN)
            dk = dot(low, query, NN)
            if i == nc - 1:
                dv_acc[span, :] = dv
                dk_acc[span, :] = dk
            else:
                dv_acc[span, :] += dv
                dk_acc[span, :] += dk
            return dot(low, keys, TN)

        dq = part(here, True)
        if i:
            dq = dq + part(pl.ds(0, i * block), False)
        dq = dq * score_scale
        dq_ref[here, :LANES] = (dq * cos_ref[here, :]).astype(bf16)
        dq_ref[here, LANES:] = (dq * sin_ref[here, :]).astype(bf16)
    lane = lax.broadcasted_iota(jnp.int32, (length, LANES), 1)
    dkv_ref[:, :LANES] = jnp.where(lane < NOPE + ROPE, dk_acc[...] * score_scale, 0.0).astype(bf16)
    dkv_ref[:, LANES:] = jnp.where(lane < VDIM, dv_acc[...], 0.0).astype(bf16)


def attend(nt, ids, own, oth, wq, wkv, cosine, sine, qtab, ktab):
    nc, half, _ = own.shape
    length = nc * nt * half
    qrank, kvrank = wq.shape[0], wkv.shape[0]
    heads = wq.shape[1] // (2 * LANES)
    whole = lambda a: pl.BlockSpec(a.shape, lambda h, ids: (0,) * a.ndim)
    column = lambda rows, width: pl.BlockSpec((rows, width), lambda h, ids: (0, h))
    split = pl.BlockSpec((nc, half, LANES), lambda h, ids: (0, 0, h))
    out = jax.ShapeDtypeStruct((length, heads * LANES), bf16)
    out_split = jax.ShapeDtypeStruct((nc, half, heads * LANES), bf16)
    kept = [jax.ShapeDtypeStruct((length, qrank), bf16), jax.ShapeDtypeStruct((length, kvrank), bf16)]
    return pl.pallas_call(
        functools.partial(forward_kernel, nt),
        grid_spec=pltpu.PrefetchScalarGridSpec(
            num_scalar_prefetch=1,
            grid=(heads,),
            in_specs=[
                whole(own),
                whole(oth),
                column(qrank, 2 * LANES),
                column(kvrank, 2 * LANES),
                whole(cosine),
                whole(sine),
                whole(qtab),
                whole(ktab),
            ],
            out_specs=[split] * 2 + [column(length, LANES)] * 3 + [whole(a) for a in kept],
        ),
        out_shape=[out_split] * 2 + [out] * 3 + kept,
        compiler_params=grid_params(),
        cost_estimate=cost(
            4 * heads * length * (length * LANES + qrank * 2 * LANES),
            16 * length * heads * LANES,
            heads * length * length // 2,
        ),
    )(ids, own, oth, wq, wkv, cosine, sine, qtab, ktab)


def attend_back(nt, ids, q, k, v, oown, ooth, gown, goth, cosine, sine):
    nc, half, _ = oown.shape
    length = q.shape[0]
    heads = q.shape[1] // LANES
    whole = lambda a: pl.BlockSpec(a.shape, lambda h, ids: (0, 0))
    column = lambda width: pl.BlockSpec((length, width), lambda h, ids: (0, h))
    split = pl.BlockSpec((nc, half, LANES), lambda h, ids: (0, 0, h))
    out = jax.ShapeDtypeStruct((length, heads * 2 * LANES), bf16)
    return pl.pallas_call(
        functools.partial(backward_kernel, nt),
        grid_spec=pltpu.PrefetchScalarGridSpec(
            num_scalar_prefetch=1,
            grid=(heads,),
            in_specs=[column(LANES)] * 3 + [split] * 4 + [whole(cosine), whole(sine)],
            out_specs=[column(2 * LANES)] * 2,
            scratch_shapes=[
                pltpu.VMEM((length, LANES), bf16),
                pltpu.VMEM((length, LANES), f32),
                pltpu.VMEM((length, LANES), f32),
            ],
        ),
        out_shape=[out] * 2,
        compiler_params=grid_params(),
        cost_estimate=cost(
            8 * heads * length * length * LANES,
            24 * length * heads * LANES,
            heads * length * length // 2,
        ),
    )(ids, q, k, v, oown, ooth, gown, goth, cosine, sine)


def split_kernel(axis, pieces, count, ids, *refs):
    width = refs[count].shape[2]
    for k in range(pieces):
        for j in range(pieces):

            @pl.when((ids[axis] ^ k) == j)
            def _():
                for i in range(count):
                    refs[count + k][i] = refs[i][:, j * width : (j + 1) * width]


def join_kernel(axis, pieces, ids, *refs):
    targets = refs[pieces:]
    width = refs[0].shape[2]
    for k in range(pieces):
        for j in range(pieces):

            @pl.when((ids[axis] ^ k) == j)
            def _():
                for i, target in enumerate(targets):
                    target[:, j * width : (j + 1) * width] = refs[k][i].astype(target.dtype)


def stack_kernel(axis, pieces, ids, *refs):
    for k in range(pieces):
        for i in range(refs[k].shape[0]):
            refs[pieces][i, ids[axis] ^ k] = refs[k][i]


def rows_kernel(ids, own, oth, target):
    half = own.shape[0]
    target[pl.ds(pl.multiple_of(ids[0] * half, half), half), :] = own[...]
    target[pl.ds(pl.multiple_of((1 - ids[0]) * half, half), half), :] = oth[...]


def spread_kernel(heads, pieces, ids, *refs):
    target = refs[pieces]
    target[...] = jnp.zeros_like(target)
    for k in range(pieces):
        for j in range(refs[k].shape[0]):
            for h in range(heads):
                target[j, ids[1] ^ k, :, h * LANES : h * LANES + VDIM] = refs[k][
                    j, :, h * VDIM : (h + 1) * VDIM
                ]


def out_kernel(own, oth, weight, keep, give):
    half = own.shape[1]
    both = jnp.concatenate([own[0], oth[0]], axis=0)
    result = dot(both, weight[...], NT)
    keep[0] = result[:half]
    give[0] = result[half:].astype(bf16)


def project_out(own, oth, weight):
    nc, half, deep = own.shape
    width = weight.shape[0]
    piece = lambda w: pl.BlockSpec((1, half, w), lambda k: (k, 0, 0))
    return pl.pallas_call(
        out_kernel,
        grid=(nc,),
        in_specs=[piece(deep)] * 2 + [pl.BlockSpec(weight.shape, lambda k: (0, 0))],
        out_specs=[piece(width)] * 2,
        out_shape=[
            jax.ShapeDtypeStruct((nc, half, width), f32),
            jax.ShapeDtypeStruct((nc, half, width), bf16),
        ],
        compiler_params=grid_params(),
        cost_estimate=cost(4 * nc * half * deep * width, 2 * weight.size + 16 * nc * half * width),
    )(own, oth, weight)


def heads_kernel(own, oth, weight, gown, goth):
    half = own.shape[1]
    both = jnp.concatenate([own[0], oth[0]], axis=0)
    result = dot(both, weight[...], NN).astype(bf16)
    gown[0] = result[:half]
    goth[0] = result[half:]


def project_heads(own, oth, weight):
    nc, half, width = own.shape
    deep = weight.shape[1]
    piece = lambda w: pl.BlockSpec((1, half, w), lambda k: (k, 0, 0))
    return pl.pallas_call(
        heads_kernel,
        grid=(nc,),
        in_specs=[piece(width)] * 2 + [pl.BlockSpec(weight.shape, lambda k: (0, 0))],
        out_specs=[piece(deep)] * 2,
        out_shape=[jax.ShapeDtypeStruct((nc, half, deep), bf16)] * 2,
        compiler_params=grid_params(),
        cost_estimate=cost(4 * nc * half * deep * width, 2 * weight.size + 8 * nc * half * width),
    )(own, oth, weight)


def middle_kernel(pieces, ids, *refs):
    tokens, gain, resid_ref, normed_ref = refs[pieces:]
    resid = tokens[...].astype(f32) + res_scale * total_of(refs[:pieces])
    resid_ref[...] = resid
    normed_ref[...] = (rms_scale(resid) * gain[...]).astype(bf16)


def leave_kernel(sizes, block, pieces, ids, *refs):
    resid, target, inner = refs[pieces:]
    nt, nz, nc = sizes
    inner[...] = resid[...] + res_scale * total_of(refs[:pieces])
    move_blocks(inner, target, nc, nz, block, lambda value: value.astype(bf16))


def mlp_kernel(
    own_steps, nm_own, nm_oth, gm_own, gm_oth, pair_hbm, down_hbm,
    hid_ref, gg_ref, gu_ref, gn_own, gn_oth, ml_own, ml_oth, w_gate, w_up, w_down, sems
):
    step = pl.program_id(0)
    blocks = sems.shape[1]
    deep = w_down.shape[0] // blocks
    copies = [
        [
            pltpu.make_async_copy(
                source.at[pl.ds((j * count + at) * deep, deep), :],
                target.at[pl.ds(j * deep, deep), :],
                sems.at[i, j],
            )
            for j in range(blocks)
        ]
        for i, (source, count, at, target) in enumerate(
            ((pair_hbm, 2, 0, w_gate), (pair_hbm, 2, 1, w_up), (down_hbm, 1, 0, w_down))
        )
    ]

    def ready(i):
        @pl.when(step == 0)
        def _():
            for copy in copies[i]:
                copy.wait()

    @pl.when(step == 0)
    def _():
        for group in copies:
            for copy in group:
                copy.start()

    mine = step < own_steps
    normed = jnp.where(mine, nm_own[...], nm_oth[...])
    ready(0)
    gate = dot(normed, w_gate[...], NN)
    ready(1)
    up_proj = dot(normed, w_up[...], NN)
    ready(2)
    grad_hidden = dot(jnp.where(mine, gm_own[...], gm_oth[...]), w_down[...], NN)
    sigma = jax.nn.sigmoid(gate)
    silu_gate = gate * sigma
    hidden = (silu_gate * up_proj).astype(bf16)
    grad_gate = (grad_hidden * up_proj * sigma * (1.0 + gate * (1.0 - sigma))).astype(bf16)
    grad_up = (grad_hidden * silu_gate).astype(bf16)
    hid_ref[...] = hidden
    gg_ref[...] = grad_gate
    gu_ref[...] = grad_up
    grad_normed = (dot(grad_gate, w_gate[...], NT) + dot(grad_up, w_up[...], NT)).astype(bf16)
    mlp = dot(hidden, w_down[...], NT).astype(bf16)

    @pl.when(mine)
    def _():
        gn_own[...] = grad_normed
        ml_own[...] = mlp

    @pl.when(jnp.logical_not(mine))
    def _():
        gn_oth[...] = grad_normed
        ml_oth[...] = mlp


def feed_forward(blocks, nm_own, nm_oth, gm_own, gm_oth, pair, down):
    rows, width = nm_own.shape
    ff = down.shape[1]
    block = min(rows, 256)
    steps = rows // block
    own = pl.BlockSpec((block, width), lambda i: (jnp.minimum(i, steps - 1), 0))
    oth = pl.BlockSpec((block, width), lambda i: (jnp.maximum(i - steps, 0), 0))
    inner = pl.BlockSpec((block, ff), lambda i: (i, 0))
    anywhere = pl.BlockSpec(memory_space=pl.ANY)
    held = jax.ShapeDtypeStruct((2 * rows, ff), bf16)
    part = jax.ShapeDtypeStruct((rows, width), bf16)
    return pl.pallas_call(
        functools.partial(mlp_kernel, steps),
        grid=(2 * steps,),
        in_specs=[own, oth, own, oth] + [anywhere] * 2,
        out_specs=[inner] * 3 + [own, oth, own, oth],
        out_shape=[held] * 3 + [part] * 4,
        scratch_shapes=[pltpu.VMEM((width, ff), bf16)] * 3
        + [pltpu.SemaphoreType.DMA((3, blocks))],
        compiler_params=grid_params(56),
        cost_estimate=cost(
            24 * rows * width * ff, 6 * width * ff + 16 * rows * width, 2 * rows * ff
        ),
    )(nm_own, nm_oth, gm_own, gm_oth, pair, down)


def product_kernel(count, targets, *refs):
    left = refs[:count]
    per = count // 2
    for i in range(targets):
        right = refs[count + i * per : count + (i + 1) * per]
        total = None
        for j in range(count):
            rows = left[j].shape[0]
            value = right[j // 2][(j % 2) * rows : (j % 2 + 1) * rows, :]
            term = dot(left[j][...], value, TN)
            total = term if total is None else total + term
        span = total.shape[0]
        refs[-1][i * span : (i + 1) * span, :] = total.astype(bf16)


def products(lefts, rights, parts):
    rows, width = lefts[0].shape
    ff = rights[0][0].shape[1]
    span = width // parts
    count = len(rights)
    flat = [a for group in rights for a in group]
    return pl.pallas_call(
        functools.partial(product_kernel, len(lefts), count),
        grid=(parts,),
        in_specs=[pl.BlockSpec((rows, span), lambda i: (0, i))] * len(lefts)
        + [pl.BlockSpec(a.shape, lambda i: (0, 0)) for a in flat],
        out_specs=pl.BlockSpec((count * span, ff), lambda i: (i, 0)),
        out_shape=jax.ShapeDtypeStruct((parts * count * span, ff), bf16),
        compiler_params=grid_params(),
        cost_estimate=cost(
            2 * count * len(lefts) * rows * width * ff,
            2 * len(lefts) * rows * width + 2 * count * width * ff,
        ),
    )(*lefts, *flat)


def back_middle_kernel(pieces, ids, *refs):
    resid_ref, cot, gain, grad_ref, attn_ref, gain_ref = refs[pieces:]
    grad_normed = total_of(refs[:pieces])
    resid = resid_ref[...]
    gain_ref[...] = jnp.sum(grad_normed * rms_scale(resid), axis=0, keepdims=True)
    grad = cot[...].astype(f32) + rms_back(resid, grad_normed * gain[...])
    grad_ref[...] = grad
    attn_ref[...] = (res_scale * grad).astype(bf16)


def grad_out_kernel(heads, ids, own, oth, oown, ooth, target):
    nz, _, block, _ = target.shape
    flat = lambda ref: ref[...].reshape(-1, ref.shape[2])
    total = dot(flat(own), flat(oown), TN) + dot(flat(oth), flat(ooth), TN)
    total = total.astype(bf16)
    for i in range(nz):
        for h in range(heads):
            target[ids[1] ^ i, 0, :, h * VDIM : (h + 1) * VDIM] = total[
                i * block : (i + 1) * block, h * LANES : h * LANES + VDIM
            ]


def grad_out_weight(sizes, block, ids, own, oth, oown, ooth):
    nt, nz, nc = sizes
    _, half, width = own.shape
    deep = oown.shape[2]
    heads = deep // LANES
    left = pl.BlockSpec((nc, half, nz * block), lambda j, ids: (0, 0, j))
    right = pl.BlockSpec((nc, half, deep), lambda j, ids: (0, 0, 0))
    return pl.pallas_call(
        functools.partial(grad_out_kernel, heads),
        grid_spec=pltpu.PrefetchScalarGridSpec(
            num_scalar_prefetch=1,
            grid=(nc,),
            in_specs=[left, left, right, right],
            out_specs=pl.BlockSpec((nz, 1, block, heads * VDIM), lambda j, ids: (0, j, 0, 0)),
        ),
        out_shape=jax.ShapeDtypeStruct((nz, nc, block, heads * VDIM), bf16),
        compiler_params=grid_params(),
        cost_estimate=cost(4 * nc * half * width * deep, 4 * nc * half * (width + deep)),
    )(ids, own, oth, oown, ooth)


def grad_latent_kernel(ids, gq, gkv, wq, wkv, keep, give, inner):
    half = keep.shape[1]
    qrank = wq.shape[0]
    inner[:, :qrank] = dot(gq[...], wq[...], NT)
    inner[:, qrank:] = dot(gkv[...], wkv[...], NT)
    keep[0] = inner[pl.ds(pl.multiple_of(ids[0] * half, half), half), :]
    give[0] = inner[pl.ds(pl.multiple_of((1 - ids[0]) * half, half), half), :].astype(bf16)


def grad_latent(sizes, ids, gq, gkv, wq, wkv):
    nt, _, nc = sizes
    length, deep = gq.shape
    block = length // nc
    half = block // nt
    width = wq.shape[0] + wkv.shape[0]
    rows = pl.BlockSpec((block, deep), lambda k, ids: (ids[2] ^ k, 0))
    whole = lambda a: pl.BlockSpec(a.shape, lambda k, ids: (0, 0))
    piece = pl.BlockSpec((1, half, width), lambda k, ids: (k, 0, 0))
    return pl.pallas_call(
        grad_latent_kernel,
        grid_spec=pltpu.PrefetchScalarGridSpec(
            num_scalar_prefetch=1,
            grid=(nc,),
            in_specs=[rows, rows, whole(wq), whole(wkv)],
            out_specs=[piece, piece],
            scratch_shapes=[pltpu.VMEM((block, width), f32)],
        ),
        out_shape=[
            jax.ShapeDtypeStruct((nc, half, width), f32),
            jax.ShapeDtypeStruct((nc, half, width), bf16),
        ],
        compiler_params=grid_params(),
        cost_estimate=cost(2 * length * deep * width, 4 * length * deep + 4 * width * deep),
    )(ids, gq, gkv, wq, wkv)


def grad_ups_kernel(qn, kvn, gq, gkv, target):
    qrank = qn.shape[1]
    both = dot(qn[...], gq[...], TN)
    straight, turned = both[:, :LANES], both[:, LANES:]
    lane = lax.broadcasted_iota(jnp.int32, straight.shape, 1)
    half = ROPE // 2
    low = (lane >= NOPE) & (lane < NOPE + half)
    high = (lane >= NOPE + half) & (lane < NOPE + ROPE)
    straight = straight + jnp.where(low, pltpu.roll(turned, LANES - half, 1), 0.0)
    straight = straight - jnp.where(high, pltpu.roll(turned, half, 1), 0.0)
    target[:qrank, :] = straight.astype(bf16)
    both = dot(kvn[:, :KVRANK], gkv[...], TN)
    lane = lax.broadcasted_iota(jnp.int32, (KVRANK, LANES), 1)
    values = pltpu.roll(both[:, LANES:], NOPE, 1)
    target[qrank:, :] = jnp.where(lane < NOPE, both[:, :LANES], values).astype(bf16)


def grad_ups(qn, kvn, gq, gkv):
    length, qrank = qn.shape
    heads = gq.shape[1] // (2 * LANES)
    whole = lambda a: pl.BlockSpec(a.shape, lambda h: (0, 0))
    column = pl.BlockSpec((length, 2 * LANES), lambda h: (0, h))
    return pl.pallas_call(
        grad_ups_kernel,
        grid=(heads,),
        in_specs=[whole(qn), whole(kvn), column, column],
        out_specs=pl.BlockSpec((qrank + KVRANK, LANES), lambda h: (0, h)),
        out_shape=jax.ShapeDtypeStruct((qrank + KVRANK, heads * LANES), bf16),
        compiler_params=grid_params(),
        cost_estimate=cost(
            4 * length * (qrank + KVRANK) * heads * LANES, 2 * length * (qrank + heads * 4 * LANES)
        ),
    )(qn, kvn, gq, gkv)


def finish_ups_kernel(heads, pieces, ids, source, q_ref, kv_ref):
    qrank = q_ref.shape[0]
    wide = NOPE + ROPE
    for j in range(pieces):
        value = source[ids[2] ^ j]
        for h in range(heads):
            start = (j * heads + h) * wide
            q_ref[:, start : start + wide] = value[:qrank, h * LANES : h * LANES + wide].astype(f32)
        start = j * heads * LANES
        kv_ref[:, start : start + heads * LANES] = value[qrank:, :].astype(f32)


def grad_enter_kernel(pieces, ids, *refs):
    q_ref, kv_ref, gain_query, gain_latent, cosine, sine, turned, lat_ref, gain_q, gain_kv = refs[
        pieces:
    ]
    qrank = q_ref.shape[1]
    total = total_of(refs[:pieces])
    q_latent, c_latent = q_ref[...], kv_ref[:, :KVRANK]
    grad_q, grad_c, grad_rope = total[:, :qrank], total[:, qrank : qrank + KVRANK], total[:, qrank + KVRANK : qrank + KVRANK + ROPE]
    gain_q[...] = jnp.sum(grad_q * rms_scale(q_latent), axis=0, keepdims=True)
    c_round = rms_scale(c_latent).astype(bf16).astype(f32)
    gain_kv[...] = jnp.sum(grad_c * c_round, axis=0, keepdims=True)
    lat_ref[:, :qrank] = rms_back(q_latent, grad_q * gain_query[...]).astype(bf16)
    lat_ref[:, qrank : qrank + KVRANK] = rms_back(c_latent, grad_c * gain_latent[...]).astype(bf16)
    other = jnp.dot(
        grad_rope * sine[...], turned[...], precision=lax.Precision.HIGHEST, preferred_element_type=f32
    )
    end = qrank + KVRANK + ROPE
    lat_ref[:, qrank + KVRANK : end] = (grad_rope * cosine[...] - other).astype(bf16)
    lat_ref[:, end:] = jnp.zeros((lat_ref.shape[0], lat_ref.shape[1] - end), bf16)


def grad_tokens_kernel(
    sizes, block, ids, lat, w_qa, w_kva, tok, gain_in, grad_ref, target, gain_ref, inner
):
    nt, nz, nc = sizes
    half = lat.shape[0]
    qrank = w_qa.shape[1]
    grad = dot(lat[:, :qrank], w_qa[...], NT) + dot(
        lat[:, qrank : qrank + KVRANK + ROPE], w_kva[...], NN
    )
    here = pl.ds(pl.multiple_of(ids[0] * half, half), half)
    hidden = tok[here, :].astype(f32)
    gain_ref[...] = jnp.sum(grad * rms_scale(hidden), axis=0, keepdims=True)
    move_blocks(grad_ref, inner, nc, nz, block)
    target[...] = (inner[...] + rms_back(hidden, grad * gain_in[...])).astype(bf16)


def grad_down_kernel(share, ids, own, oth, gown, goth, target):
    nz, block, wide = target.shape
    flat = lambda ref: ref[...].reshape(-1, ref.shape[2])
    columns = pl.ds(pl.multiple_of(ids[0] * share, share), wide)
    right = lambda ref: ref[:, :, columns].reshape(-1, wide)
    total = (dot(flat(own), right(gown), TN) + dot(flat(oth), right(goth), TN)).astype(bf16)
    for i in range(nz):
        target[ids[1] ^ i] = total[i * block : (i + 1) * block, :]


def finish_down_kernel(share, ids, own, oth, q_ref, kv_ref):
    first = jnp.where(ids[0] == 0, own[...], oth[...]).astype(f32)
    second = jnp.where(ids[0] == 0, oth[...], own[...]).astype(f32)
    rest = q_ref.shape[1] - share
    q_ref[:, :share] = first[:, :share]
    q_ref[:, share:] = second[:, :rest]
    kv_ref[...] = second[:, rest : rest + kv_ref.shape[1]]


def body(
    sizes,
    tokens,
    segments,
    gain_attn,
    w_qa,
    gain_q,
    w_kva,
    gain_kv,
    w_qb,
    w_kvb,
    w_o,
    gain_mlp,
    w_gate,
    w_up,
    w_down,
    cotangent,
):
    nt, nz, nc = sizes
    t, z, c = lax.axis_index("tensor"), lax.axis_index("dp"), lax.axis_index("ctx")
    ids = jnp.stack([t, z, c]).astype(jnp.int32)
    rows, width = tokens.shape[1:]
    half = rows // nt
    block = w_o.shape[0]
    length = nc * rows
    heads = w_qb.shape[1] // (NOPE + ROPE) // nc
    ff = w_gate.shape[1] // nz
    qrank, kvrank = w_qa.shape[1], w_kva.shape[1]
    w_kva = w_kva.T
    lat_width = -(-(qrank + kvrank) // LANES) * LANES
    line = nz == 4

    def turn_gain(value):
        return jnp.swapaxes(value.reshape(nz, nc, block), 0, 1).reshape(1, width)

    def swap(value):
        return exchange(value, "tensor", 1, nt)

    def along_ctx(value):
        if nc != 4:
            return [value] + [exchange(value, "ctx", k, nc) for k in range(1, nc)]
        cut = value.shape[0] // 2
        first, second = exchange(value, "ctx", 1, nc), exchange(value, "ctx", 2, nc)
        upper = exchange(second[:cut], "ctx", 1, nc)
        lower = exchange(first[cut:], "ctx", 2, nc)
        return [value, first, second, jnp.concatenate([upper, lower])]

    def back_ctx(parts):
        if nc != 4:
            return across(parts, "ctx", nc)
        cut = parts[0].shape[0] // 2
        upper = exchange(parts[3][:cut], "ctx", 1, nc).astype(f32)
        lower = exchange(parts[3][cut:], "ctx", 2, nc).astype(f32)
        first, second = parts[1].astype(f32), parts[2].astype(f32)
        first = jnp.concatenate([first[:cut], first[cut:] + lower]).astype(bf16)
        second = jnp.concatenate([second[:cut] + upper, second[cut:]]).astype(bf16)
        return [parts[0], exchange(first, "ctx", 1, nc), exchange(second, "ctx", 2, nc)]

    def gather_dp(value):
        if not line:
            return [value] + [exchange(value, "dp", k, nz) for k in range(1, nz)]
        first, second = exchange(value, "dp", 1, nz), exchange(value, "dp", 2, nz)
        near = lax.ppermute(value, "dp", [(1, 2), (2, 1)])
        far = lax.ppermute(second, "dp", [(1, 0), (2, 3)])
        return [value, first, second, jnp.where((z == 0) | (z == 3), far, near)]

    def scatter_dp(parts):
        if not line:
            return [parts[0]] + [exchange(parts[k], "dp", k, nz) for k in range(1, nz)]
        far = lax.ppermute(parts[3], "dp", [(0, 1), (3, 2)])
        first = exchange(parts[1], "dp", 1, nz)
        near = lax.ppermute(parts[3], "dp", [(1, 2), (2, 1)])
        second = (parts[2].astype(f32) + far.astype(f32)).astype(bf16)
        return [parts[0], first, exchange(second, "dp", 2, nz), near]

    def split_columns(values, axis, at, pieces):
        deep, wide = values[0].shape[0], values[0].shape[1] // pieces
        if pieces > 4:
            parts = jnp.stack(values).reshape(len(values), deep, pieces, wide)
            parts = jnp.moveaxis(parts, 2, 0)
            return [pick(parts, lax.axis_index(axis) ^ k) for k in range(pieces)]
        outs = [((len(values), deep, wide), values[0].dtype)] * pieces
        return plain(functools.partial(split_kernel, at, pieces, len(values)), ids, values, outs)

    def join_columns(parts, axis, at):
        pieces, (count, deep, wide) = len(parts), parts[0].shape
        if pieces > 4:
            stacked = jnp.stack(parts)
            index = lax.axis_index(axis)
            parts = [pick(stacked, index ^ j) for j in range(pieces)]
            return list(jnp.concatenate(parts, axis=2).astype(f32))
        outs = [((deep, pieces * wide), f32)] * count
        return plain(functools.partial(join_kernel, at, pieces), ids, parts, outs)

    def stack_blocks(parts, at):
        count = parts[0].shape[0]
        outs = [((count, len(parts)) + parts[0].shape[1:], parts[0].dtype)]
        return plain(functools.partial(stack_kernel, at, len(parts)), ids, parts, outs)[0]

    def across(parts, axis, size):
        return [parts[0]] + [exchange(parts[k], axis, k, size) for k in range(1, size)]

    def join_rows(own):
        outs = [((rows, width), bf16)]
        return plain(rows_kernel, ids, [own, swap(own)], outs)[0][None]

    def weight_parts(*values):
        return across(split_columns(values, "dp", 1, nz), "dp", nz)

    def gather_weights(parts):
        parts = stack_blocks(parts, 1).reshape(-1, ff)
        return lax.all_gather(parts, "ctx", axis=0, tiled=True)

    def scatter_weights(value):
        return lax.psum_scatter(value, "ctx", scatter_dimension=0, tiled=True)

    def weight_rows(value):
        parts = value.reshape(-1, nz, block, ff)
        parts = [lax.dynamic_index_in_dim(parts, z ^ k, axis=1, keepdims=False) for k in range(nz)]
        return join_columns(across(parts, "dp", nz), "dp", 1)

    def reduce_ctx(keep, give):
        parts = (keep + swap(give).astype(f32)).astype(bf16)
        return back_ctx([parts[k] for k in range(nc)])

    segment_all = segments[0]
    doc_start = jnp.sum((segment_all[None, :] < segment_all[:, None]).astype(jnp.int32), axis=1)
    positions = (jnp.arange(length, dtype=jnp.int32) - doc_start).astype(f32)
    freqs = rope_base ** (-jnp.arange(0, ROPE, 2).astype(f32) / ROPE)
    angles = positions[:, None] * freqs[None, :]
    angles = jnp.concatenate([angles, angles], axis=1)
    cosine, sine = jnp.cos(angles), jnp.sin(angles)
    fill = lambda width, value: jnp.full((length, width), value, f32)
    tail = LANES - NOPE - ROPE
    cos_table = jnp.concatenate([fill(NOPE, 1.0), cosine, fill(tail, 0.0)], axis=1)
    sin_table = jnp.concatenate([fill(NOPE, 0.0), sine, fill(tail, 0.0)], axis=1)
    same = (segment_all[:, None] == jnp.arange(3, dtype=jnp.int32)[None, :]).astype(f32)
    query_table = jnp.concatenate(
        [fill(NOPE + ROPE + 3, 0.0), same * masked_score, fill(tail - 6, 0.0)], axis=1
    )
    key_table = jnp.concatenate(
        [fill(NOPE + ROPE, 0.0), fill(3, 1.0), 1.0 - same, fill(tail - 6, 0.0)], axis=1
    )
    first_row = c * rows + t * half
    own_cos = lax.dynamic_slice_in_dim(cosine, first_row, half)
    own_sin = lax.dynamic_slice_in_dim(sine, first_row, half)
    turned = jnp.asarray(turn_matrix(), f32)

    gain_in = gain_attn.astype(f32)[None]
    gain_query = gain_q.astype(f32)[None]
    gain_latent = gain_kv.astype(f32)[None]
    gain_middle = turn_gain(gain_mlp.astype(f32))

    spread_q = jnp.asarray(spread_queries(heads), bf16)
    spread_k = jnp.asarray(spread_keys(heads), bf16)
    own_qb = lax.dynamic_slice_in_dim(w_qb, c * heads * (NOPE + ROPE), heads * (NOPE + ROPE), axis=1)
    own_kvb = lax.dynamic_slice_in_dim(w_kvb, c * heads * (NOPE + VDIM), heads * (NOPE + VDIM), axis=1)
    wide_qb = dot(own_qb, spread_q, NN).astype(bf16)
    wide_kvb = jnp.concatenate(
        [
            dot(own_kvb, spread_k, NN).astype(bf16),
            jnp.asarray(spread_rope(heads), bf16),
            jnp.zeros((lat_width - qrank - kvrank, heads * 2 * LANES), bf16),
        ],
        axis=0,
    )

    half_of = lambda w, d: ((half, w), d)
    out_parts = across(split_columns([w_o], "ctx", 2, nc), "ctx", nc)
    down_parts = weight_parts(w_down)
    outs = plain(
        functools.partial(enter_kernel, sizes, block),
        ids,
        [
            tokens[0],
            cotangent[0],
            gain_in,
            gain_query,
            gain_latent,
            w_qa,
            w_kva,
            own_cos,
            own_sin,
            turned,
        ],
        [
            half_of(width, bf16),
            half_of(lat_width, bf16),
            half_of(qrank, f32),
            half_of(kvrank, f32),
            half_of(width, bf16),
            half_of(width, bf16),
            half_of(width, bf16),
        ]
        + [half_of(nz * block, bf16)] * nc,
        [pltpu.VMEM((half, width), bf16)] * 2,
        flops=2 * half * width * (qrank + kvrank),
    )
    _, latents, q_latent, kv_latent, own_tokens, own_cotangent, grad_mlp = outs[:7]
    normed_parts = outs[7:]
    lat_parts = along_ctx(latents)
    tables = (cos_table, sin_table, query_table, key_table)

    out_parts[0] = after(out_parts[0], latents)
    own_out = stack_blocks(out_parts, 2)[0]
    down_parts[0] = after(down_parts[0], own_out, wide_qb, wide_kvb, *tables)
    down = gather_weights(down_parts)
    out_pieces = gather_dp(after(own_out, down_parts[1], down_parts[2], down_parts[3]))
    lat_parts[0] = after(lat_parts[0], out_pieces[1])
    lat_own = jnp.stack(lat_parts)
    lat_oth = swap(lat_own)
    pair_parts = weight_parts(after(w_gate, out_pieces[2]), w_up)
    o_own, o_oth, q_rot, keys, values, qn, kvn = attend(
        nt, ids, lat_own, lat_oth, after(wide_qb, out_pieces[2]), wide_kvb, *tables
    )
    out_pieces[0] = after(out_pieces[0], o_own)
    full_out = plain(
        functools.partial(spread_kernel, heads, nz),
        ids,
        out_pieces,
        [((nc, nz, block, heads * LANES), bf16)],
    )[0].reshape(width, heads * LANES)
    keep, give = project_out(o_own, o_oth, full_out)
    pair_parts[0] = after(pair_parts[0], keep)
    pair = gather_weights(pair_parts)
    gm = gather_dp(after(grad_mlp, *pair_parts[1:]))
    attn = reduce_ctx(keep, give)
    resid, normed_mid = plain(
        functools.partial(middle_kernel, len(attn)),
        ids,
        attn + [own_tokens, gain_middle],
        [half_of(width, f32), half_of(width, bf16)],
    )
    nm = gather_dp(after(normed_mid, gm[1]))
    groups = [range(0, nz // 2), range(nz // 2, nz)]
    nm_all, gm_all, hidden, grad_gate, grad_up, grad_parts, mlp_parts = [], [], [], [], [], [], []
    for group in groups:
        nm_own = jnp.concatenate([nm[k] for k in group])
        gm_own = jnp.concatenate([gm[k] for k in group])
        if hidden:
            nm_own = after(nm_own, hidden[0])
        nm_oth, gm_oth = swap(nm_own), swap(gm_own)
        nm_all += [nm_own, nm_oth]
        gm_all += [gm_own, gm_oth]
        hid, gg, gu, gn_own, gn_oth, ml_own, ml_oth = feed_forward(
            nc, nm_own, nm_oth, gm_own, gm_oth, pair, down
        )
        hidden.append(hid)
        grad_gate.append(gg)
        grad_up.append(gu)
        for parts, own, oth in ((grad_parts, gn_own, gn_oth), (mlp_parts, ml_own, ml_oth)):
            total = (own.astype(f32) + swap(oth).astype(f32)).astype(bf16)
            parts += [total[i * half : (i + 1) * half] for i in range(len(group))]
    grad_normed = scatter_dp(grad_parts)
    gm_all[0] = after(gm_all[0], grad_normed[1])
    down_product = products(gm_all, [hidden], nc)
    down_product = scatter_weights(down_product)
    nm_all[0] = after(nm_all[0], grad_normed[3])
    pair_product = products(nm_all, [grad_gate, grad_up], nc)
    grad_normed[0] = after(grad_normed[0], pair_product)

    grad_resid, grad_attn, grad_gain_mlp = plain(
        functools.partial(back_middle_kernel, nz),
        ids,
        grad_normed + [resid, own_cotangent, gain_middle],
        [half_of(width, f32), half_of(width, bf16), ((1, width), f32)],
    )
    ga_parts = along_ctx(grad_attn)
    mlp_parts = scatter_dp([after(part, grad_attn) for part in mlp_parts])
    ga_own = jnp.stack(ga_parts)
    ga_oth = swap(ga_own)
    pair_product = scatter_weights(after(pair_product, ga_own))
    g_own, g_oth = project_heads(ga_own, ga_oth, full_out)
    grad_q, grad_kv = attend_back(
        nt, ids, q_rot, keys, values, o_own, o_oth, g_own, g_oth, cos_table, sin_table
    )
    mlp_parts[0] = after(mlp_parts[0], grad_q)
    layer_out = plain(
        functools.partial(leave_kernel, sizes, block, nz),
        ids,
        mlp_parts + [resid],
        [half_of(width, bf16)],
        [pltpu.VMEM((half, width), f32)],
    )[0]
    (grad_w_down,) = weight_rows(after(down_product, *mlp_parts))
    grad_lat = reduce_ctx(*grad_latent(sizes, ids, grad_q, grad_kv, wide_qb, wide_kvb))

    ups = grad_ups(qn, after(kvn, grad_lat[0]), grad_q, grad_kv)
    deep = ups.shape[0] // nz
    ups = ups.reshape(nz, deep, heads * LANES)
    ups = scatter_dp([pick(ups, z ^ k) for k in range(nz)])
    out_product = grad_out_weight(
        sizes, block, ids, ga_own, after(ga_oth, grad_lat[0], ups[0]), o_own, o_oth
    )
    grad_lat[0] = after(grad_lat[0], out_product)
    grad_lat, grad_gain_q, grad_gain_kv = plain(
        functools.partial(grad_enter_kernel, len(grad_lat)),
        ids,
        grad_lat + [q_latent, kv_latent, gain_query, gain_latent, own_cos, own_sin, turned],
        [half_of(lat_width, bf16), ((1, qrank), f32), ((1, KVRANK), f32)],
    )
    gl_parts = along_ctx(grad_lat)
    grad_tokens, grad_gain_attn = plain(
        functools.partial(grad_tokens_kernel, sizes, block),
        ids,
        [grad_lat, w_qa, w_kva, tokens[0], gain_in, grad_resid],
        [half_of(width, bf16), ((1, width), f32)],
        [pltpu.VMEM((half, width), f32)],
        flops=2 * half * width * (qrank + kvrank),
    )
    ups[0] = after(ups[0], grad_lat)
    own = sum(p.astype(f32) for p in ups).astype(bf16)
    ups = gather_dp(own)
    out_parts = scatter_dp([out_product[k] for k in range(nz)])
    gl_parts[0] = after(gl_parts[0], grad_tokens)
    gl_own = jnp.stack(gl_parts)
    gl_oth = swap(gl_own)

    xin_own = jnp.stack(across(normed_parts, "ctx", nc))
    xin_oth = swap(xin_own)
    share = lat_width // nt // LANES * LANES
    wide = lat_width - share
    parts = plain(
        functools.partial(grad_down_kernel, share),
        ids,
        [xin_own, xin_oth, gl_own, gl_oth],
        [((nz, block, wide), bf16)],
        flops=2 * length * nz * block * wide,
    )[0]
    ups[0] = after(ups[0], parts)
    ups = stack_blocks([piece[None] for piece in ups], 1).reshape(nz * deep, heads * LANES)
    ups = along_ctx(ups)
    out_parts[0] = after(out_parts[0], parts)
    own = sum(p.astype(f32) for p in out_parts).astype(bf16)
    out_parts = across([pick(own, c ^ k)[None] for k in range(nc)], "ctx", nc)
    own = scatter_dp([parts[k] for k in range(nz)])
    grad_w_gate, grad_w_up = weight_rows(after(pair_product, own[-1]))
    own = sum(p.astype(f32) for p in own).astype(bf16)
    grad_w_qa, grad_w_kva = plain(
        functools.partial(finish_down_kernel, share),
        ids,
        [own, swap(own)],
        [((block, qrank), f32), ((block, kvrank), f32)],
    )
    (grad_w_o,) = join_columns(out_parts, "ctx", 2)
    grad_w_qb, grad_w_kvb = plain(
        functools.partial(finish_ups_kernel, heads, nc),
        ids,
        [jnp.stack(ups)],
        [((qrank, nc * heads * (NOPE + ROPE)), f32), ((KVRANK, nc * heads * LANES), f32)],
    )
    layer_out = join_rows(layer_out)
    grad_tokens = join_rows(grad_tokens)

    turned_gain = jnp.swapaxes(grad_gain_mlp.reshape(nc, nz, block), 0, 1).reshape(1, width)
    gains = jnp.concatenate([grad_gain_attn, grad_gain_q, grad_gain_kv, turned_gain], axis=1)
    gains = gains.reshape(-1, LANES)
    for axis, size in (("tensor", nt), ("ctx", nc), ("dp", nz)):
        step = 1
        while step < size:
            gains = gains + exchange(gains, axis, step, size)
            step *= 2
    gains = gains.reshape(-1)
    ends = np.cumsum([width, qrank, KVRANK])
    grad_gain_attn, grad_gain_q, grad_gain_kv, grad_gain_mlp = jnp.split(gains, ends)
    return (
        layer_out,
        grad_tokens,
        grad_gain_attn,
        grad_w_qa,
        grad_gain_q,
        grad_w_kva,
        grad_gain_kv,
        grad_w_qb,
        grad_w_kvb,
        grad_w_o,
        grad_gain_mlp,
        grad_w_gate,
        grad_w_up,
        grad_w_down,
    )


def solution(mesh):
    placed = (
        P("dp", "ctx", None),
        P("dp", None),
        P(),
        P(),
        P(),
        P(),
        P(),
        P(None, "tensor"),
        P(None, "tensor"),
        P(("dp", "ctx"), "tensor"),
        P(),
        P(("dp", "ctx"), "tensor"),
        P(("dp", "ctx"), "tensor"),
        P(("dp", "ctx"), "tensor"),
        P("dp", "ctx", None),
    )
    sizes = tuple(mesh.shape[name] for name in ("tensor", "dp", "ctx"))
    return jax.shard_map(
        functools.partial(body, sizes),
        mesh=mesh,
        in_specs=placed,
        out_specs=(
            P("dp", "ctx", None),
            P("dp", "ctx", None),
            P(),
            P(("dp", "ctx"), None),
            P(),
            P(("dp", "ctx"), None),
            P(),
            P(None, "tensor"),
            P(None, "tensor"),
            P(("dp", "ctx"), "tensor"),
            P(),
            P(("dp", "ctx"), "tensor"),
            P(("dp", "ctx"), "tensor"),
            P(("dp", "ctx"), "tensor"),
        ),
        check_vma=False,
    )
```

```python
import functools
import math

import jax
import jax.numpy as jnp
import numpy as np
from jax import lax
from jax.experimental import pallas as pl
from jax.experimental.pallas import tpu as pltpu
from jax.sharding import PartitionSpec as P

NOPE = 64
ROPE = 32
VDIM = 64
KVRANK = 256
LANES = 128
QUERY_BLOCK = 256

eps_norm = 1e-05
res_scale = 1.4 / math.sqrt(62.0)
rope_base = 10000.0
masked_score = -1e30
score_scale = 1.0 / math.sqrt(NOPE + ROPE)
exponent = score_scale * math.log2(math.e)

f32 = jnp.float32
bf16 = jnp.bfloat16


def rms_scale(values):
    return values * lax.rsqrt(jnp.mean(values * values, axis=-1, keepdims=True) + eps_norm)


def dot(left, right, contract):
    return lax.dot_general(left, right, (contract, ((), ())), preferred_element_type=f32)


NN = ((1,), (0,))
NT = ((1,), (1,))
TN = ((0,), (0,))


def exchange(value, axis, step, size):
    return lax.ppermute(value, axis, [(i, i ^ step) for i in range(size)])


def after(value, *done):
    return lax.optimization_barrier((value,) + done)[0]


def pick(stacked, index):
    return lax.dynamic_index_in_dim(stacked, index, axis=0, keepdims=False)


def spread_queries(heads):
    out = np.zeros((heads, NOPE + ROPE, heads, 2, LANES), np.float32)
    half = ROPE // 2
    for h in range(heads):
        for j in range(NOPE + ROPE):
            out[h, j, h, 0, j] = 1.0
        for j in range(half):
            out[h, NOPE + half + j, h, 1, NOPE + j] = -1.0
            out[h, NOPE + j, h, 1, NOPE + half + j] = 1.0
    return out.reshape(heads * (NOPE + ROPE), heads * 2 * LANES)


def spread_keys(heads):
    out = np.zeros((heads, NOPE + VDIM, heads, 2, LANES), np.float32)
    for h in range(heads):
        for j in range(NOPE):
            out[h, j, h, 0, j] = 1.0
        for j in range(VDIM):
            out[h, NOPE + j, h, 1, j] = 1.0
    return out.reshape(heads * (NOPE + VDIM), heads * 2 * LANES)


def spread_rope(heads):
    out = np.zeros((ROPE, heads, 2, LANES), np.float32)
    for j in range(ROPE):
        out[j, :, 0, NOPE + j] = 1.0
    return out.reshape(ROPE, heads * 2 * LANES)


def spread_values(heads):
    out = np.zeros((heads, VDIM, heads, LANES), np.float32)
    for h in range(heads):
        for j in range(VDIM):
            out[h, j, h, j] = 1.0
    return out.reshape(heads * VDIM, heads * LANES)


def split_low(value):
    first = value.astype(bf16).astype(f32)
    second = (value - first).astype(bf16).astype(f32)
    third = (value - first - second).astype(bf16).astype(f32)
    return first, second, third


def rms_back(values, grad):
    inverse = lax.rsqrt(jnp.mean(values * values, axis=-1, keepdims=True) + eps_norm)
    scaled = values * inverse
    return (grad - scaled * jnp.mean(grad * scaled, axis=-1, keepdims=True)) * inverse


def turn_matrix():
    half = ROPE // 2
    out = np.zeros((ROPE, ROPE), np.float32)
    for j in range(half):
        out[half + j, j] = -1.0
        out[j, half + j] = 1.0
    return out


def total_of(refs):
    total = refs[0][...].astype(f32)
    for ref in refs[1:]:
        total = total + ref[...].astype(f32)
    return total


def move_blocks(source, target, outer, inner, block, cast=None):
    for i in range(outer):
        for j in range(inner):
            value = source[:, (i * inner + j) * block : (i * inner + j + 1) * block]
            target[:, (j * outer + i) * block : (j * outer + i + 1) * block] = (
                value if cast is None else cast(value)
            )


SCALARS = pl.BlockSpec(memory_space=pltpu.SMEM)
LOCAL = pl.BlockSpec(memory_space=pltpu.VMEM)


def params(megabytes=48):
    return pltpu.CompilerParams(vmem_limit_bytes=megabytes * 1024 * 1024)


def grid_params(megabytes=48):
    return pltpu.CompilerParams(
        dimension_semantics=("arbitrary",), vmem_limit_bytes=megabytes * 1024 * 1024
    )


def cost(flops=0, moved=0, special=0):
    return pl.CostEstimate(
        flops=flops // 10, bytes_accessed=moved // 10, transcendentals=special // 10
    )


def plain(kernel, ids, operands, outs, scratch=(), flops=0, megabytes=48):
    moved = sum(a.size * a.dtype.itemsize for a in operands)
    moved += sum(math.prod(s) * jnp.dtype(d).itemsize for s, d in outs)
    return pl.pallas_call(
        kernel,
        in_specs=[SCALARS] + [LOCAL] * len(operands),
        out_specs=[LOCAL] * len(outs),
        out_shape=[jax.ShapeDtypeStruct(s, d) for s, d in outs],
        scratch_shapes=list(scratch),
        compiler_params=params(megabytes),
        cost_estimate=cost(flops, moved),
    )(ids, *operands)


def enter_kernel(
    sizes, block, ids, tok, cot, gain_in, gain_query, gain_latent, w_qa, w_kva, cosine, sine, turned,
    normed_ref, lat_ref, q_ref, kv_ref, x_ref, cot_ref, gm_ref, *rest
):
    nt, nz, nc = sizes
    pieces, (inner, plain_ref) = rest[:nc], rest[nc:]
    half = normed_ref.shape[0]
    qrank = w_qa.shape[1]
    here = pl.ds(pl.multiple_of(ids[0] * half, half), half)
    own = tok[here, :]
    hidden = own.astype(f32)
    normed = (rms_scale(hidden) * gain_in[...]).astype(bf16)
    normed_ref[...] = normed
    q_latent = dot(normed, w_qa[...], NN)
    kv_latent = dot(normed, w_kva[...], NT)
    q_ref[...] = q_latent
    kv_ref[...] = kv_latent
    lat_ref[:, :qrank] = (rms_scale(q_latent) * gain_query[...]).astype(bf16)
    c_round = rms_scale(kv_latent[:, :KVRANK]).astype(bf16).astype(f32)
    lat_ref[:, qrank : qrank + KVRANK] = (c_round * gain_latent[...]).astype(bf16)
    rope = kv_latent[:, KVRANK:]
    other = jnp.dot(rope, turned[...], precision=lax.Precision.HIGHEST, preferred_element_type=f32)
    end = qrank + KVRANK + ROPE
    lat_ref[:, qrank + KVRANK : end] = (rope * cosine[...] + other * sine[...]).astype(bf16)
    lat_ref[:, end:] = jnp.zeros((half, lat_ref.shape[1] - end), bf16)
    move_blocks(normed_ref, inner, nz, nc, block)
    span = nz * block
    for k in range(nc):
        start = pl.multiple_of((ids[2] ^ k) * span, span)
        pieces[k][...] = inner[:, pl.ds(start, span)]
    plain_ref[...] = own
    move_blocks(plain_ref, x_ref, nz, nc, block)
    plain_ref[...] = cot[here, :]
    move_blocks(plain_ref, cot_ref, nz, nc, block)
    gm_ref[...] = (res_scale * cot_ref[...].astype(f32)).astype(bf16)


def forward_kernel(
    nt, ids, own_ref, oth_ref, wq_ref, wkv_ref, cos_ref, sin_ref, qtab_ref, ktab_ref,
    oown_ref, ooth_ref, q_ref, k_ref, v_ref, qn_ref, kvn_ref
):
    t, c = ids[0], ids[2]
    nc, half = own_ref.shape[0], own_ref.shape[1]
    length, qrank = qn_ref.shape
    block = nt * half

    @pl.when(pl.program_id(0) == 0)
    def _():
        for j in range(nc):
            for i in range(nt):
                rows = pl.ds((j * nt + i) * half, half)
                value = jnp.where(t == i, own_ref[c ^ j], oth_ref[c ^ j])
                qn_ref[rows, :] = value[:, :qrank]
                kvn_ref[rows, :] = value[:, qrank:]

    raw = jnp.dot(qn_ref[...], wq_ref[...], preferred_element_type=f32)
    query = raw[:, :LANES] * cos_ref[...] + raw[:, LANES:] * sin_ref[...] + qtab_ref[...]
    q_ref[...] = query.astype(bf16)
    both = jnp.dot(kvn_ref[...], wkv_ref[...], preferred_element_type=f32)
    k_ref[...] = (both[:, :LANES] + ktab_ref[...]).astype(bf16)
    lane = lax.broadcasted_iota(jnp.int32, (length, LANES), 1)
    ones = (lane >= VDIM) & (lane < VDIM + 3)
    v_ref[...] = jnp.where(ones, 1.0, both[:, LANES:]).astype(bf16)
    lane = lax.broadcasted_iota(jnp.int32, (block, LANES), 1)
    after = lax.broadcasted_iota(jnp.int32, (block, block), 1) > lax.broadcasted_iota(
        jnp.int32, (block, block), 0
    )
    for i in range(nc):
        here = pl.ds(i * block, block)
        query = q_ref[here, :]
        own = dot(query, k_ref[here, :], NT)
        own = jnp.where(after, masked_score, own)
        highest = jnp.max(own, axis=1, keepdims=True)
        if i:
            before = pl.ds(0, i * block)
            past = dot(query, k_ref[before, :], NT)
            highest = jnp.maximum(highest, jnp.max(past, axis=1, keepdims=True))
        weights = jnp.exp2((own - highest) * exponent).astype(bf16)
        mixed = dot(weights, v_ref[here, :], NN)
        if i:
            weights = jnp.exp2((past - highest) * exponent).astype(bf16)
            mixed = mixed + dot(weights, v_ref[before, :], NN)
        total = mixed[:, VDIM : VDIM + 1]
        out = jnp.where(lane < VDIM, mixed / total, 0.0).astype(bf16)
        for j in range(nt):
            part = out[j * half : (j + 1) * half]

            @pl.when(t == j)
            def _():
                oown_ref[c ^ i] = part

            @pl.when(t != j)
            def _():
                ooth_ref[c ^ i] = part

        first, second, third = split_low(-(highest + jnp.log2(total) / exponent))
        at = NOPE + ROPE
        kept = jnp.where(
            lane == at,
            first,
            jnp.where(lane == at + 1, second, jnp.where(lane == at + 2, third, query.astype(f32))),
        )
        q_ref[here, :] = kept.astype(bf16)


def backward_kernel(
    nt, ids, q_ref, k_ref, v_ref, oown_ref, ooth_ref, gown_ref, goth_ref, cos_ref, sin_ref,
    dq_ref, dkv_ref, grad_ref, dk_acc, dv_acc
):
    t, c = ids[0], ids[2]
    nc, half = gown_ref.shape[0], gown_ref.shape[1]
    length = q_ref.shape[0]
    block = nt * half
    lane = lax.broadcasted_iota(jnp.int32, (half, LANES), 1)
    for j in range(nc):
        for i in range(nt):
            grad = jnp.where(t == i, gown_ref[c ^ j], goth_ref[c ^ j]).astype(f32)
            out = jnp.where(t == i, oown_ref[c ^ j], ooth_ref[c ^ j]).astype(f32)
            first, second, third = split_low(-jnp.sum(grad * out, axis=1, keepdims=True))
            grad = jnp.where(
                lane == VDIM,
                first,
                jnp.where(lane == VDIM + 1, second, jnp.where(lane == VDIM + 2, third, grad)),
            )
            grad_ref[pl.ds((j * nt + i) * half, half), :] = grad.astype(bf16)
    after = lax.broadcasted_iota(jnp.int32, (block, block), 0) > lax.broadcasted_iota(
        jnp.int32, (block, block), 1
    )
    for i in reversed(range(nc)):
        here = pl.ds(i * block, block)
        query, grad = q_ref[here, :], grad_ref[here, :]

        def part(span, masked):
            keys = k_ref[span, :]
            scores = dot(keys, query, NT)
            if masked:
                scores = jnp.where(after, masked_score, scores)
            probs = jnp.exp2(scores * exponent)
            inward = dot(v_ref[span, :], grad, NT)
            low = (probs * inward).astype(bf16)
            dv = dot(probs.astype(bf16), grad, NN)
            dk = dot(low, query, NN)
            if i == nc - 1:
                dv_acc[span, :] = dv
                dk_acc[span, :] = dk
            else:
                dv_acc[span, :] += dv
                dk_acc[span, :] += dk
            return dot(low, keys, TN)

        dq = part(here, True)
        if i:
            dq = dq + part(pl.ds(0, i * block), False)
        dq = dq * score_scale
        dq_ref[here, :LANES] = (dq * cos_ref[here, :]).astype(bf16)
        dq_ref[here, LANES:] = (dq * sin_ref[here, :]).astype(bf16)
    lane = lax.broadcasted_iota(jnp.int32, (length, LANES), 1)
    dkv_ref[:, :LANES] = jnp.where(lane < NOPE + ROPE, dk_acc[...] * score_scale, 0.0).astype(bf16)
    dkv_ref[:, LANES:] = jnp.where(lane < VDIM, dv_acc[...], 0.0).astype(bf16)


def attend(nt, ids, own, oth, wq, wkv, cosine, sine, qtab, ktab):
    nc, half, _ = own.shape
    length = nc * nt * half
    qrank, kvrank = wq.shape[0], wkv.shape[0]
    heads = wq.shape[1] // (2 * LANES)
    whole = lambda a: pl.BlockSpec(a.shape, lambda h, ids: (0,) * a.ndim)
    column = lambda rows, width: pl.BlockSpec((rows, width), lambda h, ids: (0, h))
    split = pl.BlockSpec((nc, half, LANES), lambda h, ids: (0, 0, h))
    out = jax.ShapeDtypeStruct((length, heads * LANES), bf16)
    out_split = jax.ShapeDtypeStruct((nc, half, heads * LANES), bf16)
    kept = [jax.ShapeDtypeStruct((length, qrank), bf16), jax.ShapeDtypeStruct((length, kvrank), bf16)]
    return pl.pallas_call(
        functools.partial(forward_kernel, nt),
        grid_spec=pltpu.PrefetchScalarGridSpec(
            num_scalar_prefetch=1,
            grid=(heads,),
            in_specs=[
                whole(own),
                whole(oth),
                column(qrank, 2 * LANES),
                column(kvrank, 2 * LANES),
                whole(cosine),
                whole(sine),
                whole(qtab),
                whole(ktab),
            ],
            out_specs=[split] * 2 + [column(length, LANES)] * 3 + [whole(a) for a in kept],
        ),
        out_shape=[out_split] * 2 + [out] * 3 + kept,
        compiler_params=grid_params(),
        cost_estimate=cost(
            4 * heads * length * (length * LANES + qrank * 2 * LANES),
            16 * length * heads * LANES,
            heads * length * length // 2,
        ),
    )(ids, own, oth, wq, wkv, cosine, sine, qtab, ktab)


def attend_back(nt, ids, q, k, v, oown, ooth, gown, goth, cosine, sine):
    nc, half, _ = oown.shape
    length = q.shape[0]
    heads = q.shape[1] // LANES
    whole = lambda a: pl.BlockSpec(a.shape, lambda h, ids: (0, 0))
    column = lambda width: pl.BlockSpec((length, width), lambda h, ids: (0, h))
    split = pl.BlockSpec((nc, half, LANES), lambda h, ids: (0, 0, h))
    out = jax.ShapeDtypeStruct((length, heads * 2 * LANES), bf16)
    return pl.pallas_call(
        functools.partial(backward_kernel, nt),
        grid_spec=pltpu.PrefetchScalarGridSpec(
            num_scalar_prefetch=1,
            grid=(heads,),
            in_specs=[column(LANES)] * 3 + [split] * 4 + [whole(cosine), whole(sine)],
            out_specs=[column(2 * LANES)] * 2,
            scratch_shapes=[
                pltpu.VMEM((length, LANES), bf16),
                pltpu.VMEM((length, LANES), f32),
                pltpu.VMEM((length, LANES), f32),
            ],
        ),
        out_shape=[out] * 2,
        compiler_params=grid_params(),
        cost_estimate=cost(
            8 * heads * length * length * LANES,
            24 * length * heads * LANES,
            heads * length * length // 2,
        ),
    )(ids, q, k, v, oown, ooth, gown, goth, cosine, sine)


def split_kernel(axis, pieces, count, ids, *refs):
    width = refs[count].shape[2]
    for k in range(pieces):
        for j in range(pieces):

            @pl.when((ids[axis] ^ k) == j)
            def _():
                for i in range(count):
                    refs[count + k][i] = refs[i][:, j * width : (j + 1) * width]


def join_kernel(axis, pieces, ids, *refs):
    targets = refs[pieces:]
    width = refs[0].shape[2]
    for k in range(pieces):
        for j in range(pieces):

            @pl.when((ids[axis] ^ k) == j)
            def _():
                for i, target in enumerate(targets):
                    target[:, j * width : (j + 1) * width] = refs[k][i].astype(target.dtype)


def stack_kernel(axis, pieces, ids, *refs):
    for k in range(pieces):
        for i in range(refs[k].shape[0]):
            refs[pieces][i, ids[axis] ^ k] = refs[k][i]


def rows_kernel(ids, own, oth, target):
    half = own.shape[0]
    target[pl.ds(pl.multiple_of(ids[0] * half, half), half), :] = own[...]
    target[pl.ds(pl.multiple_of((1 - ids[0]) * half, half), half), :] = oth[...]


def spread_kernel(heads, pieces, ids, *refs):
    target = refs[pieces]
    target[...] = jnp.zeros_like(target)
    for k in range(pieces):
        for j in range(refs[k].shape[0]):
            for h in range(heads):
                target[j, ids[1] ^ k, :, h * LANES : h * LANES + VDIM] = refs[k][
                    j, :, h * VDIM : (h + 1) * VDIM
                ]


def out_kernel(own, oth, weight, keep, give):
    per, half, _ = own.shape
    both = jnp.concatenate([ref[i] for ref in (own, oth) for i in range(per)], axis=0)
    result = dot(both, weight[...], NT)
    for i in range(per):
        keep[i] = result[i * half : (i + 1) * half]
        give[i] = result[(per + i) * half : (per + i + 1) * half].astype(bf16)


def project_out(own, oth, weight):
    nc, half, deep = own.shape
    width = weight.shape[0]
    per = math.gcd(nc, 2)
    piece = lambda w: pl.BlockSpec((per, half, w), lambda k: (k, 0, 0))
    return pl.pallas_call(
        out_kernel,
        grid=(nc // per,),
        in_specs=[piece(deep)] * 2 + [pl.BlockSpec(weight.shape, lambda k: (0, 0))],
        out_specs=[piece(width)] * 2,
        out_shape=[
            jax.ShapeDtypeStruct((nc, half, width), f32),
            jax.ShapeDtypeStruct((nc, half, width), bf16),
        ],
        compiler_params=grid_params(),
        cost_estimate=cost(4 * nc * half * deep * width, 2 * weight.size + 16 * nc * half * width),
    )(own, oth, weight)


def heads_kernel(own, oth, weight, gown, goth):
    per, half, _ = own.shape
    both = jnp.concatenate([ref[i] for ref in (own, oth) for i in range(per)], axis=0)
    result = dot(both, weight[...], NN).astype(bf16)
    for i in range(per):
        gown[i] = result[i * half : (i + 1) * half]
        goth[i] = result[(per + i) * half : (per + i + 1) * half]


def project_heads(own, oth, weight):
    nc, half, width = own.shape
    deep = weight.shape[1]
    per = math.gcd(nc, 2)
    piece = lambda w: pl.BlockSpec((per, half, w), lambda k: (k, 0, 0))
    return pl.pallas_call(
        heads_kernel,
        grid=(nc // per,),
        in_specs=[piece(width)] * 2 + [pl.BlockSpec(weight.shape, lambda k: (0, 0))],
        out_specs=[piece(deep)] * 2,
        out_shape=[jax.ShapeDtypeStruct((nc, half, deep), bf16)] * 2,
        compiler_params=grid_params(),
        cost_estimate=cost(4 * nc * half * deep * width, 2 * weight.size + 8 * nc * half * width),
    )(own, oth, weight)


def middle_kernel(pieces, ids, *refs):
    tokens, gain, resid_ref, normed_ref = refs[pieces:]
    resid = tokens[...].astype(f32) + res_scale * total_of(refs[:pieces])
    resid_ref[...] = resid
    normed_ref[...] = (rms_scale(resid) * gain[...]).astype(bf16)


def leave_kernel(sizes, block, pieces, ids, *refs):
    resid, target, inner = refs[pieces:]
    nt, nz, nc = sizes
    inner[...] = resid[...] + res_scale * total_of(refs[:pieces])
    move_blocks(inner, target, nc, nz, block, lambda value: value.astype(bf16))


def mlp_kernel(
    nm_own, nm_oth, gm_own, gm_oth, pair_hbm, down_hbm,
    hid_ref, gg_ref, gu_ref, gn_own, gn_oth, ml_own, ml_oth, w_gate, w_up, w_down, sems
):
    step = pl.program_id(0)
    blocks = sems.shape[1]
    deep = w_down.shape[0] // blocks
    copies = [
        [
            pltpu.make_async_copy(
                source.at[pl.ds((j * count + at) * deep, deep), :],
                target.at[pl.ds(j * deep, deep), :],
                sems.at[i, j],
            )
            for j in range(blocks)
        ]
        for i, (source, count, at, target) in enumerate(
            ((pair_hbm, 2, 0, w_gate), (pair_hbm, 2, 1, w_up), (down_hbm, 1, 0, w_down))
        )
    ]

    def ready(i):
        @pl.when(step == 0)
        def _():
            for copy in copies[i]:
                copy.wait()

    @pl.when(step == 0)
    def _():
        for group in copies:
            for copy in group:
                copy.start()

    block = nm_own.shape[0]
    normed = jnp.concatenate([nm_own[...], nm_oth[...]], axis=0)
    ready(0)
    gate = dot(normed, w_gate[...], NN)
    ready(1)
    up_proj = dot(normed, w_up[...], NN)
    ready(2)
    grad_hidden = dot(jnp.concatenate([gm_own[...], gm_oth[...]], axis=0), w_down[...], NN)
    sigma = jax.nn.sigmoid(gate)
    silu_gate = gate * sigma
    hidden = (silu_gate * up_proj).astype(bf16)
    grad_gate = (grad_hidden * up_proj * sigma * (1.0 + gate * (1.0 - sigma))).astype(bf16)
    grad_up = (grad_hidden * silu_gate).astype(bf16)
    for target, value in ((hid_ref, hidden), (gg_ref, grad_gate), (gu_ref, grad_up)):
        target[0] = value[:block]
        target[1] = value[block:]
    mlp = dot(hidden, w_down[...], NT).astype(bf16)
    ml_own[...] = mlp[:block]
    ml_oth[...] = mlp[block:]
    grad_normed = (dot(grad_gate, w_gate[...], NT) + dot(grad_up, w_up[...], NT)).astype(bf16)
    gn_own[...] = grad_normed[:block]
    gn_oth[...] = grad_normed[block:]


def feed_forward(blocks, nm_own, nm_oth, gm_own, gm_oth, pair, down):
    rows, width = nm_own.shape
    ff = down.shape[1]
    block = min(rows, 256)
    part_of = pl.BlockSpec((block, width), lambda i: (i, 0))
    inner = pl.BlockSpec((2, block, ff), lambda i: (0, i, 0))
    anywhere = pl.BlockSpec(memory_space=pl.ANY)
    held = jax.ShapeDtypeStruct((2, rows, ff), bf16)
    part = jax.ShapeDtypeStruct((rows, width), bf16)
    made = pl.pallas_call(
        mlp_kernel,
        grid=(rows // block,),
        in_specs=[part_of] * 4 + [anywhere] * 2,
        out_specs=[inner] * 3 + [part_of] * 4,
        out_shape=[held] * 3 + [part] * 4,
        scratch_shapes=[pltpu.VMEM((width, ff), bf16)] * 3
        + [pltpu.SemaphoreType.DMA((3, blocks))],
        compiler_params=grid_params(60),
        cost_estimate=cost(
            24 * rows * width * ff, 6 * width * ff + 16 * rows * width, 2 * rows * ff
        ),
    )(nm_own, nm_oth, gm_own, gm_oth, pair, down)
    return [a.reshape(2 * rows, ff) for a in made[:3]] + list(made[3:])


def product_kernel(count, targets, *refs):
    left = refs[:count]
    per = count // 2
    for i in range(targets):
        right = refs[count + i * per : count + (i + 1) * per]
        total = None
        for j in range(count):
            rows = left[j].shape[0]
            value = right[j // 2][(j % 2) * rows : (j % 2 + 1) * rows, :]
            term = dot(left[j][...], value, TN)
            total = term if total is None else total + term
        span = total.shape[0]
        refs[-1][i * span : (i + 1) * span, :] = total.astype(bf16)


def products(lefts, rights, parts):
    rows, width = lefts[0].shape
    ff = rights[0][0].shape[1]
    span = width // parts
    count = len(rights)
    flat = [a for group in rights for a in group]
    return pl.pallas_call(
        functools.partial(product_kernel, len(lefts), count),
        grid=(parts,),
        in_specs=[pl.BlockSpec((rows, span), lambda i: (0, i))] * len(lefts)
        + [pl.BlockSpec(a.shape, lambda i: (0, 0)) for a in flat],
        out_specs=pl.BlockSpec((count * span, ff), lambda i: (i, 0)),
        out_shape=jax.ShapeDtypeStruct((parts * count * span, ff), bf16),
        compiler_params=grid_params(),
        cost_estimate=cost(
            2 * count * len(lefts) * rows * width * ff,
            2 * len(lefts) * rows * width + 2 * count * width * ff,
        ),
    )(*lefts, *flat)


def back_middle_kernel(pieces, ids, *refs):
    resid_ref, cot, gain, grad_ref, attn_ref, gain_ref = refs[pieces:]
    grad_normed = total_of(refs[:pieces])
    resid = resid_ref[...]
    gain_ref[...] = jnp.sum(grad_normed * rms_scale(resid), axis=0, keepdims=True)
    grad = cot[...].astype(f32) + rms_back(resid, grad_normed * gain[...])
    grad_ref[...] = grad
    attn_ref[...] = (res_scale * grad).astype(bf16)


def grad_out_kernel(heads, ids, own, oth, oown, ooth, target):
    nz, _, block, _ = target.shape
    flat = lambda ref: ref[...].reshape(-1, ref.shape[2])
    total = dot(flat(own), flat(oown), TN) + dot(flat(oth), flat(ooth), TN)
    total = total.astype(bf16)
    for i in range(nz):
        for h in range(heads):
            target[ids[1] ^ i, 0, :, h * VDIM : (h + 1) * VDIM] = total[
                i * block : (i + 1) * block, h * LANES : h * LANES + VDIM
            ]


def grad_out_weight(sizes, block, ids, own, oth, oown, ooth):
    nt, nz, nc = sizes
    _, half, width = own.shape
    deep = oown.shape[2]
    heads = deep // LANES
    left = pl.BlockSpec((nc, half, nz * block), lambda j, ids: (0, 0, j))
    right = pl.BlockSpec((nc, half, deep), lambda j, ids: (0, 0, 0))
    return pl.pallas_call(
        functools.partial(grad_out_kernel, heads),
        grid_spec=pltpu.PrefetchScalarGridSpec(
            num_scalar_prefetch=1,
            grid=(nc,),
            in_specs=[left, left, right, right],
            out_specs=pl.BlockSpec((nz, 1, block, heads * VDIM), lambda j, ids: (0, j, 0, 0)),
        ),
        out_shape=jax.ShapeDtypeStruct((nz, nc, block, heads * VDIM), bf16),
        compiler_params=grid_params(),
        cost_estimate=cost(4 * nc * half * width * deep, 4 * nc * half * (width + deep)),
    )(ids, own, oth, oown, ooth)


def grad_latent_kernel(ids, gq, gkv, wq, wkv, keep, give, inner):
    half = keep.shape[1]
    qrank = wq.shape[0]
    inner[:, :qrank] = dot(gq[...], wq[...], NT)
    inner[:, qrank:] = dot(gkv[...], wkv[...], NT)
    keep[0] = inner[pl.ds(pl.multiple_of(ids[0] * half, half), half), :]
    give[0] = inner[pl.ds(pl.multiple_of((1 - ids[0]) * half, half), half), :].astype(bf16)


def grad_latent(sizes, ids, gq, gkv, wq, wkv):
    nt, _, nc = sizes
    length, deep = gq.shape
    block = length // nc
    half = block // nt
    width = wq.shape[0] + wkv.shape[0]
    rows = pl.BlockSpec((block, deep), lambda k, ids: (ids[2] ^ k, 0))
    whole = lambda a: pl.BlockSpec(a.shape, lambda k, ids: (0, 0))
    piece = pl.BlockSpec((1, half, width), lambda k, ids: (k, 0, 0))
    return pl.pallas_call(
        grad_latent_kernel,
        grid_spec=pltpu.PrefetchScalarGridSpec(
            num_scalar_prefetch=1,
            grid=(nc,),
            in_specs=[rows, rows, whole(wq), whole(wkv)],
            out_specs=[piece, piece],
            scratch_shapes=[pltpu.VMEM((block, width), f32)],
        ),
        out_shape=[
            jax.ShapeDtypeStruct((nc, half, width), f32),
            jax.ShapeDtypeStruct((nc, half, width), bf16),
        ],
        compiler_params=grid_params(),
        cost_estimate=cost(2 * length * deep * width, 4 * length * deep + 4 * width * deep),
    )(ids, gq, gkv, wq, wkv)


def grad_ups_kernel(qn, kvn, gq, gkv, target):
    qrank = qn.shape[1]
    both = dot(qn[...], gq[...], TN)
    straight, turned = both[:, :LANES], both[:, LANES:]
    lane = lax.broadcasted_iota(jnp.int32, straight.shape, 1)
    half = ROPE // 2
    low = (lane >= NOPE) & (lane < NOPE + half)
    high = (lane >= NOPE + half) & (lane < NOPE + ROPE)
    straight = straight + jnp.where(low, pltpu.roll(turned, LANES - half, 1), 0.0)
    straight = straight - jnp.where(high, pltpu.roll(turned, half, 1), 0.0)
    target[:qrank, :] = straight.astype(bf16)
    both = dot(kvn[:, :KVRANK], gkv[...], TN)
    lane = lax.broadcasted_iota(jnp.int32, (KVRANK, LANES), 1)
    values = pltpu.roll(both[:, LANES:], NOPE, 1)
    target[qrank:, :] = jnp.where(lane < NOPE, both[:, :LANES], values).astype(bf16)


def grad_ups(qn, kvn, gq, gkv):
    length, qrank = qn.shape
    heads = gq.shape[1] // (2 * LANES)
    whole = lambda a: pl.BlockSpec(a.shape, lambda h: (0, 0))
    column = pl.BlockSpec((length, 2 * LANES), lambda h: (0, h))
    return pl.pallas_call(
        grad_ups_kernel,
        grid=(heads,),
        in_specs=[whole(qn), whole(kvn), column, column],
        out_specs=pl.BlockSpec((qrank + KVRANK, LANES), lambda h: (0, h)),
        out_shape=jax.ShapeDtypeStruct((qrank + KVRANK, heads * LANES), bf16),
        compiler_params=grid_params(),
        cost_estimate=cost(
            4 * length * (qrank + KVRANK) * heads * LANES, 2 * length * (qrank + heads * 4 * LANES)
        ),
    )(qn, kvn, gq, gkv)


def finish_ups_kernel(heads, pieces, ids, source, q_ref, kv_ref):
    qrank = q_ref.shape[0]
    wide = NOPE + ROPE
    for j in range(pieces):
        value = source[ids[2] ^ j]
        for h in range(heads):
            start = (j * heads + h) * wide
            q_ref[:, start : start + wide] = value[:qrank, h * LANES : h * LANES + wide].astype(f32)
        start = j * heads * LANES
        kv_ref[:, start : start + heads * LANES] = value[qrank:, :].astype(f32)


def grad_enter_kernel(pieces, ids, *refs):
    q_ref, kv_ref, gain_query, gain_latent, cosine, sine, turned, lat_ref, gain_q, gain_kv = refs[
        pieces:
    ]
    qrank = q_ref.shape[1]
    total = total_of(refs[:pieces])
    q_latent, c_latent = q_ref[...], kv_ref[:, :KVRANK]
    grad_q, grad_c, grad_rope = total[:, :qrank], total[:, qrank : qrank + KVRANK], total[:, qrank + KVRANK : qrank + KVRANK + ROPE]
    gain_q[...] = jnp.sum(grad_q * rms_scale(q_latent), axis=0, keepdims=True)
    c_round = rms_scale(c_latent).astype(bf16).astype(f32)
    gain_kv[...] = jnp.sum(grad_c * c_round, axis=0, keepdims=True)
    lat_ref[:, :qrank] = rms_back(q_latent, grad_q * gain_query[...]).astype(bf16)
    lat_ref[:, qrank : qrank + KVRANK] = rms_back(c_latent, grad_c * gain_latent[...]).astype(bf16)
    other = jnp.dot(
        grad_rope * sine[...], turned[...], precision=lax.Precision.HIGHEST, preferred_element_type=f32
    )
    end = qrank + KVRANK + ROPE
    lat_ref[:, qrank + KVRANK : end] = (grad_rope * cosine[...] - other).astype(bf16)
    lat_ref[:, end:] = jnp.zeros((lat_ref.shape[0], lat_ref.shape[1] - end), bf16)


def grad_tokens_kernel(
    sizes, block, ids, lat, w_qa, w_kva, tok, gain_in, grad_ref, target, gain_ref, inner
):
    nt, nz, nc = sizes
    half = lat.shape[0]
    qrank = w_qa.shape[1]
    grad = dot(lat[:, :qrank], w_qa[...], NT) + dot(
        lat[:, qrank : qrank + KVRANK + ROPE], w_kva[...], NN
    )
    here = pl.ds(pl.multiple_of(ids[0] * half, half), half)
    hidden = tok[here, :].astype(f32)
    gain_ref[...] = jnp.sum(grad * rms_scale(hidden), axis=0, keepdims=True)
    move_blocks(grad_ref, inner, nc, nz, block)
    target[...] = (inner[...] + rms_back(hidden, grad * gain_in[...])).astype(bf16)


def grad_down_kernel(share, ids, own, oth, gown, goth, target):
    nz, block, wide = target.shape
    flat = lambda ref: ref[...].reshape(-1, ref.shape[2])
    columns = pl.ds(pl.multiple_of(ids[0] * share, share), wide)
    right = lambda ref: ref[:, :, columns].reshape(-1, wide)
    total = (dot(flat(own), right(gown), TN) + dot(flat(oth), right(goth), TN)).astype(bf16)
    for i in range(nz):
        target[ids[1] ^ i] = total[i * block : (i + 1) * block, :]


def finish_down_kernel(share, ids, own, oth, q_ref, kv_ref):
    first = jnp.where(ids[0] == 0, own[...], oth[...]).astype(f32)
    second = jnp.where(ids[0] == 0, oth[...], own[...]).astype(f32)
    rest = q_ref.shape[1] - share
    q_ref[:, :share] = first[:, :share]
    q_ref[:, share:] = second[:, :rest]
    kv_ref[...] = second[:, rest : rest + kv_ref.shape[1]]


def body(
    sizes,
    tokens,
    segments,
    gain_attn,
    w_qa,
    gain_q,
    w_kva,
    gain_kv,
    w_qb,
    w_kvb,
    w_o,
    gain_mlp,
    w_gate,
    w_up,
    w_down,
    cotangent,
):
    nt, nz, nc = sizes
    t, z, c = lax.axis_index("tensor"), lax.axis_index("dp"), lax.axis_index("ctx")
    ids = jnp.stack([t, z, c]).astype(jnp.int32)
    rows, width = tokens.shape[1:]
    half = rows // nt
    block = w_o.shape[0]
    length = nc * rows
    heads = w_qb.shape[1] // (NOPE + ROPE) // nc
    ff = w_gate.shape[1] // nz
    qrank, kvrank = w_qa.shape[1], w_kva.shape[1]
    w_kva = w_kva.T
    lat_width = -(-(qrank + kvrank) // LANES) * LANES
    line = nz == 4

    def turn_gain(value):
        return jnp.swapaxes(value.reshape(nz, nc, block), 0, 1).reshape(1, width)

    def swap(value):
        return exchange(value, "tensor", 1, nt)

    def along_ctx(value):
        if nc != 4:
            return [value] + [exchange(value, "ctx", k, nc) for k in range(1, nc)]
        cut = value.shape[0] // 2
        first, second = exchange(value, "ctx", 1, nc), exchange(value, "ctx", 2, nc)
        upper = exchange(second[:cut], "ctx", 1, nc)
        lower = exchange(first[cut:], "ctx", 2, nc)
        return [value, first, second, jnp.concatenate([upper, lower])]

    def back_ctx(parts):
        if nc != 4:
            return across(parts, "ctx", nc)
        cut = parts[0].shape[0] // 2
        upper = exchange(parts[3][:cut], "ctx", 1, nc).astype(f32)
        lower = exchange(parts[3][cut:], "ctx", 2, nc).astype(f32)
        first, second = parts[1].astype(f32), parts[2].astype(f32)
        first = jnp.concatenate([first[:cut], first[cut:] + lower]).astype(bf16)
        second = jnp.concatenate([second[:cut] + upper, second[cut:]]).astype(bf16)
        return [parts[0], exchange(first, "ctx", 1, nc), exchange(second, "ctx", 2, nc)]

    def gather_dp(value):
        if not line:
            return [value] + [exchange(value, "dp", k, nz) for k in range(1, nz)]
        first, second = exchange(value, "dp", 1, nz), exchange(value, "dp", 2, nz)
        near = lax.ppermute(value, "dp", [(1, 2), (2, 1)])
        far = lax.ppermute(second, "dp", [(1, 0), (2, 3)])
        return [value, first, second, jnp.where((z == 0) | (z == 3), far, near)]

    def scatter_dp(parts):
        if not line:
            return [parts[0]] + [exchange(parts[k], "dp", k, nz) for k in range(1, nz)]
        far = lax.ppermute(parts[3], "dp", [(0, 1), (3, 2)])
        first = exchange(parts[1], "dp", 1, nz)
        near = lax.ppermute(parts[3], "dp", [(1, 2), (2, 1)])
        second = (parts[2].astype(f32) + far.astype(f32)).astype(bf16)
        return [parts[0], first, exchange(second, "dp", 2, nz), near]

    def split_columns(values, axis, at, pieces):
        deep, wide = values[0].shape[0], values[0].shape[1] // pieces
        if pieces > 4:
            parts = jnp.stack(values).reshape(len(values), deep, pieces, wide)
            parts = jnp.moveaxis(parts, 2, 0)
            return [pick(parts, lax.axis_index(axis) ^ k) for k in range(pieces)]
        outs = [((len(values), deep, wide), values[0].dtype)] * pieces
        return plain(functools.partial(split_kernel, at, pieces, len(values)), ids, values, outs)

    def join_columns(parts, axis, at):
        pieces, (count, deep, wide) = len(parts), parts[0].shape
        if pieces > 4:
            stacked = jnp.stack(parts)
            index = lax.axis_index(axis)
            parts = [pick(stacked, index ^ j) for j in range(pieces)]
            return list(jnp.concatenate(parts, axis=2).astype(f32))
        outs = [((deep, pieces * wide), f32)] * count
        return plain(functools.partial(join_kernel, at, pieces), ids, parts, outs)

    def stack_blocks(parts, at):
        count = parts[0].shape[0]
        outs = [((count, len(parts)) + parts[0].shape[1:], parts[0].dtype)]
        return plain(functools.partial(stack_kernel, at, len(parts)), ids, parts, outs)[0]

    def across(parts, axis, size):
        return [parts[0]] + [exchange(parts[k], axis, k, size) for k in range(1, size)]

    def join_rows(own):
        outs = [((rows, width), bf16)]
        return plain(rows_kernel, ids, [own, swap(own)], outs)[0][None]

    def weight_parts(*values):
        return across(split_columns(values, "dp", 1, nz), "dp", nz)

    def gather_weights(parts):
        parts = stack_blocks(parts, 1).reshape(-1, ff)
        return lax.all_gather(parts, "ctx", axis=0, tiled=True)

    def scatter_weights(value):
        return lax.psum_scatter(value, "ctx", scatter_dimension=0, tiled=True)

    def weight_rows(value):
        parts = value.reshape(-1, nz, block, ff)
        parts = [lax.dynamic_index_in_dim(parts, z ^ k, axis=1, keepdims=False) for k in range(nz)]
        return join_columns(across(parts, "dp", nz), "dp", 1)

    def reduce_ctx(keep, give):
        parts = (keep + swap(give).astype(f32)).astype(bf16)
        return back_ctx([parts[k] for k in range(nc)])

    segment_all = segments[0]
    doc_start = jnp.sum((segment_all[None, :] < segment_all[:, None]).astype(jnp.int32), axis=1)
    positions = (jnp.arange(length, dtype=jnp.int32) - doc_start).astype(f32)
    freqs = rope_base ** (-jnp.arange(0, ROPE, 2).astype(f32) / ROPE)
    angles = positions[:, None] * freqs[None, :]
    angles = jnp.concatenate([angles, angles], axis=1)
    cosine, sine = jnp.cos(angles), jnp.sin(angles)
    fill = lambda width, value: jnp.full((length, width), value, f32)
    tail = LANES - NOPE - ROPE
    cos_table = jnp.concatenate([fill(NOPE, 1.0), cosine, fill(tail, 0.0)], axis=1)
    sin_table = jnp.concatenate([fill(NOPE, 0.0), sine, fill(tail, 0.0)], axis=1)
    same = (segment_all[:, None] == jnp.arange(3, dtype=jnp.int32)[None, :]).astype(f32)
    query_table = jnp.concatenate(
        [fill(NOPE + ROPE + 3, 0.0), same * masked_score, fill(tail - 6, 0.0)], axis=1
    )
    key_table = jnp.concatenate(
        [fill(NOPE + ROPE, 0.0), fill(3, 1.0), 1.0 - same, fill(tail - 6, 0.0)], axis=1
    )
    first_row = c * rows + t * half
    own_cos = lax.dynamic_slice_in_dim(cosine, first_row, half)
    own_sin = lax.dynamic_slice_in_dim(sine, first_row, half)
    turned = jnp.asarray(turn_matrix(), f32)

    gain_in = gain_attn.astype(f32)[None]
    gain_query = gain_q.astype(f32)[None]
    gain_latent = gain_kv.astype(f32)[None]
    gain_middle = turn_gain(gain_mlp.astype(f32))

    spread_q = jnp.asarray(spread_queries(heads), bf16)
    spread_k = jnp.asarray(spread_keys(heads), bf16)
    own_qb = lax.dynamic_slice_in_dim(w_qb, c * heads * (NOPE + ROPE), heads * (NOPE + ROPE), axis=1)
    own_kvb = lax.dynamic_slice_in_dim(w_kvb, c * heads * (NOPE + VDIM), heads * (NOPE + VDIM), axis=1)
    wide_qb = dot(own_qb, spread_q, NN).astype(bf16)
    wide_kvb = jnp.concatenate(
        [
            dot(own_kvb, spread_k, NN).astype(bf16),
            jnp.asarray(spread_rope(heads), bf16),
            jnp.zeros((lat_width - qrank - kvrank, heads * 2 * LANES), bf16),
        ],
        axis=0,
    )

    half_of = lambda w, d: ((half, w), d)
    out_parts = across(split_columns([w_o], "ctx", 2, nc), "ctx", nc)
    down_parts = weight_parts(w_down)
    outs = plain(
        functools.partial(enter_kernel, sizes, block),
        ids,
        [
            tokens[0],
            cotangent[0],
            gain_in,
            gain_query,
            gain_latent,
            w_qa,
            w_kva,
            own_cos,
            own_sin,
            turned,
        ],
        [
            half_of(width, bf16),
            half_of(lat_width, bf16),
            half_of(qrank, f32),
            half_of(kvrank, f32),
            half_of(width, bf16),
            half_of(width, bf16),
            half_of(width, bf16),
        ]
        + [half_of(nz * block, bf16)] * nc,
        [pltpu.VMEM((half, width), bf16)] * 2,
        flops=2 * half * width * (qrank + kvrank),
    )
    _, latents, q_latent, kv_latent, own_tokens, own_cotangent, grad_mlp = outs[:7]
    normed_parts = outs[7:]
    lat_parts = along_ctx(latents)
    tables = (cos_table, sin_table, query_table, key_table)

    out_parts[0] = after(out_parts[0], latents)
    own_out = stack_blocks(out_parts, 2)[0]
    down_parts[0] = after(down_parts[0], own_out, wide_qb, wide_kvb, *tables)
    down = gather_weights(down_parts)
    out_pieces = gather_dp(after(own_out, down_parts[1], down_parts[2], down_parts[3]))
    lat_parts[0] = after(lat_parts[0], out_pieces[1])
    lat_own = jnp.stack(lat_parts)
    lat_oth = swap(lat_own)
    pair_parts = weight_parts(after(w_gate, out_pieces[2]), w_up)
    o_own, o_oth, q_rot, keys, values, qn, kvn = attend(
        nt, ids, lat_own, lat_oth, after(wide_qb, out_pieces[2]), wide_kvb, *tables
    )
    out_pieces[0] = after(out_pieces[0], o_own)
    full_out = plain(
        functools.partial(spread_kernel, heads, nz),
        ids,
        out_pieces,
        [((nc, nz, block, heads * LANES), bf16)],
    )[0].reshape(width, heads * LANES)
    keep, give = project_out(o_own, o_oth, full_out)
    pair_parts[0] = after(pair_parts[0], keep)
    pair = gather_weights(pair_parts)
    gm = gather_dp(after(grad_mlp, *pair_parts[1:]))
    attn = reduce_ctx(keep, give)
    resid, normed_mid = plain(
        functools.partial(middle_kernel, len(attn)),
        ids,
        attn + [own_tokens, gain_middle],
        [half_of(width, f32), half_of(width, bf16)],
    )
    nm = gather_dp(after(normed_mid, gm[1]))
    groups = [range(0, nz // 2), range(nz // 2, nz)]
    nm_all, gm_all, hidden, grad_gate, grad_up, grad_parts, mlp_parts = [], [], [], [], [], [], []
    for group in groups:
        nm_own = jnp.concatenate([nm[k] for k in group])
        gm_own = jnp.concatenate([gm[k] for k in group])
        if hidden:
            nm_own = after(nm_own, hidden[0])
        nm_oth, gm_oth = swap(nm_own), swap(gm_own)
        nm_all += [nm_own, nm_oth]
        gm_all += [gm_own, gm_oth]
        hid, gg, gu, gn_own, gn_oth, ml_own, ml_oth = feed_forward(
            nc, nm_own, nm_oth, gm_own, gm_oth, pair, down
        )
        hidden.append(hid)
        grad_gate.append(gg)
        grad_up.append(gu)
        for parts, own, oth in ((grad_parts, gn_own, gn_oth), (mlp_parts, ml_own, ml_oth)):
            total = (own.astype(f32) + swap(oth).astype(f32)).astype(bf16)
            parts += [total[i * half : (i + 1) * half] for i in range(len(group))]
    grad_normed = scatter_dp(grad_parts)
    gm_all[0] = after(gm_all[0], grad_normed[1])
    down_product = products(gm_all, [hidden], nc)
    down_product = scatter_weights(down_product)
    nm_all[0] = after(nm_all[0], grad_normed[3])
    pair_product = products(nm_all, [grad_gate, grad_up], nc)
    grad_normed[0] = after(grad_normed[0], pair_product)

    grad_resid, grad_attn, grad_gain_mlp = plain(
        functools.partial(back_middle_kernel, nz),
        ids,
        grad_normed + [resid, own_cotangent, gain_middle],
        [half_of(width, f32), half_of(width, bf16), ((1, width), f32)],
    )
    ga_parts = along_ctx(grad_attn)
    mlp_parts = scatter_dp([after(part, grad_attn) for part in mlp_parts])
    ga_own = jnp.stack(ga_parts)
    ga_oth = swap(ga_own)
    pair_product = scatter_weights(after(pair_product, ga_own))
    g_own, g_oth = project_heads(ga_own, ga_oth, full_out)
    grad_q, grad_kv = attend_back(
        nt, ids, q_rot, keys, values, o_own, o_oth, g_own, g_oth, cos_table, sin_table
    )
    mlp_parts[0] = after(mlp_parts[0], grad_q)
    layer_out = plain(
        functools.partial(leave_kernel, sizes, block, nz),
        ids,
        mlp_parts + [resid],
        [half_of(width, bf16)],
        [pltpu.VMEM((half, width), f32)],
    )[0]
    (grad_w_down,) = weight_rows(after(down_product, *mlp_parts))
    grad_lat = reduce_ctx(*grad_latent(sizes, ids, grad_q, grad_kv, wide_qb, wide_kvb))

    ups = grad_ups(qn, after(kvn, grad_lat[0]), grad_q, grad_kv)
    deep = ups.shape[0] // nz
    ups = ups.reshape(nz, deep, heads * LANES)
    ups = scatter_dp([pick(ups, z ^ k) for k in range(nz)])
    out_product = grad_out_weight(
        sizes, block, ids, ga_own, after(ga_oth, grad_lat[0], ups[0]), o_own, o_oth
    )
    grad_lat[0] = after(grad_lat[0], out_product)
    grad_lat, grad_gain_q, grad_gain_kv = plain(
        functools.partial(grad_enter_kernel, len(grad_lat)),
        ids,
        grad_lat + [q_latent, kv_latent, gain_query, gain_latent, own_cos, own_sin, turned],
        [half_of(lat_width, bf16), ((1, qrank), f32), ((1, KVRANK), f32)],
    )
    gl_parts = along_ctx(grad_lat)
    grad_tokens, grad_gain_attn = plain(
        functools.partial(grad_tokens_kernel, sizes, block),
        ids,
        [grad_lat, w_qa, w_kva, tokens[0], gain_in, grad_resid],
        [half_of(width, bf16), ((1, width), f32)],
        [pltpu.VMEM((half, width), f32)],
        flops=2 * half * width * (qrank + kvrank),
    )
    ups[0] = after(ups[0], grad_lat)
    own = sum(p.astype(f32) for p in ups).astype(bf16)
    ups = gather_dp(own)
    out_parts = scatter_dp([out_product[k] for k in range(nz)])
    gl_parts[0] = after(gl_parts[0], grad_tokens)
    gl_own = jnp.stack(gl_parts)
    gl_oth = swap(gl_own)

    xin_own = jnp.stack(across(normed_parts, "ctx", nc))
    xin_oth = swap(xin_own)
    share = lat_width // nt // LANES * LANES
    wide = lat_width - share
    parts = plain(
        functools.partial(grad_down_kernel, share),
        ids,
        [xin_own, xin_oth, gl_own, gl_oth],
        [((nz, block, wide), bf16)],
        flops=2 * length * nz * block * wide,
    )[0]
    ups[0] = after(ups[0], parts)
    ups = stack_blocks([piece[None] for piece in ups], 1).reshape(nz * deep, heads * LANES)
    ups = along_ctx(ups)
    out_parts[0] = after(out_parts[0], parts)
    own = sum(p.astype(f32) for p in out_parts).astype(bf16)
    out_parts = across([pick(own, c ^ k)[None] for k in range(nc)], "ctx", nc)
    own = scatter_dp([parts[k] for k in range(nz)])
    grad_w_gate, grad_w_up = weight_rows(after(pair_product, own[-1]))
    own = sum(p.astype(f32) for p in own).astype(bf16)
    grad_w_qa, grad_w_kva = plain(
        functools.partial(finish_down_kernel, share),
        ids,
        [own, swap(own)],
        [((block, qrank), f32), ((block, kvrank), f32)],
    )
    (grad_w_o,) = join_columns(out_parts, "ctx", 2)
    grad_w_qb, grad_w_kvb = plain(
        functools.partial(finish_ups_kernel, heads, nc),
        ids,
        [jnp.stack(ups)],
        [((qrank, nc * heads * (NOPE + ROPE)), f32), ((KVRANK, nc * heads * LANES), f32)],
    )
    layer_out = join_rows(layer_out)
    grad_tokens = join_rows(grad_tokens)

    turned_gain = jnp.swapaxes(grad_gain_mlp.reshape(nc, nz, block), 0, 1).reshape(1, width)
    gains = jnp.concatenate([grad_gain_attn, grad_gain_q, grad_gain_kv, turned_gain], axis=1)
    gains = gains.reshape(-1, LANES)
    for axis, size in (("tensor", nt), ("ctx", nc), ("dp", nz)):
        step = 1
        while step < size:
            gains = gains + exchange(gains, axis, step, size)
            step *= 2
    gains = gains.reshape(-1)
    ends = np.cumsum([width, qrank, KVRANK])
    grad_gain_attn, grad_gain_q, grad_gain_kv, grad_gain_mlp = jnp.split(gains, ends)
    return (
        layer_out,
        grad_tokens,
        grad_gain_attn,
        grad_w_qa,
        grad_gain_q,
        grad_w_kva,
        grad_gain_kv,
        grad_w_qb,
        grad_w_kvb,
        grad_w_o,
        grad_gain_mlp,
        grad_w_gate,
        grad_w_up,
        grad_w_down,
    )


def solution(mesh):
    placed = (
        P("dp", "ctx", None),
        P("dp", None),
        P(),
        P(),
        P(),
        P(),
        P(),
        P(None, "tensor"),
        P(None, "tensor"),
        P(("dp", "ctx"), "tensor"),
        P(),
        P(("dp", "ctx"), "tensor"),
        P(("dp", "ctx"), "tensor"),
        P(("dp", "ctx"), "tensor"),
        P("dp", "ctx", None),
    )
    sizes = tuple(mesh.shape[name] for name in ("tensor", "dp", "ctx"))
    return jax.shard_map(
        functools.partial(body, sizes),
        mesh=mesh,
        in_specs=placed,
        out_specs=(
            P("dp", "ctx", None),
            P("dp", "ctx", None),
            P(),
            P(("dp", "ctx"), None),
            P(),
            P(("dp", "ctx"), None),
            P(),
            P(None, "tensor"),
            P(None, "tensor"),
            P(("dp", "ctx"), "tensor"),
            P(),
            P(("dp", "ctx"), "tensor"),
            P(("dp", "ctx"), "tensor"),
            P(("dp", "ctx"), "tensor"),
        ),
        check_vma=False,
    )
```

```python
import functools
import math

import jax
import jax.numpy as jnp
import numpy as np
from jax import lax
from jax.experimental import pallas as pl
from jax.experimental.pallas import tpu as pltpu
from jax.sharding import PartitionSpec as P

NOPE = 64
ROPE = 32
VDIM = 64
KVRANK = 256
LANES = 128
QUERY_BLOCK = 256

eps_norm = 1e-05
res_scale = 1.4 / math.sqrt(62.0)
rope_base = 10000.0
masked_score = -1e30
score_scale = 1.0 / math.sqrt(NOPE + ROPE)
exponent = score_scale * math.log2(math.e)

f32 = jnp.float32
bf16 = jnp.bfloat16


def rms_scale(values):
    return values * lax.rsqrt(jnp.mean(values * values, axis=-1, keepdims=True) + eps_norm)


def dot(left, right, contract):
    return lax.dot_general(left, right, (contract, ((), ())), preferred_element_type=f32)


NN = ((1,), (0,))
NT = ((1,), (1,))
TN = ((0,), (0,))


def exchange(value, axis, step, size):
    return lax.ppermute(value, axis, [(i, i ^ step) for i in range(size)])


def after(value, *done):
    return lax.optimization_barrier((value,) + done)[0]


def pick(stacked, index):
    return lax.dynamic_index_in_dim(stacked, index, axis=0, keepdims=False)


def spread_queries(heads):
    out = np.zeros((heads, NOPE + ROPE, heads, 2, LANES), np.float32)
    half = ROPE // 2
    for h in range(heads):
        for j in range(NOPE + ROPE):
            out[h, j, h, 0, j] = 1.0
        for j in range(half):
            out[h, NOPE + half + j, h, 1, NOPE + j] = -1.0
            out[h, NOPE + j, h, 1, NOPE + half + j] = 1.0
    return out.reshape(heads * (NOPE + ROPE), heads * 2 * LANES)


def spread_keys(heads):
    out = np.zeros((heads, NOPE + VDIM, heads, 2, LANES), np.float32)
    for h in range(heads):
        for j in range(NOPE):
            out[h, j, h, 0, j] = 1.0
        for j in range(VDIM):
            out[h, NOPE + j, h, 1, j] = 1.0
    return out.reshape(heads * (NOPE + VDIM), heads * 2 * LANES)


def spread_rope(heads):
    out = np.zeros((ROPE, heads, 2, LANES), np.float32)
    for j in range(ROPE):
        out[j, :, 0, NOPE + j] = 1.0
    return out.reshape(ROPE, heads * 2 * LANES)


def spread_values(heads):
    out = np.zeros((heads, VDIM, heads, LANES), np.float32)
    for h in range(heads):
        for j in range(VDIM):
            out[h, j, h, j] = 1.0
    return out.reshape(heads * VDIM, heads * LANES)


def split_low(value):
    first = value.astype(bf16).astype(f32)
    second = (value - first).astype(bf16).astype(f32)
    third = (value - first - second).astype(bf16).astype(f32)
    return first, second, third


def rms_back(values, grad):
    inverse = lax.rsqrt(jnp.mean(values * values, axis=-1, keepdims=True) + eps_norm)
    scaled = values * inverse
    return (grad - scaled * jnp.mean(grad * scaled, axis=-1, keepdims=True)) * inverse


def turn_matrix():
    half = ROPE // 2
    out = np.zeros((ROPE, ROPE), np.float32)
    for j in range(half):
        out[half + j, j] = -1.0
        out[j, half + j] = 1.0
    return out


def frequencies(lanes, start):
    half = ROPE // 2
    out = np.zeros((1, lanes), np.float32)
    freqs = rope_base ** (-np.arange(0, ROPE, 2).astype(np.float32) / ROPE)
    out[0, start : start + half] = freqs
    out[0, start + half : start + ROPE] = freqs
    return out


def documents(segments, index):
    first = jnp.sum((segments < 1).astype(jnp.int32))
    second = jnp.sum((segments < 2).astype(jnp.int32))
    number = (index >= first).astype(jnp.int32) + (index >= second).astype(jnp.int32)
    start = jnp.where(index >= second, second, jnp.where(index >= first, first, 0))
    return number, start


def total_of(refs):
    total = refs[0][...].astype(f32)
    for ref in refs[1:]:
        total = total + ref[...].astype(f32)
    return total


def move_blocks(source, target, outer, inner, block, cast=None):
    for i in range(outer):
        for j in range(inner):
            value = source[:, (i * inner + j) * block : (i * inner + j + 1) * block]
            target[:, (j * outer + i) * block : (j * outer + i + 1) * block] = (
                value if cast is None else cast(value)
            )


SCALARS = pl.BlockSpec(memory_space=pltpu.SMEM)
LOCAL = pl.BlockSpec(memory_space=pltpu.VMEM)


def params(megabytes=48):
    return pltpu.CompilerParams(vmem_limit_bytes=megabytes * 1024 * 1024)


def grid_params(megabytes=48):
    return pltpu.CompilerParams(
        dimension_semantics=("arbitrary",), vmem_limit_bytes=megabytes * 1024 * 1024
    )


def cost(flops=0, moved=0, special=0):
    return pl.CostEstimate(
        flops=flops // 10, bytes_accessed=moved // 10, transcendentals=special // 10
    )


def plain(kernel, ids, operands, outs, scratch=(), flops=0, megabytes=48):
    moved = sum(a.size * a.dtype.itemsize for a in operands)
    moved += sum(math.prod(s) * jnp.dtype(d).itemsize for s, d in outs)
    return pl.pallas_call(
        kernel,
        in_specs=[SCALARS] + [LOCAL] * len(operands),
        out_specs=[LOCAL] * len(outs),
        out_shape=[jax.ShapeDtypeStruct(s, d) for s, d in outs],
        scratch_shapes=list(scratch),
        compiler_params=params(megabytes),
        cost_estimate=cost(flops, moved),
    )(ids, *operands)


def enter_kernel(
    sizes, block, ids, tok, cot, segments, freqs, gain_in, gain_query, gain_latent, w_qa, w_kva, turned,
    cos_ref, sin_ref, normed_ref, lat_ref, q_ref, kv_ref, x_ref, cot_ref, gm_ref, *rest
):
    nt, nz, nc = sizes
    pieces, (inner, plain_ref) = rest[:nc], rest[nc:]
    half = normed_ref.shape[0]
    qrank = w_qa.shape[1]
    index = (ids[2] * nt + ids[0]) * half + lax.broadcasted_iota(jnp.int32, (half, ROPE), 0)
    _, start = documents(segments[...], index)
    angles = (index - start).astype(f32) * freqs[...]
    cosine, sine = jnp.cos(angles), jnp.sin(angles)
    cos_ref[...] = cosine
    sin_ref[...] = sine
    here = pl.ds(pl.multiple_of(ids[0] * half, half), half)
    own = tok[here, :]
    hidden = own.astype(f32)
    normed = (rms_scale(hidden) * gain_in[...]).astype(bf16)
    normed_ref[...] = normed
    q_latent = dot(normed, w_qa[...], NN)
    kv_latent = dot(normed, w_kva[...], NT)
    q_ref[...] = q_latent
    kv_ref[...] = kv_latent
    lat_ref[:, :qrank] = (rms_scale(q_latent) * gain_query[...]).astype(bf16)
    c_round = rms_scale(kv_latent[:, :KVRANK]).astype(bf16).astype(f32)
    lat_ref[:, qrank : qrank + KVRANK] = (c_round * gain_latent[...]).astype(bf16)
    rope = kv_latent[:, KVRANK:]
    other = jnp.dot(rope, turned[...], precision=lax.Precision.HIGHEST, preferred_element_type=f32)
    end = qrank + KVRANK + ROPE
    lat_ref[:, qrank + KVRANK : end] = (rope * cosine + other * sine).astype(bf16)
    lat_ref[:, end:] = jnp.zeros((half, lat_ref.shape[1] - end), bf16)
    move_blocks(normed_ref, inner, nz, nc, block)
    span = nz * block
    for k in range(nc):
        start = pl.multiple_of((ids[2] ^ k) * span, span)
        pieces[k][...] = inner[:, pl.ds(start, span)]
    plain_ref[...] = own
    move_blocks(plain_ref, x_ref, nz, nc, block)
    plain_ref[...] = cot[here, :]
    move_blocks(plain_ref, cot_ref, nz, nc, block)
    gm_ref[...] = (res_scale * cot_ref[...].astype(f32)).astype(bf16)


def forward_kernel(
    nt, ids, own_ref, oth_ref, wq_ref, wkv_ref, segments, freqs,
    oown_ref, ooth_ref, q_ref, k_ref, v_ref, qn_ref, kvn_ref, cos_ref, sin_ref, qtab_ref, ktab_ref
):
    t, c = ids[0], ids[2]
    nc, half = own_ref.shape[0], own_ref.shape[1]
    length, qrank = qn_ref.shape
    block = nt * half

    @pl.when(pl.program_id(0) == 0)
    def _():
        for j in range(nc):
            for i in range(nt):
                rows = pl.ds((j * nt + i) * half, half)
                value = jnp.where(t == i, own_ref[c ^ j], oth_ref[c ^ j])
                qn_ref[rows, :] = value[:, :qrank]
                kvn_ref[rows, :] = value[:, qrank:]
        index = lax.broadcasted_iota(jnp.int32, (length, LANES), 0)
        lane = lax.broadcasted_iota(jnp.int32, (length, LANES), 1)
        number, start = documents(segments[...], index)
        angles = (index - start).astype(f32) * freqs[...]
        cos_ref[...] = jnp.where(lane < NOPE + ROPE, jnp.cos(angles), 0.0)
        sin_ref[...] = jnp.sin(angles)
        at = lane - (NOPE + ROPE + 3)
        same = at == number
        qtab_ref[...] = jnp.where(same, masked_score, 0.0)
        ones = (at >= -3) & (at < 3) & jnp.logical_not(same)
        ktab_ref[...] = jnp.where(ones, 1.0, 0.0)

    raw = jnp.dot(qn_ref[...], wq_ref[...], preferred_element_type=f32)
    query = raw[:, :LANES] * cos_ref[...] + raw[:, LANES:] * sin_ref[...] + qtab_ref[...]
    q_ref[...] = query.astype(bf16)
    both = jnp.dot(kvn_ref[...], wkv_ref[...], preferred_element_type=f32)
    k_ref[...] = (both[:, :LANES] + ktab_ref[...]).astype(bf16)
    lane = lax.broadcasted_iota(jnp.int32, (length, LANES), 1)
    ones = (lane >= VDIM) & (lane < VDIM + 3)
    v_ref[...] = jnp.where(ones, 1.0, both[:, LANES:]).astype(bf16)
    lane = lax.broadcasted_iota(jnp.int32, (block, LANES), 1)
    after = lax.broadcasted_iota(jnp.int32, (block, block), 1) > lax.broadcasted_iota(
        jnp.int32, (block, block), 0
    )
    for i in range(nc):
        here = pl.ds(i * block, block)
        query = q_ref[here, :]
        own = dot(query, k_ref[here, :], NT)
        own = jnp.where(after, masked_score, own)
        highest = jnp.max(own, axis=1, keepdims=True)
        if i:
            before = pl.ds(0, i * block)
            past = dot(query, k_ref[before, :], NT)
            highest = jnp.maximum(highest, jnp.max(past, axis=1, keepdims=True))
        weights = jnp.exp2((own - highest) * exponent).astype(bf16)
        mixed = dot(weights, v_ref[here, :], NN)
        if i:
            weights = jnp.exp2((past - highest) * exponent).astype(bf16)
            mixed = mixed + dot(weights, v_ref[before, :], NN)
        total = mixed[:, VDIM : VDIM + 1]
        out = jnp.where(lane < VDIM, mixed / total, 0.0).astype(bf16)
        for j in range(nt):
            part = out[j * half : (j + 1) * half]

            @pl.when(t == j)
            def _():
                oown_ref[c ^ i] = part

            @pl.when(t != j)
            def _():
                ooth_ref[c ^ i] = part

        first, second, third = split_low(-(highest + jnp.log2(total) / exponent))
        at = NOPE + ROPE
        kept = jnp.where(
            lane == at,
            first,
            jnp.where(lane == at + 1, second, jnp.where(lane == at + 2, third, query.astype(f32))),
        )
        q_ref[here, :] = kept.astype(bf16)


def backward_kernel(
    nt, ids, q_ref, k_ref, v_ref, oown_ref, ooth_ref, gown_ref, goth_ref, cos_ref, sin_ref,
    dq_ref, dkv_ref, grad_ref, dk_acc, dv_acc
):
    t, c = ids[0], ids[2]
    nc, half = gown_ref.shape[0], gown_ref.shape[1]
    length = q_ref.shape[0]
    block = nt * half
    lane = lax.broadcasted_iota(jnp.int32, (half, LANES), 1)
    for j in range(nc):
        for i in range(nt):
            grad = jnp.where(t == i, gown_ref[c ^ j], goth_ref[c ^ j]).astype(f32)
            out = jnp.where(t == i, oown_ref[c ^ j], ooth_ref[c ^ j]).astype(f32)
            first, second, third = split_low(-jnp.sum(grad * out, axis=1, keepdims=True))
            grad = jnp.where(
                lane == VDIM,
                first,
                jnp.where(lane == VDIM + 1, second, jnp.where(lane == VDIM + 2, third, grad)),
            )
            grad_ref[pl.ds((j * nt + i) * half, half), :] = grad.astype(bf16)
    after = lax.broadcasted_iota(jnp.int32, (block, block), 0) > lax.broadcasted_iota(
        jnp.int32, (block, block), 1
    )
    for i in reversed(range(nc)):
        here = pl.ds(i * block, block)
        query, grad = q_ref[here, :], grad_ref[here, :]

        def part(span, masked):
            keys = k_ref[span, :]
            scores = dot(keys, query, NT)
            if masked:
                scores = jnp.where(after, masked_score, scores)
            probs = jnp.exp2(scores * exponent)
            inward = dot(v_ref[span, :], grad, NT)
            low = (probs * inward).astype(bf16)
            dv = dot(probs.astype(bf16), grad, NN)
            dk = dot(low, query, NN)
            if i == nc - 1:
                dv_acc[span, :] = dv
                dk_acc[span, :] = dk
            else:
                dv_acc[span, :] += dv
                dk_acc[span, :] += dk
            return dot(low, keys, TN)

        dq = part(here, True)
        if i:
            dq = dq + part(pl.ds(0, i * block), False)
        dq = dq * score_scale
        dq_ref[here, :LANES] = (dq * cos_ref[here, :]).astype(bf16)
        dq_ref[here, LANES:] = (dq * sin_ref[here, :]).astype(bf16)
    lane = lax.broadcasted_iota(jnp.int32, (length, LANES), 1)
    dkv_ref[:, :LANES] = jnp.where(lane < NOPE + ROPE, dk_acc[...] * score_scale, 0.0).astype(bf16)
    dkv_ref[:, LANES:] = jnp.where(lane < VDIM, dv_acc[...], 0.0).astype(bf16)


def attend(nt, ids, own, oth, wq, wkv, segments):
    nc, half, _ = own.shape
    length = nc * nt * half
    qrank, kvrank = wq.shape[0], wkv.shape[0]
    heads = wq.shape[1] // (2 * LANES)
    whole = lambda a: pl.BlockSpec(a.shape, lambda h, ids: (0,) * a.ndim)
    column = lambda rows, width: pl.BlockSpec((rows, width), lambda h, ids: (0, h))
    split = pl.BlockSpec((nc, half, LANES), lambda h, ids: (0, 0, h))
    out = jax.ShapeDtypeStruct((length, heads * LANES), bf16)
    out_split = jax.ShapeDtypeStruct((nc, half, heads * LANES), bf16)
    kept = [
        jax.ShapeDtypeStruct((length, qrank), bf16),
        jax.ShapeDtypeStruct((length, kvrank), bf16),
        jax.ShapeDtypeStruct((length, LANES), f32),
        jax.ShapeDtypeStruct((length, LANES), f32),
    ]
    freqs = jnp.asarray(frequencies(LANES, NOPE))
    return pl.pallas_call(
        functools.partial(forward_kernel, nt),
        grid_spec=pltpu.PrefetchScalarGridSpec(
            num_scalar_prefetch=1,
            grid=(heads,),
            in_specs=[
                whole(own),
                whole(oth),
                column(qrank, 2 * LANES),
                column(kvrank, 2 * LANES),
                whole(segments),
                whole(freqs),
            ],
            out_specs=[split] * 2 + [column(length, LANES)] * 3 + [whole(a) for a in kept],
            scratch_shapes=[pltpu.VMEM((length, LANES), f32)] * 2,
        ),
        out_shape=[out_split] * 2 + [out] * 3 + kept,
        compiler_params=grid_params(),
        cost_estimate=cost(
            4 * heads * length * (length * LANES + qrank * 2 * LANES),
            16 * length * heads * LANES,
            heads * length * length // 2,
        ),
    )(ids, own, oth, wq, wkv, segments, freqs)


def attend_back(nt, ids, q, k, v, oown, ooth, gown, goth, cosine, sine):
    nc, half, _ = oown.shape
    length = q.shape[0]
    heads = q.shape[1] // LANES
    whole = lambda a: pl.BlockSpec(a.shape, lambda h, ids: (0, 0))
    column = lambda width: pl.BlockSpec((length, width), lambda h, ids: (0, h))
    split = pl.BlockSpec((nc, half, LANES), lambda h, ids: (0, 0, h))
    out = jax.ShapeDtypeStruct((length, heads * 2 * LANES), bf16)
    return pl.pallas_call(
        functools.partial(backward_kernel, nt),
        grid_spec=pltpu.PrefetchScalarGridSpec(
            num_scalar_prefetch=1,
            grid=(heads,),
            in_specs=[column(LANES)] * 3 + [split] * 4 + [whole(cosine), whole(sine)],
            out_specs=[column(2 * LANES)] * 2,
            scratch_shapes=[
                pltpu.VMEM((length, LANES), bf16),
                pltpu.VMEM((length, LANES), f32),
                pltpu.VMEM((length, LANES), f32),
            ],
        ),
        out_shape=[out] * 2,
        compiler_params=grid_params(),
        cost_estimate=cost(
            8 * heads * length * length * LANES,
            24 * length * heads * LANES,
            heads * length * length // 2,
        ),
    )(ids, q, k, v, oown, ooth, gown, goth, cosine, sine)


def split_kernel(axis, pieces, count, ids, *refs):
    width = refs[count].shape[2]
    for k in range(pieces):
        for j in range(pieces):

            @pl.when((ids[axis] ^ k) == j)
            def _():
                for i in range(count):
                    refs[count + k][i] = refs[i][:, j * width : (j + 1) * width]


def join_kernel(axis, pieces, ids, *refs):
    targets = refs[pieces:]
    width = refs[0].shape[2]
    for k in range(pieces):
        for j in range(pieces):

            @pl.when((ids[axis] ^ k) == j)
            def _():
                for i, target in enumerate(targets):
                    target[:, j * width : (j + 1) * width] = refs[k][i].astype(target.dtype)


def stack_kernel(axis, pieces, ids, *refs):
    for k in range(pieces):
        for i in range(refs[k].shape[0]):
            refs[pieces][i, ids[axis] ^ k] = refs[k][i]


def rows_kernel(ids, own, oth, target):
    half = own.shape[0]
    target[pl.ds(pl.multiple_of(ids[0] * half, half), half), :] = own[...]
    target[pl.ds(pl.multiple_of((1 - ids[0]) * half, half), half), :] = oth[...]


def spread_kernel(heads, pieces, ids, *refs):
    target = refs[pieces]
    target[...] = jnp.zeros_like(target)
    for k in range(pieces):
        for j in range(refs[k].shape[0]):
            for h in range(heads):
                target[j, ids[1] ^ k, :, h * LANES : h * LANES + VDIM] = refs[k][
                    j, :, h * VDIM : (h + 1) * VDIM
                ]


def out_kernel(own, oth, weight, keep, give):
    per, half, _ = own.shape
    both = jnp.concatenate([ref[i] for ref in (own, oth) for i in range(per)], axis=0)
    result = dot(both, weight[...], NT)
    for i in range(per):
        keep[i] = result[i * half : (i + 1) * half]
        give[i] = result[(per + i) * half : (per + i + 1) * half].astype(bf16)


def project_out(own, oth, weight):
    nc, half, deep = own.shape
    width = weight.shape[0]
    per = math.gcd(nc, 2)
    piece = lambda w: pl.BlockSpec((per, half, w), lambda k: (k, 0, 0))
    return pl.pallas_call(
        out_kernel,
        grid=(nc // per,),
        in_specs=[piece(deep)] * 2 + [pl.BlockSpec(weight.shape, lambda k: (0, 0))],
        out_specs=[piece(width)] * 2,
        out_shape=[
            jax.ShapeDtypeStruct((nc, half, width), f32),
            jax.ShapeDtypeStruct((nc, half, width), bf16),
        ],
        compiler_params=grid_params(),
        cost_estimate=cost(4 * nc * half * deep * width, 2 * weight.size + 16 * nc * half * width),
    )(own, oth, weight)


def heads_kernel(own, oth, weight, gown, goth):
    per, half, _ = own.shape
    both = jnp.concatenate([ref[i] for ref in (own, oth) for i in range(per)], axis=0)
    result = dot(both, weight[...], NN).astype(bf16)
    for i in range(per):
        gown[i] = result[i * half : (i + 1) * half]
        goth[i] = result[(per + i) * half : (per + i + 1) * half]


def project_heads(own, oth, weight):
    nc, half, width = own.shape
    deep = weight.shape[1]
    per = math.gcd(nc, 2)
    piece = lambda w: pl.BlockSpec((per, half, w), lambda k: (k, 0, 0))
    return pl.pallas_call(
        heads_kernel,
        grid=(nc // per,),
        in_specs=[piece(width)] * 2 + [pl.BlockSpec(weight.shape, lambda k: (0, 0))],
        out_specs=[piece(deep)] * 2,
        out_shape=[jax.ShapeDtypeStruct((nc, half, deep), bf16)] * 2,
        compiler_params=grid_params(),
        cost_estimate=cost(4 * nc * half * deep * width, 2 * weight.size + 8 * nc * half * width),
    )(own, oth, weight)


def middle_kernel(pieces, ids, *refs):
    tokens, gain, resid_ref, normed_ref = refs[pieces:]
    resid = tokens[...].astype(f32) + res_scale * total_of(refs[:pieces])
    resid_ref[...] = resid
    normed_ref[...] = (rms_scale(resid) * gain[...]).astype(bf16)


def leave_kernel(sizes, block, pieces, ids, *refs):
    resid, target, inner = refs[pieces:]
    nt, nz, nc = sizes
    inner[...] = resid[...] + res_scale * total_of(refs[:pieces])
    move_blocks(inner, target, nc, nz, block, lambda value: value.astype(bf16))


def mlp_kernel(
    nm_own, nm_oth, gm_own, gm_oth, pair_hbm, down_hbm,
    hid_ref, gg_ref, gu_ref, gn_own, gn_oth, ml_own, ml_oth, w_gate, w_up, w_down, sems
):
    step = pl.program_id(0)
    blocks = sems.shape[1]
    deep = w_down.shape[0] // blocks
    copies = [
        [
            pltpu.make_async_copy(
                source.at[pl.ds((j * count + at) * deep, deep), :],
                target.at[pl.ds(j * deep, deep), :],
                sems.at[i, j],
            )
            for j in range(blocks)
        ]
        for i, (source, count, at, target) in enumerate(
            ((pair_hbm, 2, 0, w_gate), (pair_hbm, 2, 1, w_up), (down_hbm, 1, 0, w_down))
        )
    ]

    def ready(i):
        @pl.when(step == 0)
        def _():
            for copy in copies[i]:
                copy.wait()

    @pl.when(step == 0)
    def _():
        for group in copies:
            for copy in group:
                copy.start()

    block = nm_own.shape[0]
    normed = jnp.concatenate([nm_own[...], nm_oth[...]], axis=0)
    ready(0)
    gate = dot(normed, w_gate[...], NN)
    ready(1)
    up_proj = dot(normed, w_up[...], NN)
    ready(2)
    grad_hidden = dot(jnp.concatenate([gm_own[...], gm_oth[...]], axis=0), w_down[...], NN)
    sigma = jax.nn.sigmoid(gate)
    silu_gate = gate * sigma
    hidden = (silu_gate * up_proj).astype(bf16)
    grad_gate = (grad_hidden * up_proj * sigma * (1.0 + gate * (1.0 - sigma))).astype(bf16)
    grad_up = (grad_hidden * silu_gate).astype(bf16)
    for target, value in ((hid_ref, hidden), (gg_ref, grad_gate), (gu_ref, grad_up)):
        target[0] = value[:block]
        target[1] = value[block:]
    mlp = dot(hidden, w_down[...], NT).astype(bf16)
    ml_own[...] = mlp[:block]
    ml_oth[...] = mlp[block:]
    grad_normed = (dot(grad_gate, w_gate[...], NT) + dot(grad_up, w_up[...], NT)).astype(bf16)
    gn_own[...] = grad_normed[:block]
    gn_oth[...] = grad_normed[block:]


def feed_forward(blocks, nm_own, nm_oth, gm_own, gm_oth, pair, down):
    rows, width = nm_own.shape
    ff = down.shape[1]
    block = min(rows, 256)
    part_of = pl.BlockSpec((block, width), lambda i: (i, 0))
    inner = pl.BlockSpec((2, block, ff), lambda i: (0, i, 0))
    anywhere = pl.BlockSpec(memory_space=pl.ANY)
    held = jax.ShapeDtypeStruct((2, rows, ff), bf16)
    part = jax.ShapeDtypeStruct((rows, width), bf16)
    made = pl.pallas_call(
        mlp_kernel,
        grid=(rows // block,),
        in_specs=[part_of] * 4 + [anywhere] * 2,
        out_specs=[inner] * 3 + [part_of] * 4,
        out_shape=[held] * 3 + [part] * 4,
        scratch_shapes=[pltpu.VMEM((width, ff), bf16)] * 3
        + [pltpu.SemaphoreType.DMA((3, blocks))],
        compiler_params=grid_params(60),
        cost_estimate=cost(
            24 * rows * width * ff, 6 * width * ff + 16 * rows * width, 2 * rows * ff
        ),
    )(nm_own, nm_oth, gm_own, gm_oth, pair, down)
    return [a.reshape(2 * rows, ff) for a in made[:3]] + list(made[3:])


def product_kernel(count, targets, *refs):
    left = refs[:count]
    per = count // 2
    for i in range(targets):
        right = refs[count + i * per : count + (i + 1) * per]
        total = None
        for j in range(count):
            rows = left[j].shape[0]
            value = right[j // 2][(j % 2) * rows : (j % 2 + 1) * rows, :]
            term = dot(left[j][...], value, TN)
            total = term if total is None else total + term
        span = total.shape[0]
        refs[-1][i * span : (i + 1) * span, :] = total.astype(bf16)


def products(lefts, rights, parts):
    rows, width = lefts[0].shape
    ff = rights[0][0].shape[1]
    span = width // parts
    count = len(rights)
    flat = [a for group in rights for a in group]
    return pl.pallas_call(
        functools.partial(product_kernel, len(lefts), count),
        grid=(parts,),
        in_specs=[pl.BlockSpec((rows, span), lambda i: (0, i))] * len(lefts)
        + [pl.BlockSpec(a.shape, lambda i: (0, 0)) for a in flat],
        out_specs=pl.BlockSpec((count * span, ff), lambda i: (i, 0)),
        out_shape=jax.ShapeDtypeStruct((parts * count * span, ff), bf16),
        compiler_params=grid_params(),
        cost_estimate=cost(
            2 * count * len(lefts) * rows * width * ff,
            2 * len(lefts) * rows * width + 2 * count * width * ff,
        ),
    )(*lefts, *flat)


def back_middle_kernel(pieces, ids, *refs):
    resid_ref, cot, gain, grad_ref, attn_ref, gain_ref = refs[pieces:]
    grad_normed = total_of(refs[:pieces])
    resid = resid_ref[...]
    gain_ref[...] = jnp.sum(grad_normed * rms_scale(resid), axis=0, keepdims=True)
    grad = cot[...].astype(f32) + rms_back(resid, grad_normed * gain[...])
    grad_ref[...] = grad
    attn_ref[...] = (res_scale * grad).astype(bf16)


def grad_out_kernel(heads, ids, own, oth, oown, ooth, target):
    nz, _, block, _ = target.shape
    flat = lambda ref: ref[...].reshape(-1, ref.shape[2])
    total = dot(flat(own), flat(oown), TN) + dot(flat(oth), flat(ooth), TN)
    total = total.astype(bf16)
    for i in range(nz):
        for h in range(heads):
            target[ids[1] ^ i, 0, :, h * VDIM : (h + 1) * VDIM] = total[
                i * block : (i + 1) * block, h * LANES : h * LANES + VDIM
            ]


def grad_out_weight(sizes, block, ids, own, oth, oown, ooth):
    nt, nz, nc = sizes
    _, half, width = own.shape
    deep = oown.shape[2]
    heads = deep // LANES
    left = pl.BlockSpec((nc, half, nz * block), lambda j, ids: (0, 0, j))
    right = pl.BlockSpec((nc, half, deep), lambda j, ids: (0, 0, 0))
    return pl.pallas_call(
        functools.partial(grad_out_kernel, heads),
        grid_spec=pltpu.PrefetchScalarGridSpec(
            num_scalar_prefetch=1,
            grid=(nc,),
            in_specs=[left, left, right, right],
            out_specs=pl.BlockSpec((nz, 1, block, heads * VDIM), lambda j, ids: (0, j, 0, 0)),
        ),
        out_shape=jax.ShapeDtypeStruct((nz, nc, block, heads * VDIM), bf16),
        compiler_params=grid_params(),
        cost_estimate=cost(4 * nc * half * width * deep, 4 * nc * half * (width + deep)),
    )(ids, own, oth, oown, ooth)


def grad_latent_kernel(ids, gq, gkv, wq, wkv, keep, give, inner):
    half = keep.shape[1]
    qrank = wq.shape[0]
    inner[:, :qrank] = dot(gq[...], wq[...], NT)
    inner[:, qrank:] = dot(gkv[...], wkv[...], NT)
    keep[0] = inner[pl.ds(pl.multiple_of(ids[0] * half, half), half), :]
    give[0] = inner[pl.ds(pl.multiple_of((1 - ids[0]) * half, half), half), :].astype(bf16)


def grad_latent(sizes, ids, gq, gkv, wq, wkv):
    nt, _, nc = sizes
    length, deep = gq.shape
    block = length // nc
    half = block // nt
    width = wq.shape[0] + wkv.shape[0]
    rows = pl.BlockSpec((block, deep), lambda k, ids: (ids[2] ^ k, 0))
    whole = lambda a: pl.BlockSpec(a.shape, lambda k, ids: (0, 0))
    piece = pl.BlockSpec((1, half, width), lambda k, ids: (k, 0, 0))
    return pl.pallas_call(
        grad_latent_kernel,
        grid_spec=pltpu.PrefetchScalarGridSpec(
            num_scalar_prefetch=1,
            grid=(nc,),
            in_specs=[rows, rows, whole(wq), whole(wkv)],
            out_specs=[piece, piece],
            scratch_shapes=[pltpu.VMEM((block, width), f32)],
        ),
        out_shape=[
            jax.ShapeDtypeStruct((nc, half, width), f32),
            jax.ShapeDtypeStruct((nc, half, width), bf16),
        ],
        compiler_params=grid_params(),
        cost_estimate=cost(2 * length * deep * width, 4 * length * deep + 4 * width * deep),
    )(ids, gq, gkv, wq, wkv)


def grad_ups_kernel(qn, kvn, gq, gkv, target):
    qrank = qn.shape[1]
    both = dot(qn[...], gq[...], TN)
    straight, turned = both[:, :LANES], both[:, LANES:]
    lane = lax.broadcasted_iota(jnp.int32, straight.shape, 1)
    half = ROPE // 2
    low = (lane >= NOPE) & (lane < NOPE + half)
    high = (lane >= NOPE + half) & (lane < NOPE + ROPE)
    straight = straight + jnp.where(low, pltpu.roll(turned, LANES - half, 1), 0.0)
    straight = straight - jnp.where(high, pltpu.roll(turned, half, 1), 0.0)
    target[:qrank, :] = straight.astype(bf16)
    both = dot(kvn[:, :KVRANK], gkv[...], TN)
    lane = lax.broadcasted_iota(jnp.int32, (KVRANK, LANES), 1)
    values = pltpu.roll(both[:, LANES:], NOPE, 1)
    target[qrank:, :] = jnp.where(lane < NOPE, both[:, :LANES], values).astype(bf16)


def grad_ups(qn, kvn, gq, gkv):
    length, qrank = qn.shape
    heads = gq.shape[1] // (2 * LANES)
    whole = lambda a: pl.BlockSpec(a.shape, lambda h: (0, 0))
    column = pl.BlockSpec((length, 2 * LANES), lambda h: (0, h))
    return pl.pallas_call(
        grad_ups_kernel,
        grid=(heads,),
        in_specs=[whole(qn), whole(kvn), column, column],
        out_specs=pl.BlockSpec((qrank + KVRANK, LANES), lambda h: (0, h)),
        out_shape=jax.ShapeDtypeStruct((qrank + KVRANK, heads * LANES), bf16),
        compiler_params=grid_params(),
        cost_estimate=cost(
            4 * length * (qrank + KVRANK) * heads * LANES, 2 * length * (qrank + heads * 4 * LANES)
        ),
    )(qn, kvn, gq, gkv)


def finish_ups_kernel(heads, pieces, ids, source, q_ref, kv_ref):
    qrank = q_ref.shape[0]
    wide = NOPE + ROPE
    for j in range(pieces):
        value = source[ids[2] ^ j]
        for h in range(heads):
            start = (j * heads + h) * wide
            q_ref[:, start : start + wide] = value[:qrank, h * LANES : h * LANES + wide].astype(f32)
        start = j * heads * LANES
        kv_ref[:, start : start + heads * LANES] = value[qrank:, :].astype(f32)


def grad_enter_kernel(pieces, ids, *refs):
    q_ref, kv_ref, gain_query, gain_latent, cosine, sine, turned, lat_ref, gain_q, gain_kv = refs[
        pieces:
    ]
    qrank = q_ref.shape[1]
    total = total_of(refs[:pieces])
    q_latent, c_latent = q_ref[...], kv_ref[:, :KVRANK]
    grad_q, grad_c, grad_rope = total[:, :qrank], total[:, qrank : qrank + KVRANK], total[:, qrank + KVRANK : qrank + KVRANK + ROPE]
    gain_q[...] = jnp.sum(grad_q * rms_scale(q_latent), axis=0, keepdims=True)
    c_round = rms_scale(c_latent).astype(bf16).astype(f32)
    gain_kv[...] = jnp.sum(grad_c * c_round, axis=0, keepdims=True)
    lat_ref[:, :qrank] = rms_back(q_latent, grad_q * gain_query[...]).astype(bf16)
    lat_ref[:, qrank : qrank + KVRANK] = rms_back(c_latent, grad_c * gain_latent[...]).astype(bf16)
    other = jnp.dot(
        grad_rope * sine[...], turned[...], precision=lax.Precision.HIGHEST, preferred_element_type=f32
    )
    end = qrank + KVRANK + ROPE
    lat_ref[:, qrank + KVRANK : end] = (grad_rope * cosine[...] - other).astype(bf16)
    lat_ref[:, end:] = jnp.zeros((lat_ref.shape[0], lat_ref.shape[1] - end), bf16)


def grad_tokens_kernel(
    sizes, block, ids, lat, w_qa, w_kva, tok, gain_in, grad_ref, target, gain_ref, inner
):
    nt, nz, nc = sizes
    half = lat.shape[0]
    qrank = w_qa.shape[1]
    grad = dot(lat[:, :qrank], w_qa[...], NT) + dot(
        lat[:, qrank : qrank + KVRANK + ROPE], w_kva[...], NN
    )
    here = pl.ds(pl.multiple_of(ids[0] * half, half), half)
    hidden = tok[here, :].astype(f32)
    gain_ref[...] = jnp.sum(grad * rms_scale(hidden), axis=0, keepdims=True)
    move_blocks(grad_ref, inner, nc, nz, block)
    target[...] = (inner[...] + rms_back(hidden, grad * gain_in[...])).astype(bf16)


def grad_down_kernel(share, ids, own, oth, gown, goth, target):
    nz, block, wide = target.shape
    flat = lambda ref: ref[...].reshape(-1, ref.shape[2])
    columns = pl.ds(pl.multiple_of(ids[0] * share, share), wide)
    right = lambda ref: ref[:, :, columns].reshape(-1, wide)
    total = (dot(flat(own), right(gown), TN) + dot(flat(oth), right(goth), TN)).astype(bf16)
    for i in range(nz):
        target[ids[1] ^ i] = total[i * block : (i + 1) * block, :]


def finish_down_kernel(share, ids, own, oth, q_ref, kv_ref):
    first = jnp.where(ids[0] == 0, own[...], oth[...]).astype(f32)
    second = jnp.where(ids[0] == 0, oth[...], own[...]).astype(f32)
    rest = q_ref.shape[1] - share
    q_ref[:, :share] = first[:, :share]
    q_ref[:, share:] = second[:, :rest]
    kv_ref[...] = second[:, rest : rest + kv_ref.shape[1]]


def body(
    sizes,
    tokens,
    segments,
    gain_attn,
    w_qa,
    gain_q,
    w_kva,
    gain_kv,
    w_qb,
    w_kvb,
    w_o,
    gain_mlp,
    w_gate,
    w_up,
    w_down,
    cotangent,
):
    nt, nz, nc = sizes
    t, z, c = lax.axis_index("tensor"), lax.axis_index("dp"), lax.axis_index("ctx")
    ids = jnp.stack([t, z, c]).astype(jnp.int32)
    rows, width = tokens.shape[1:]
    half = rows // nt
    block = w_o.shape[0]
    length = nc * rows
    heads = w_qb.shape[1] // (NOPE + ROPE) // nc
    ff = w_gate.shape[1] // nz
    qrank, kvrank = w_qa.shape[1], w_kva.shape[1]
    w_kva = w_kva.T
    lat_width = -(-(qrank + kvrank) // LANES) * LANES
    line = nz == 4

    def turn_gain(value):
        return jnp.swapaxes(value.reshape(nz, nc, block), 0, 1).reshape(1, width)

    def swap(value):
        return exchange(value, "tensor", 1, nt)

    def along_ctx(value):
        if nc != 4:
            return [value] + [exchange(value, "ctx", k, nc) for k in range(1, nc)]
        cut = value.shape[0] // 2
        first, second = exchange(value, "ctx", 1, nc), exchange(value, "ctx", 2, nc)
        upper = exchange(second[:cut], "ctx", 1, nc)
        lower = exchange(first[cut:], "ctx", 2, nc)
        return [value, first, second, jnp.concatenate([upper, lower])]

    def back_ctx(parts):
        if nc != 4:
            return across(parts, "ctx", nc)
        cut = parts[0].shape[0] // 2
        upper = exchange(parts[3][:cut], "ctx", 1, nc).astype(f32)
        lower = exchange(parts[3][cut:], "ctx", 2, nc).astype(f32)
        first, second = parts[1].astype(f32), parts[2].astype(f32)
        first = jnp.concatenate([first[:cut], first[cut:] + lower]).astype(bf16)
        second = jnp.concatenate([second[:cut] + upper, second[cut:]]).astype(bf16)
        return [parts[0], exchange(first, "ctx", 1, nc), exchange(second, "ctx", 2, nc)]

    def gather_dp(value):
        if not line:
            return [value] + [exchange(value, "dp", k, nz) for k in range(1, nz)]
        first, second = exchange(value, "dp", 1, nz), exchange(value, "dp", 2, nz)
        near = lax.ppermute(value, "dp", [(1, 2), (2, 1)])
        far = lax.ppermute(second, "dp", [(1, 0), (2, 3)])
        return [value, first, second, jnp.where((z == 0) | (z == 3), far, near)]

    def scatter_dp(parts):
        if not line:
            return [parts[0]] + [exchange(parts[k], "dp", k, nz) for k in range(1, nz)]
        far = lax.ppermute(parts[3], "dp", [(0, 1), (3, 2)])
        first = exchange(parts[1], "dp", 1, nz)
        near = lax.ppermute(parts[3], "dp", [(1, 2), (2, 1)])
        second = (parts[2].astype(f32) + far.astype(f32)).astype(bf16)
        return [parts[0], first, exchange(second, "dp", 2, nz), near]

    def split_columns(values, axis, at, pieces):
        deep, wide = values[0].shape[0], values[0].shape[1] // pieces
        if pieces > 4:
            parts = jnp.stack(values).reshape(len(values), deep, pieces, wide)
            parts = jnp.moveaxis(parts, 2, 0)
            return [pick(parts, lax.axis_index(axis) ^ k) for k in range(pieces)]
        outs = [((len(values), deep, wide), values[0].dtype)] * pieces
        return plain(functools.partial(split_kernel, at, pieces, len(values)), ids, values, outs)

    def join_columns(parts, axis, at):
        pieces, (count, deep, wide) = len(parts), parts[0].shape
        if pieces > 4:
            stacked = jnp.stack(parts)
            index = lax.axis_index(axis)
            parts = [pick(stacked, index ^ j) for j in range(pieces)]
            return list(jnp.concatenate(parts, axis=2).astype(f32))
        outs = [((deep, pieces * wide), f32)] * count
        return plain(functools.partial(join_kernel, at, pieces), ids, parts, outs)

    def stack_blocks(parts, at):
        count = parts[0].shape[0]
        outs = [((count, len(parts)) + parts[0].shape[1:], parts[0].dtype)]
        return plain(functools.partial(stack_kernel, at, len(parts)), ids, parts, outs)[0]

    def across(parts, axis, size):
        return [parts[0]] + [exchange(parts[k], axis, k, size) for k in range(1, size)]

    def join_rows(own):
        outs = [((rows, width), bf16)]
        return plain(rows_kernel, ids, [own, swap(own)], outs)[0][None]

    def weight_parts(*values):
        return across(split_columns(values, "dp", 1, nz), "dp", nz)

    def gather_weights(parts):
        parts = stack_blocks(parts, 1).reshape(-1, ff)
        return lax.all_gather(parts, "ctx", axis=0, tiled=True)

    def scatter_weights(value):
        return lax.psum_scatter(value, "ctx", scatter_dimension=0, tiled=True)

    def weight_rows(value):
        parts = value.reshape(-1, nz, block, ff)
        parts = [lax.dynamic_index_in_dim(parts, z ^ k, axis=1, keepdims=False) for k in range(nz)]
        return join_columns(across(parts, "dp", nz), "dp", 1)

    def reduce_ctx(keep, give):
        parts = (keep + swap(give).astype(f32)).astype(bf16)
        return back_ctx([parts[k] for k in range(nc)])

    turned = jnp.asarray(turn_matrix(), f32)

    gain_in = gain_attn.astype(f32)[None]
    gain_query = gain_q.astype(f32)[None]
    gain_latent = gain_kv.astype(f32)[None]
    gain_middle = turn_gain(gain_mlp.astype(f32))

    spread_q = jnp.asarray(spread_queries(heads), bf16)
    spread_k = jnp.asarray(spread_keys(heads), bf16)
    own_qb = lax.dynamic_slice_in_dim(w_qb, c * heads * (NOPE + ROPE), heads * (NOPE + ROPE), axis=1)
    own_kvb = lax.dynamic_slice_in_dim(w_kvb, c * heads * (NOPE + VDIM), heads * (NOPE + VDIM), axis=1)
    wide_qb = dot(own_qb, spread_q, NN).astype(bf16)
    wide_kvb = jnp.concatenate(
        [
            dot(own_kvb, spread_k, NN).astype(bf16),
            jnp.asarray(spread_rope(heads), bf16),
            jnp.zeros((lat_width - qrank - kvrank, heads * 2 * LANES), bf16),
        ],
        axis=0,
    )

    half_of = lambda w, d: ((half, w), d)
    out_parts = across(split_columns([w_o], "ctx", 2, nc), "ctx", nc)
    down_parts = weight_parts(w_down)
    outs = plain(
        functools.partial(enter_kernel, sizes, block),
        ids,
        [
            tokens[0],
            cotangent[0],
            segments,
            jnp.asarray(frequencies(ROPE, 0)),
            gain_in,
            gain_query,
            gain_latent,
            w_qa,
            w_kva,
            turned,
        ],
        [
            half_of(ROPE, f32),
            half_of(ROPE, f32),
            half_of(width, bf16),
            half_of(lat_width, bf16),
            half_of(qrank, f32),
            half_of(kvrank, f32),
            half_of(width, bf16),
            half_of(width, bf16),
            half_of(width, bf16),
        ]
        + [half_of(nz * block, bf16)] * nc,
        [pltpu.VMEM((half, width), bf16)] * 2,
        flops=2 * half * width * (qrank + kvrank),
    )
    own_cos, own_sin, _, latents, q_latent, kv_latent, own_tokens, own_cotangent, grad_mlp = outs[:9]
    normed_parts = outs[9:]
    lat_parts = along_ctx(latents)

    out_parts[0] = after(out_parts[0], latents)
    own_out = stack_blocks(out_parts, 2)[0]
    down_parts[0] = after(down_parts[0], own_out, wide_qb, wide_kvb)
    down = gather_weights(down_parts)
    out_pieces = gather_dp(after(own_out, down_parts[1], down_parts[2], down_parts[3]))
    lat_parts[0] = after(lat_parts[0], out_pieces[1])
    lat_own = jnp.stack(lat_parts)
    lat_oth = swap(lat_own)
    pair_parts = weight_parts(after(w_gate, out_pieces[2]), w_up)
    o_own, o_oth, q_rot, keys, values, qn, kvn, cos_table, sin_table = attend(
        nt, ids, lat_own, lat_oth, after(wide_qb, out_pieces[2]), wide_kvb, segments
    )
    out_pieces[0] = after(out_pieces[0], o_own)
    full_out = plain(
        functools.partial(spread_kernel, heads, nz),
        ids,
        out_pieces,
        [((nc, nz, block, heads * LANES), bf16)],
    )[0].reshape(width, heads * LANES)
    keep, give = project_out(o_own, o_oth, full_out)
    pair_parts[0] = after(pair_parts[0], keep)
    pair = gather_weights(pair_parts)
    gm = gather_dp(after(grad_mlp, *pair_parts[1:]))
    attn = reduce_ctx(keep, give)
    resid, normed_mid = plain(
        functools.partial(middle_kernel, len(attn)),
        ids,
        attn + [own_tokens, gain_middle],
        [half_of(width, f32), half_of(width, bf16)],
    )
    nm = gather_dp(after(normed_mid, gm[1]))
    groups = [range(0, nz // 2), range(nz // 2, nz)]
    nm_all, gm_all, hidden, grad_gate, grad_up, grad_parts, mlp_parts = [], [], [], [], [], [], []
    for group in groups:
        nm_own = jnp.concatenate([nm[k] for k in group])
        gm_own = jnp.concatenate([gm[k] for k in group])
        if hidden:
            nm_own = after(nm_own, hidden[0])
        nm_oth, gm_oth = swap(nm_own), swap(gm_own)
        nm_all += [nm_own, nm_oth]
        gm_all += [gm_own, gm_oth]
        hid, gg, gu, gn_own, gn_oth, ml_own, ml_oth = feed_forward(
            nc, nm_own, nm_oth, gm_own, gm_oth, pair, down
        )
        hidden.append(hid)
        grad_gate.append(gg)
        grad_up.append(gu)
        for parts, own, oth in ((grad_parts, gn_own, gn_oth), (mlp_parts, ml_own, ml_oth)):
            total = (own.astype(f32) + swap(oth).astype(f32)).astype(bf16)
            parts += [total[i * half : (i + 1) * half] for i in range(len(group))]
    grad_normed = scatter_dp(grad_parts)
    gm_all[0] = after(gm_all[0], grad_normed[1])
    down_product = products(gm_all, [hidden], nc)
    down_product = scatter_weights(down_product)
    nm_all[0] = after(nm_all[0], grad_normed[3])
    pair_product = products(nm_all, [grad_gate, grad_up], nc)
    grad_normed[0] = after(grad_normed[0], pair_product)

    grad_resid, grad_attn, grad_gain_mlp = plain(
        functools.partial(back_middle_kernel, nz),
        ids,
        grad_normed + [resid, own_cotangent, gain_middle],
        [half_of(width, f32), half_of(width, bf16), ((1, width), f32)],
    )
    ga_parts = along_ctx(grad_attn)
    mlp_parts = scatter_dp([after(part, grad_attn) for part in mlp_parts])
    ga_own = jnp.stack(ga_parts)
    ga_oth = swap(ga_own)
    pair_product = scatter_weights(after(pair_product, ga_own))
    g_own, g_oth = project_heads(ga_own, ga_oth, full_out)
    grad_q, grad_kv = attend_back(
        nt, ids, q_rot, keys, values, o_own, o_oth, g_own, g_oth, cos_table, sin_table
    )
    mlp_parts[0] = after(mlp_parts[0], grad_q)
    layer_out = plain(
        functools.partial(leave_kernel, sizes, block, nz),
        ids,
        mlp_parts + [resid],
        [half_of(width, bf16)],
        [pltpu.VMEM((half, width), f32)],
    )[0]
    (grad_w_down,) = weight_rows(after(down_product, *mlp_parts))
    grad_lat = reduce_ctx(*grad_latent(sizes, ids, grad_q, grad_kv, wide_qb, wide_kvb))

    ups = grad_ups(qn, after(kvn, grad_lat[0]), grad_q, grad_kv)
    deep = ups.shape[0] // nz
    ups = ups.reshape(nz, deep, heads * LANES)
    ups = scatter_dp([pick(ups, z ^ k) for k in range(nz)])
    out_product = grad_out_weight(
        sizes, block, ids, ga_own, after(ga_oth, grad_lat[0], ups[0]), o_own, o_oth
    )
    grad_lat[0] = after(grad_lat[0], out_product)
    grad_lat, grad_gain_q, grad_gain_kv = plain(
        functools.partial(grad_enter_kernel, len(grad_lat)),
        ids,
        grad_lat + [q_latent, kv_latent, gain_query, gain_latent, own_cos, own_sin, turned],
        [half_of(lat_width, bf16), ((1, qrank), f32), ((1, KVRANK), f32)],
    )
    gl_parts = along_ctx(grad_lat)
    grad_tokens, grad_gain_attn = plain(
        functools.partial(grad_tokens_kernel, sizes, block),
        ids,
        [grad_lat, w_qa, w_kva, tokens[0], gain_in, grad_resid],
        [half_of(width, bf16), ((1, width), f32)],
        [pltpu.VMEM((half, width), f32)],
        flops=2 * half * width * (qrank + kvrank),
    )
    ups[0] = after(ups[0], grad_lat)
    own = sum(p.astype(f32) for p in ups).astype(bf16)
    ups = gather_dp(own)
    out_parts = scatter_dp([out_product[k] for k in range(nz)])
    gl_parts[0] = after(gl_parts[0], grad_tokens)
    gl_own = jnp.stack(gl_parts)
    gl_oth = swap(gl_own)

    xin_own = jnp.stack(across(normed_parts, "ctx", nc))
    xin_oth = swap(xin_own)
    share = lat_width // nt // LANES * LANES
    wide = lat_width - share
    parts = plain(
        functools.partial(grad_down_kernel, share),
        ids,
        [xin_own, xin_oth, gl_own, gl_oth],
        [((nz, block, wide), bf16)],
        flops=2 * length * nz * block * wide,
    )[0]
    ups[0] = after(ups[0], parts)
    ups = stack_blocks([piece[None] for piece in ups], 1).reshape(nz * deep, heads * LANES)
    ups = along_ctx(ups)
    out_parts[0] = after(out_parts[0], parts)
    own = sum(p.astype(f32) for p in out_parts).astype(bf16)
    out_parts = across([pick(own, c ^ k)[None] for k in range(nc)], "ctx", nc)
    own = scatter_dp([parts[k] for k in range(nz)])
    grad_w_gate, grad_w_up = weight_rows(after(pair_product, own[-1]))
    own = sum(p.astype(f32) for p in own).astype(bf16)
    grad_w_qa, grad_w_kva = plain(
        functools.partial(finish_down_kernel, share),
        ids,
        [own, swap(own)],
        [((block, qrank), f32), ((block, kvrank), f32)],
    )
    (grad_w_o,) = join_columns(out_parts, "ctx", 2)
    grad_w_qb, grad_w_kvb = plain(
        functools.partial(finish_ups_kernel, heads, nc),
        ids,
        [jnp.stack(ups)],
        [((qrank, nc * heads * (NOPE + ROPE)), f32), ((KVRANK, nc * heads * LANES), f32)],
    )
    layer_out = join_rows(layer_out)
    grad_tokens = join_rows(grad_tokens)

    turned_gain = jnp.swapaxes(grad_gain_mlp.reshape(nc, nz, block), 0, 1).reshape(1, width)
    gains = jnp.concatenate([grad_gain_attn, grad_gain_q, grad_gain_kv, turned_gain], axis=1)
    gains = gains.reshape(-1, LANES)
    for axis, size in (("tensor", nt), ("ctx", nc), ("dp", nz)):
        step = 1
        while step < size:
            gains = gains + exchange(gains, axis, step, size)
            step *= 2
    gains = gains.reshape(-1)
    ends = np.cumsum([width, qrank, KVRANK])
    grad_gain_attn, grad_gain_q, grad_gain_kv, grad_gain_mlp = jnp.split(gains, ends)
    return (
        layer_out,
        grad_tokens,
        grad_gain_attn,
        grad_w_qa,
        grad_gain_q,
        grad_w_kva,
        grad_gain_kv,
        grad_w_qb,
        grad_w_kvb,
        grad_w_o,
        grad_gain_mlp,
        grad_w_gate,
        grad_w_up,
        grad_w_down,
    )


def solution(mesh):
    placed = (
        P("dp", "ctx", None),
        P("dp", None),
        P(),
        P(),
        P(),
        P(),
        P(),
        P(None, "tensor"),
        P(None, "tensor"),
        P(("dp", "ctx"), "tensor"),
        P(),
        P(("dp", "ctx"), "tensor"),
        P(("dp", "ctx"), "tensor"),
        P(("dp", "ctx"), "tensor"),
        P("dp", "ctx", None),
    )
    sizes = tuple(mesh.shape[name] for name in ("tensor", "dp", "ctx"))
    return jax.shard_map(
        functools.partial(body, sizes),
        mesh=mesh,
        in_specs=placed,
        out_specs=(
            P("dp", "ctx", None),
            P("dp", "ctx", None),
            P(),
            P(("dp", "ctx"), None),
            P(),
            P(("dp", "ctx"), None),
            P(),
            P(None, "tensor"),
            P(None, "tensor"),
            P(("dp", "ctx"), "tensor"),
            P(),
            P(("dp", "ctx"), "tensor"),
            P(("dp", "ctx"), "tensor"),
            P(("dp", "ctx"), "tensor"),
        ),
        check_vma=False,
    )
```

```python
import functools
import math

import jax
import jax.numpy as jnp
import numpy as np
from jax import lax
from jax.experimental import pallas as pl
from jax.experimental.pallas import tpu as pltpu
from jax.sharding import PartitionSpec as P

NOPE = 64
ROPE = 32
VDIM = 64
KVRANK = 256
LANES = 128
QUERY_BLOCK = 256

eps_norm = 1e-05
res_scale = 1.4 / math.sqrt(62.0)
rope_base = 10000.0
masked_score = -1e30
score_scale = 1.0 / math.sqrt(NOPE + ROPE)
exponent = score_scale * math.log2(math.e)

f32 = jnp.float32
bf16 = jnp.bfloat16


def rms_scale(values):
    return values * lax.rsqrt(jnp.mean(values * values, axis=-1, keepdims=True) + eps_norm)


def dot(left, right, contract):
    return lax.dot_general(left, right, (contract, ((), ())), preferred_element_type=f32)


NN = ((1,), (0,))
NT = ((1,), (1,))
TN = ((0,), (0,))


def exchange(value, axis, step, size):
    return lax.ppermute(value, axis, [(i, i ^ step) for i in range(size)])


def after(value, *done):
    return lax.optimization_barrier((value,) + done)[0]


def pick(stacked, index):
    return lax.dynamic_index_in_dim(stacked, index, axis=0, keepdims=False)


def spread_queries(heads):
    out = np.zeros((heads, NOPE + ROPE, heads, 2, LANES), np.float32)
    half = ROPE // 2
    for h in range(heads):
        for j in range(NOPE + ROPE):
            out[h, j, h, 0, j] = 1.0
        for j in range(half):
            out[h, NOPE + half + j, h, 1, NOPE + j] = -1.0
            out[h, NOPE + j, h, 1, NOPE + half + j] = 1.0
    return out.reshape(heads * (NOPE + ROPE), heads * 2 * LANES)


def spread_keys(heads):
    out = np.zeros((heads, NOPE + VDIM, heads, 2, LANES), np.float32)
    for h in range(heads):
        for j in range(NOPE):
            out[h, j, h, 0, j] = 1.0
        for j in range(VDIM):
            out[h, NOPE + j, h, 1, j] = 1.0
    return out.reshape(heads * (NOPE + VDIM), heads * 2 * LANES)


def spread_rope(heads):
    out = np.zeros((ROPE, heads, 2, LANES), np.float32)
    for j in range(ROPE):
        out[j, :, 0, NOPE + j] = 1.0
    return out.reshape(ROPE, heads * 2 * LANES)


def spread_values(heads):
    out = np.zeros((heads, VDIM, heads, LANES), np.float32)
    for h in range(heads):
        for j in range(VDIM):
            out[h, j, h, j] = 1.0
    return out.reshape(heads * VDIM, heads * LANES)


def split_low(value):
    first = value.astype(bf16).astype(f32)
    second = (value - first).astype(bf16).astype(f32)
    third = (value - first - second).astype(bf16).astype(f32)
    return first, second, third


def rms_back(values, grad):
    inverse = lax.rsqrt(jnp.mean(values * values, axis=-1, keepdims=True) + eps_norm)
    scaled = values * inverse
    return (grad - scaled * jnp.mean(grad * scaled, axis=-1, keepdims=True)) * inverse


def turn_matrix():
    half = ROPE // 2
    out = np.zeros((ROPE, ROPE), np.float32)
    for j in range(half):
        out[half + j, j] = -1.0
        out[j, half + j] = 1.0
    return out


def frequencies(lanes, start):
    half = ROPE // 2
    out = np.zeros((1, lanes), np.float32)
    freqs = rope_base ** (-np.arange(0, ROPE, 2).astype(np.float32) / ROPE)
    out[0, start : start + half] = freqs
    out[0, start + half : start + ROPE] = freqs
    return out


def documents(segments, index):
    first = jnp.sum((segments < 1).astype(jnp.int32))
    second = jnp.sum((segments < 2).astype(jnp.int32))
    number = (index >= first).astype(jnp.int32) + (index >= second).astype(jnp.int32)
    start = jnp.where(index >= second, second, jnp.where(index >= first, first, 0))
    return number, start


def total_of(refs):
    total = refs[0][...].astype(f32)
    for ref in refs[1:]:
        total = total + ref[...].astype(f32)
    return total


def move_blocks(source, target, outer, inner, block, cast=None):
    for i in range(outer):
        for j in range(inner):
            value = source[:, (i * inner + j) * block : (i * inner + j + 1) * block]
            target[:, (j * outer + i) * block : (j * outer + i + 1) * block] = (
                value if cast is None else cast(value)
            )


SCALARS = pl.BlockSpec(memory_space=pltpu.SMEM)
LOCAL = pl.BlockSpec(memory_space=pltpu.VMEM)


def params(megabytes=48):
    return pltpu.CompilerParams(vmem_limit_bytes=megabytes * 1024 * 1024)


def grid_params(megabytes=48):
    return pltpu.CompilerParams(
        dimension_semantics=("arbitrary",), vmem_limit_bytes=megabytes * 1024 * 1024
    )


def cost(flops=0, moved=0, special=0):
    return pl.CostEstimate(
        flops=flops // 10, bytes_accessed=moved // 10, transcendentals=special // 10
    )


def plain(kernel, ids, operands, outs, scratch=(), flops=0, megabytes=48):
    moved = sum(a.size * a.dtype.itemsize for a in operands)
    moved += sum(math.prod(s) * jnp.dtype(d).itemsize for s, d in outs)
    return pl.pallas_call(
        kernel,
        in_specs=[SCALARS] + [LOCAL] * len(operands),
        out_specs=[LOCAL] * len(outs),
        out_shape=[jax.ShapeDtypeStruct(s, d) for s, d in outs],
        scratch_shapes=list(scratch),
        compiler_params=params(megabytes),
        cost_estimate=cost(flops, moved),
    )(ids, *operands)


def enter_kernel(
    sizes, block, ids, tok, cot, segments, freqs, gain_in, gain_query, gain_latent, w_qa, w_kva, turned,
    cos_ref, sin_ref, normed_ref, lat_ref, q_ref, kv_ref, x_ref, cot_ref, gm_ref, *rest
):
    nt, nz, nc = sizes
    pieces, (inner, plain_ref) = rest[:nc], rest[nc:]
    half = normed_ref.shape[0]
    qrank = w_qa.shape[1]
    index = (ids[2] * nt + ids[0]) * half + lax.broadcasted_iota(jnp.int32, (half, ROPE), 0)
    _, start = documents(segments[...], index)
    angles = (index - start).astype(f32) * freqs[...]
    cosine, sine = jnp.cos(angles), jnp.sin(angles)
    cos_ref[...] = cosine
    sin_ref[...] = sine
    here = pl.ds(pl.multiple_of(ids[0] * half, half), half)
    own = tok[here, :]
    hidden = own.astype(f32)
    normed = (rms_scale(hidden) * gain_in[...]).astype(bf16)
    normed_ref[...] = normed
    q_latent = dot(normed, w_qa[...], NN)
    kv_latent = dot(normed, w_kva[...], NT)
    q_ref[...] = q_latent
    kv_ref[...] = kv_latent
    lat_ref[:, :qrank] = (rms_scale(q_latent) * gain_query[...]).astype(bf16)
    c_round = rms_scale(kv_latent[:, :KVRANK]).astype(bf16).astype(f32)
    lat_ref[:, qrank : qrank + KVRANK] = (c_round * gain_latent[...]).astype(bf16)
    rope = kv_latent[:, KVRANK:]
    other = jnp.dot(rope, turned[...], precision=lax.Precision.HIGHEST, preferred_element_type=f32)
    end = qrank + KVRANK + ROPE
    lat_ref[:, qrank + KVRANK : end] = (rope * cosine + other * sine).astype(bf16)
    lat_ref[:, end:] = jnp.zeros((half, lat_ref.shape[1] - end), bf16)
    move_blocks(normed_ref, inner, nz, nc, block)
    span = nz * block
    for k in range(nc):
        start = pl.multiple_of((ids[2] ^ k) * span, span)
        pieces[k][...] = inner[:, pl.ds(start, span)]
    plain_ref[...] = own
    move_blocks(plain_ref, x_ref, nz, nc, block)
    plain_ref[...] = cot[here, :]
    move_blocks(plain_ref, cot_ref, nz, nc, block)
    gm_ref[...] = (res_scale * cot_ref[...].astype(f32)).astype(bf16)


def forward_kernel(
    nt, ids, own_ref, oth_ref, wq_ref, wkv_ref, segments, freqs,
    oown_ref, ooth_ref, q_ref, k_ref, v_ref, qn_ref, kvn_ref, cos_ref, sin_ref, qtab_ref, ktab_ref
):
    t, c = ids[0], ids[2]
    nc, half = own_ref.shape[0], own_ref.shape[1]
    length, qrank = qn_ref.shape
    block = nt * half

    @pl.when(pl.program_id(0) == 0)
    def _():
        for j in range(nc):
            for i in range(nt):
                rows = pl.ds((j * nt + i) * half, half)
                value = jnp.where(t == i, own_ref[c ^ j], oth_ref[c ^ j])
                qn_ref[rows, :] = value[:, :qrank]
                kvn_ref[rows, :] = value[:, qrank:]
        index = lax.broadcasted_iota(jnp.int32, (length, LANES), 0)
        lane = lax.broadcasted_iota(jnp.int32, (length, LANES), 1)
        number, start = documents(segments[...], index)
        angles = (index - start).astype(f32) * freqs[...]
        cos_ref[...] = jnp.where(lane < NOPE + ROPE, jnp.cos(angles), 0.0)
        sin_ref[...] = jnp.sin(angles)
        at = lane - (NOPE + ROPE + 3)
        same = at == number
        qtab_ref[...] = jnp.where(same, masked_score, 0.0)
        ones = (at >= -3) & (at < 3) & jnp.logical_not(same)
        ktab_ref[...] = jnp.where(ones, 1.0, 0.0)

    raw = jnp.dot(qn_ref[...], wq_ref[...], preferred_element_type=f32)
    query = raw[:, :LANES] * cos_ref[...] + raw[:, LANES:] * sin_ref[...] + qtab_ref[...]
    q_ref[...] = query.astype(bf16)
    both = jnp.dot(kvn_ref[...], wkv_ref[...], preferred_element_type=f32)
    k_ref[...] = (both[:, :LANES] + ktab_ref[...]).astype(bf16)
    lane = lax.broadcasted_iota(jnp.int32, (length, LANES), 1)
    ones = (lane >= VDIM) & (lane < VDIM + 3)
    v_ref[...] = jnp.where(ones, 1.0, both[:, LANES:]).astype(bf16)
    lane = lax.broadcasted_iota(jnp.int32, (block, LANES), 1)
    after = lax.broadcasted_iota(jnp.int32, (block, block), 1) > lax.broadcasted_iota(
        jnp.int32, (block, block), 0
    )
    for i in range(nc):
        here = pl.ds(i * block, block)
        query = q_ref[here, :]
        own = dot(query, k_ref[here, :], NT)
        own = jnp.where(after, masked_score, own)
        highest = jnp.max(own, axis=1, keepdims=True)
        if i:
            before = pl.ds(0, i * block)
            past = dot(query, k_ref[before, :], NT)
            highest = jnp.maximum(highest, jnp.max(past, axis=1, keepdims=True))
        weights = jnp.exp2((own - highest) * exponent).astype(bf16)
        mixed = dot(weights, v_ref[here, :], NN)
        if i:
            weights = jnp.exp2((past - highest) * exponent).astype(bf16)
            mixed = mixed + dot(weights, v_ref[before, :], NN)
        total = mixed[:, VDIM : VDIM + 1]
        out = jnp.where(lane < VDIM, mixed / total, 0.0).astype(bf16)
        for j in range(nt):
            part = out[j * half : (j + 1) * half]

            @pl.when(t == j)
            def _():
                oown_ref[c ^ i] = part

            @pl.when(t != j)
            def _():
                ooth_ref[c ^ i] = part

        first, second, third = split_low(-(highest + jnp.log2(total) / exponent))
        at = NOPE + ROPE
        kept = jnp.where(
            lane == at,
            first,
            jnp.where(lane == at + 1, second, jnp.where(lane == at + 2, third, query.astype(f32))),
        )
        q_ref[here, :] = kept.astype(bf16)


def backward_kernel(
    nt, ids, q_ref, k_ref, v_ref, oown_ref, ooth_ref, gown_ref, goth_ref, cos_ref, sin_ref,
    dq_ref, dkv_ref, grad_ref, dk_acc, dv_acc
):
    t, c = ids[0], ids[2]
    nc, half = gown_ref.shape[0], gown_ref.shape[1]
    length = q_ref.shape[0]
    block = nt * half
    lane = lax.broadcasted_iota(jnp.int32, (half, LANES), 1)
    for j in range(nc):
        for i in range(nt):
            grad = jnp.where(t == i, gown_ref[c ^ j], goth_ref[c ^ j]).astype(f32)
            out = jnp.where(t == i, oown_ref[c ^ j], ooth_ref[c ^ j]).astype(f32)
            first, second, third = split_low(-jnp.sum(grad * out, axis=1, keepdims=True))
            grad = jnp.where(
                lane == VDIM,
                first,
                jnp.where(lane == VDIM + 1, second, jnp.where(lane == VDIM + 2, third, grad)),
            )
            grad_ref[pl.ds((j * nt + i) * half, half), :] = grad.astype(bf16)
    after = lax.broadcasted_iota(jnp.int32, (block, block), 0) > lax.broadcasted_iota(
        jnp.int32, (block, block), 1
    )
    for i in reversed(range(nc)):
        here = pl.ds(i * block, block)
        query, grad = q_ref[here, :], grad_ref[here, :]

        def part(span, masked):
            keys = k_ref[span, :]
            scores = dot(keys, query, NT)
            if masked:
                scores = jnp.where(after, masked_score, scores)
            probs = jnp.exp2(scores * exponent)
            inward = dot(v_ref[span, :], grad, NT)
            low = (probs * inward).astype(bf16)
            dv = dot(probs.astype(bf16), grad, NN)
            dk = dot(low, query, NN)
            if i == nc - 1:
                dv_acc[span, :] = dv
                dk_acc[span, :] = dk
            else:
                dv_acc[span, :] += dv
                dk_acc[span, :] += dk
            return dot(low, keys, TN)

        dq = part(here, True)
        if i:
            dq = dq + part(pl.ds(0, i * block), False)
        dq = dq * score_scale
        dq_ref[here, :LANES] = (dq * cos_ref[here, :]).astype(bf16)
        dq_ref[here, LANES:] = (dq * sin_ref[here, :]).astype(bf16)
    lane = lax.broadcasted_iota(jnp.int32, (length, LANES), 1)
    dkv_ref[:, :LANES] = jnp.where(lane < NOPE + ROPE, dk_acc[...] * score_scale, 0.0).astype(bf16)
    dkv_ref[:, LANES:] = jnp.where(lane < VDIM, dv_acc[...], 0.0).astype(bf16)


def attend(nt, ids, own, oth, wq, wkv, segments):
    nc, half, _ = own.shape
    length = nc * nt * half
    qrank, kvrank = wq.shape[0], wkv.shape[0]
    heads = wq.shape[1] // (2 * LANES)
    whole = lambda a: pl.BlockSpec(a.shape, lambda h, ids: (0,) * a.ndim)
    column = lambda rows, width: pl.BlockSpec((rows, width), lambda h, ids: (0, h))
    split = pl.BlockSpec((nc, half, LANES), lambda h, ids: (0, 0, h))
    out = jax.ShapeDtypeStruct((length, heads * LANES), bf16)
    out_split = jax.ShapeDtypeStruct((nc, half, heads * LANES), bf16)
    kept = [
        jax.ShapeDtypeStruct((length, qrank), bf16),
        jax.ShapeDtypeStruct((length, kvrank), bf16),
        jax.ShapeDtypeStruct((length, LANES), f32),
        jax.ShapeDtypeStruct((length, LANES), f32),
    ]
    freqs = jnp.asarray(frequencies(LANES, NOPE))
    return pl.pallas_call(
        functools.partial(forward_kernel, nt),
        grid_spec=pltpu.PrefetchScalarGridSpec(
            num_scalar_prefetch=1,
            grid=(heads,),
            in_specs=[
                whole(own),
                whole(oth),
                column(qrank, 2 * LANES),
                column(kvrank, 2 * LANES),
                whole(segments),
                whole(freqs),
            ],
            out_specs=[split] * 2 + [column(length, LANES)] * 3 + [whole(a) for a in kept],
            scratch_shapes=[pltpu.VMEM((length, LANES), f32)] * 2,
        ),
        out_shape=[out_split] * 2 + [out] * 3 + kept,
        compiler_params=grid_params(),
        cost_estimate=cost(
            4 * heads * length * (length * LANES + qrank * 2 * LANES),
            16 * length * heads * LANES,
            heads * length * length // 2,
        ),
    )(ids, own, oth, wq, wkv, segments, freqs)


def attend_back(nt, ids, q, k, v, oown, ooth, gown, goth, cosine, sine):
    nc, half, _ = oown.shape
    length = q.shape[0]
    heads = q.shape[1] // LANES
    whole = lambda a: pl.BlockSpec(a.shape, lambda h, ids: (0, 0))
    column = lambda width: pl.BlockSpec((length, width), lambda h, ids: (0, h))
    split = pl.BlockSpec((nc, half, LANES), lambda h, ids: (0, 0, h))
    out = jax.ShapeDtypeStruct((length, heads * 2 * LANES), bf16)
    return pl.pallas_call(
        functools.partial(backward_kernel, nt),
        grid_spec=pltpu.PrefetchScalarGridSpec(
            num_scalar_prefetch=1,
            grid=(heads,),
            in_specs=[column(LANES)] * 3 + [split] * 4 + [whole(cosine), whole(sine)],
            out_specs=[column(2 * LANES)] * 2,
            scratch_shapes=[
                pltpu.VMEM((length, LANES), bf16),
                pltpu.VMEM((length, LANES), f32),
                pltpu.VMEM((length, LANES), f32),
            ],
        ),
        out_shape=[out] * 2,
        compiler_params=grid_params(),
        cost_estimate=cost(
            8 * heads * length * length * LANES,
            24 * length * heads * LANES,
            heads * length * length // 2,
        ),
    )(ids, q, k, v, oown, ooth, gown, goth, cosine, sine)


def split_kernel(axis, pieces, count, ids, *refs):
    width = refs[count].shape[2]
    for k in range(pieces):
        for j in range(pieces):

            @pl.when((ids[axis] ^ k) == j)
            def _():
                for i in range(count):
                    refs[count + k][i] = refs[i][:, j * width : (j + 1) * width]


def join_kernel(axis, pieces, ids, *refs):
    targets = refs[pieces:]
    width = refs[0].shape[2]
    for k in range(pieces):
        for j in range(pieces):

            @pl.when((ids[axis] ^ k) == j)
            def _():
                for i, target in enumerate(targets):
                    target[:, j * width : (j + 1) * width] = refs[k][i].astype(target.dtype)


def stack_kernel(axis, pieces, ids, *refs):
    for k in range(pieces):
        for i in range(refs[k].shape[0]):
            refs[pieces][i, ids[axis] ^ k] = refs[k][i]


def rows_kernel(ids, own, oth, target):
    half = own.shape[0]
    target[pl.ds(pl.multiple_of(ids[0] * half, half), half), :] = own[...]
    target[pl.ds(pl.multiple_of((1 - ids[0]) * half, half), half), :] = oth[...]


def spread_kernel(heads, pieces, ids, *refs):
    target = refs[pieces]
    target[...] = jnp.zeros_like(target)
    for k in range(pieces):
        for j in range(refs[k].shape[0]):
            for h in range(heads):
                target[j, ids[1] ^ k, :, h * LANES : h * LANES + VDIM] = refs[k][
                    j, :, h * VDIM : (h + 1) * VDIM
                ]


def out_kernel(own, oth, weight, keep, give):
    per, half, _ = own.shape
    both = jnp.concatenate([ref[i] for ref in (own, oth) for i in range(per)], axis=0)
    result = dot(both, weight[...], NT)
    for i in range(per):
        keep[i] = result[i * half : (i + 1) * half]
        give[i] = result[(per + i) * half : (per + i + 1) * half].astype(bf16)


def project_out(own, oth, weight):
    nc, half, deep = own.shape
    width = weight.shape[0]
    per = math.gcd(nc, 2)
    piece = lambda w: pl.BlockSpec((per, half, w), lambda k: (k, 0, 0))
    return pl.pallas_call(
        out_kernel,
        grid=(nc // per,),
        in_specs=[piece(deep)] * 2 + [pl.BlockSpec(weight.shape, lambda k: (0, 0))],
        out_specs=[piece(width)] * 2,
        out_shape=[
            jax.ShapeDtypeStruct((nc, half, width), f32),
            jax.ShapeDtypeStruct((nc, half, width), bf16),
        ],
        compiler_params=grid_params(),
        cost_estimate=cost(4 * nc * half * deep * width, 2 * weight.size + 16 * nc * half * width),
    )(own, oth, weight)


def heads_kernel(own, oth, weight, gown, goth):
    per, half, _ = own.shape
    both = jnp.concatenate([ref[i] for ref in (own, oth) for i in range(per)], axis=0)
    result = dot(both, weight[...], NN).astype(bf16)
    for i in range(per):
        gown[i] = result[i * half : (i + 1) * half]
        goth[i] = result[(per + i) * half : (per + i + 1) * half]


def project_heads(own, oth, weight):
    nc, half, width = own.shape
    deep = weight.shape[1]
    per = math.gcd(nc, 2)
    piece = lambda w: pl.BlockSpec((per, half, w), lambda k: (k, 0, 0))
    return pl.pallas_call(
        heads_kernel,
        grid=(nc // per,),
        in_specs=[piece(width)] * 2 + [pl.BlockSpec(weight.shape, lambda k: (0, 0))],
        out_specs=[piece(deep)] * 2,
        out_shape=[jax.ShapeDtypeStruct((nc, half, deep), bf16)] * 2,
        compiler_params=grid_params(),
        cost_estimate=cost(4 * nc * half * deep * width, 2 * weight.size + 8 * nc * half * width),
    )(own, oth, weight)


def middle_kernel(pieces, ids, *refs):
    tokens, gain, resid_ref, normed_ref = refs[pieces:]
    resid = tokens[...].astype(f32) + res_scale * total_of(refs[:pieces])
    resid_ref[...] = resid
    normed_ref[...] = (rms_scale(resid) * gain[...]).astype(bf16)


def leave_kernel(sizes, block, pieces, ids, *refs):
    resid, target, inner = refs[pieces:]
    nt, nz, nc = sizes
    inner[...] = resid[...] + res_scale * total_of(refs[:pieces])
    move_blocks(inner, target, nc, nz, block, lambda value: value.astype(bf16))


def mlp_kernel(
    nm_own, nm_oth, gm_own, gm_oth, pair_hbm, down_hbm,
    hid_ref, gg_ref, gu_ref, gn_own, gn_oth, ml_own, ml_oth, w_gate, w_up, w_down, sems
):
    step = pl.program_id(0)
    blocks = sems.shape[1]
    deep = w_down.shape[0] // blocks
    copies = [
        [
            pltpu.make_async_copy(
                source.at[pl.ds((j * count + at) * deep, deep), :],
                target.at[pl.ds(j * deep, deep), :],
                sems.at[i, j],
            )
            for j in range(blocks)
        ]
        for i, (source, count, at, target) in enumerate(
            ((pair_hbm, 2, 0, w_gate), (pair_hbm, 2, 1, w_up), (down_hbm, 1, 0, w_down))
        )
    ]

    def ready(i):
        @pl.when(step == 0)
        def _():
            for copy in copies[i]:
                copy.wait()

    @pl.when(step == 0)
    def _():
        for group in copies:
            for copy in group:
                copy.start()

    block = nm_own.shape[0]
    normed = jnp.concatenate([nm_own[...], nm_oth[...]], axis=0)
    ready(0)
    gate = dot(normed, w_gate[...], NN)
    ready(1)
    up_proj = dot(normed, w_up[...], NN)
    ready(2)
    grad_hidden = dot(jnp.concatenate([gm_own[...], gm_oth[...]], axis=0), w_down[...], NN)
    sigma = jax.nn.sigmoid(gate)
    silu_gate = gate * sigma
    hidden = (silu_gate * up_proj).astype(bf16)
    grad_gate = (grad_hidden * up_proj * sigma * (1.0 + gate * (1.0 - sigma))).astype(bf16)
    grad_up = (grad_hidden * silu_gate).astype(bf16)
    for target, value in ((hid_ref, hidden), (gg_ref, grad_gate), (gu_ref, grad_up)):
        target[0] = value[:block]
        target[1] = value[block:]
    mlp = dot(hidden, w_down[...], NT).astype(bf16)
    ml_own[...] = mlp[:block]
    ml_oth[...] = mlp[block:]
    grad_normed = (dot(grad_gate, w_gate[...], NT) + dot(grad_up, w_up[...], NT)).astype(bf16)
    gn_own[...] = grad_normed[:block]
    gn_oth[...] = grad_normed[block:]


def feed_forward(blocks, nm_own, nm_oth, gm_own, gm_oth, pair, down):
    rows, width = nm_own.shape
    ff = down.shape[1]
    block = min(rows, 256)
    part_of = pl.BlockSpec((block, width), lambda i: (i, 0))
    inner = pl.BlockSpec((2, block, ff), lambda i: (0, i, 0))
    anywhere = pl.BlockSpec(memory_space=pl.ANY)
    held = jax.ShapeDtypeStruct((2, rows, ff), bf16)
    part = jax.ShapeDtypeStruct((rows, width), bf16)
    made = pl.pallas_call(
        mlp_kernel,
        grid=(rows // block,),
        in_specs=[part_of] * 4 + [anywhere] * 2,
        out_specs=[inner] * 3 + [part_of] * 4,
        out_shape=[held] * 3 + [part] * 4,
        scratch_shapes=[pltpu.VMEM((width, ff), bf16)] * 3
        + [pltpu.SemaphoreType.DMA((3, blocks))],
        compiler_params=grid_params(60),
        cost_estimate=cost(
            24 * rows * width * ff, 6 * width * ff + 16 * rows * width, 2 * rows * ff
        ),
    )(nm_own, nm_oth, gm_own, gm_oth, pair, down)
    return [a.reshape(2 * rows, ff) for a in made[:3]] + list(made[3:])


def product_kernel(count, targets, *refs):
    left = jnp.concatenate([ref[...] for ref in refs[:count]], axis=0)
    per = count // 2
    for i in range(targets):
        right = [ref[...] for ref in refs[count + i * per : count + (i + 1) * per]]
        total = dot(left, jnp.concatenate(right, axis=0), TN)
        span = total.shape[0]
        refs[-1][i * span : (i + 1) * span, :] = total.astype(bf16)


def products(lefts, rights, parts):
    rows, width = lefts[0].shape
    ff = rights[0][0].shape[1]
    span = width // parts
    count = len(rights)
    flat = [a for group in rights for a in group]
    return pl.pallas_call(
        functools.partial(product_kernel, len(lefts), count),
        grid=(parts,),
        in_specs=[pl.BlockSpec((rows, span), lambda i: (0, i))] * len(lefts)
        + [pl.BlockSpec(a.shape, lambda i: (0, 0)) for a in flat],
        out_specs=pl.BlockSpec((count * span, ff), lambda i: (i, 0)),
        out_shape=jax.ShapeDtypeStruct((parts * count * span, ff), bf16),
        compiler_params=grid_params(),
        cost_estimate=cost(
            2 * count * len(lefts) * rows * width * ff,
            2 * len(lefts) * rows * width + 2 * count * width * ff,
        ),
    )(*lefts, *flat)


def back_middle_kernel(pieces, ids, *refs):
    resid_ref, cot, gain, grad_ref, attn_ref, gain_ref = refs[pieces:]
    grad_normed = total_of(refs[:pieces])
    resid = resid_ref[...]
    gain_ref[...] = jnp.sum(grad_normed * rms_scale(resid), axis=0, keepdims=True)
    grad = cot[...].astype(f32) + rms_back(resid, grad_normed * gain[...])
    grad_ref[...] = grad
    attn_ref[...] = (res_scale * grad).astype(bf16)


def grad_out_kernel(heads, ids, own, oth, oown, ooth, target):
    nz, _, block, _ = target.shape
    flat = lambda ref: ref[...].reshape(-1, ref.shape[2])
    total = dot(flat(own), flat(oown), TN) + dot(flat(oth), flat(ooth), TN)
    total = total.astype(bf16)
    for i in range(nz):
        for h in range(heads):
            target[ids[1] ^ i, 0, :, h * VDIM : (h + 1) * VDIM] = total[
                i * block : (i + 1) * block, h * LANES : h * LANES + VDIM
            ]


def grad_out_weight(sizes, block, ids, own, oth, oown, ooth):
    nt, nz, nc = sizes
    _, half, width = own.shape
    deep = oown.shape[2]
    heads = deep // LANES
    left = pl.BlockSpec((nc, half, nz * block), lambda j, ids: (0, 0, j))
    right = pl.BlockSpec((nc, half, deep), lambda j, ids: (0, 0, 0))
    return pl.pallas_call(
        functools.partial(grad_out_kernel, heads),
        grid_spec=pltpu.PrefetchScalarGridSpec(
            num_scalar_prefetch=1,
            grid=(nc,),
            in_specs=[left, left, right, right],
            out_specs=pl.BlockSpec((nz, 1, block, heads * VDIM), lambda j, ids: (0, j, 0, 0)),
        ),
        out_shape=jax.ShapeDtypeStruct((nz, nc, block, heads * VDIM), bf16),
        compiler_params=grid_params(),
        cost_estimate=cost(4 * nc * half * width * deep, 4 * nc * half * (width + deep)),
    )(ids, own, oth, oown, ooth)


def grad_latent_kernel(ids, gq, gkv, wq, wkv, keep, give, inner):
    half = keep.shape[1]
    qrank = wq.shape[0]
    inner[:, :qrank] = dot(gq[...], wq[...], NT)
    inner[:, qrank:] = dot(gkv[...], wkv[...], NT)
    keep[0] = inner[pl.ds(pl.multiple_of(ids[0] * half, half), half), :]
    give[0] = inner[pl.ds(pl.multiple_of((1 - ids[0]) * half, half), half), :].astype(bf16)


def grad_latent(sizes, ids, gq, gkv, wq, wkv):
    nt, _, nc = sizes
    length, deep = gq.shape
    block = length // nc
    half = block // nt
    width = wq.shape[0] + wkv.shape[0]
    rows = pl.BlockSpec((block, deep), lambda k, ids: (ids[2] ^ k, 0))
    whole = lambda a: pl.BlockSpec(a.shape, lambda k, ids: (0, 0))
    piece = pl.BlockSpec((1, half, width), lambda k, ids: (k, 0, 0))
    return pl.pallas_call(
        grad_latent_kernel,
        grid_spec=pltpu.PrefetchScalarGridSpec(
            num_scalar_prefetch=1,
            grid=(nc,),
            in_specs=[rows, rows, whole(wq), whole(wkv)],
            out_specs=[piece, piece],
            scratch_shapes=[pltpu.VMEM((block, width), f32)],
        ),
        out_shape=[
            jax.ShapeDtypeStruct((nc, half, width), f32),
            jax.ShapeDtypeStruct((nc, half, width), bf16),
        ],
        compiler_params=grid_params(),
        cost_estimate=cost(2 * length * deep * width, 4 * length * deep + 4 * width * deep),
    )(ids, gq, gkv, wq, wkv)


def grad_ups_kernel(qn, kvn, gq, gkv, target):
    qrank = qn.shape[1]
    both = dot(qn[...], gq[...], TN)
    straight, turned = both[:, :LANES], both[:, LANES:]
    lane = lax.broadcasted_iota(jnp.int32, straight.shape, 1)
    half = ROPE // 2
    low = (lane >= NOPE) & (lane < NOPE + half)
    high = (lane >= NOPE + half) & (lane < NOPE + ROPE)
    straight = straight + jnp.where(low, pltpu.roll(turned, LANES - half, 1), 0.0)
    straight = straight - jnp.where(high, pltpu.roll(turned, half, 1), 0.0)
    target[:qrank, :] = straight.astype(bf16)
    both = dot(kvn[:, :KVRANK], gkv[...], TN)
    lane = lax.broadcasted_iota(jnp.int32, (KVRANK, LANES), 1)
    values = pltpu.roll(both[:, LANES:], NOPE, 1)
    target[qrank:, :] = jnp.where(lane < NOPE, both[:, :LANES], values).astype(bf16)


def grad_ups(qn, kvn, gq, gkv):
    length, qrank = qn.shape
    heads = gq.shape[1] // (2 * LANES)
    whole = lambda a: pl.BlockSpec(a.shape, lambda h: (0, 0))
    column = pl.BlockSpec((length, 2 * LANES), lambda h: (0, h))
    return pl.pallas_call(
        grad_ups_kernel,
        grid=(heads,),
        in_specs=[whole(qn), whole(kvn), column, column],
        out_specs=pl.BlockSpec((qrank + KVRANK, LANES), lambda h: (0, h)),
        out_shape=jax.ShapeDtypeStruct((qrank + KVRANK, heads * LANES), bf16),
        compiler_params=grid_params(),
        cost_estimate=cost(
            4 * length * (qrank + KVRANK) * heads * LANES, 2 * length * (qrank + heads * 4 * LANES)
        ),
    )(qn, kvn, gq, gkv)


def finish_ups_kernel(heads, pieces, ids, source, q_ref, kv_ref):
    qrank = q_ref.shape[0]
    wide = NOPE + ROPE
    for j in range(pieces):
        value = source[ids[2] ^ j]
        for h in range(heads):
            start = (j * heads + h) * wide
            q_ref[:, start : start + wide] = value[:qrank, h * LANES : h * LANES + wide].astype(f32)
        start = j * heads * LANES
        kv_ref[:, start : start + heads * LANES] = value[qrank:, :].astype(f32)


def grad_enter_kernel(pieces, ids, *refs):
    q_ref, kv_ref, gain_query, gain_latent, cosine, sine, turned, lat_ref, gain_q, gain_kv = refs[
        pieces:
    ]
    qrank = q_ref.shape[1]
    total = total_of(refs[:pieces])
    q_latent, c_latent = q_ref[...], kv_ref[:, :KVRANK]
    grad_q, grad_c, grad_rope = total[:, :qrank], total[:, qrank : qrank + KVRANK], total[:, qrank + KVRANK : qrank + KVRANK + ROPE]
    gain_q[...] = jnp.sum(grad_q * rms_scale(q_latent), axis=0, keepdims=True)
    c_round = rms_scale(c_latent).astype(bf16).astype(f32)
    gain_kv[...] = jnp.sum(grad_c * c_round, axis=0, keepdims=True)
    lat_ref[:, :qrank] = rms_back(q_latent, grad_q * gain_query[...]).astype(bf16)
    lat_ref[:, qrank : qrank + KVRANK] = rms_back(c_latent, grad_c * gain_latent[...]).astype(bf16)
    other = jnp.dot(
        grad_rope * sine[...], turned[...], precision=lax.Precision.HIGHEST, preferred_element_type=f32
    )
    end = qrank + KVRANK + ROPE
    lat_ref[:, qrank + KVRANK : end] = (grad_rope * cosine[...] - other).astype(bf16)
    lat_ref[:, end:] = jnp.zeros((lat_ref.shape[0], lat_ref.shape[1] - end), bf16)


def grad_tokens_kernel(
    sizes, block, ids, lat, w_qa, w_kva, tok, gain_in, grad_ref, target, gain_ref, inner
):
    nt, nz, nc = sizes
    half = lat.shape[0]
    qrank = w_qa.shape[1]
    grad = dot(lat[:, :qrank], w_qa[...], NT) + dot(
        lat[:, qrank : qrank + KVRANK + ROPE], w_kva[...], NN
    )
    here = pl.ds(pl.multiple_of(ids[0] * half, half), half)
    hidden = tok[here, :].astype(f32)
    gain_ref[...] = jnp.sum(grad * rms_scale(hidden), axis=0, keepdims=True)
    move_blocks(grad_ref, inner, nc, nz, block)
    target[...] = (inner[...] + rms_back(hidden, grad * gain_in[...])).astype(bf16)


def grad_down_kernel(share, ids, own, oth, gown, goth, target):
    nz, block, wide = target.shape
    flat = lambda ref: ref[...].reshape(-1, ref.shape[2])
    columns = pl.ds(pl.multiple_of(ids[0] * share, share), wide)
    right = lambda ref: ref[:, :, columns].reshape(-1, wide)
    total = (dot(flat(own), right(gown), TN) + dot(flat(oth), right(goth), TN)).astype(bf16)
    for i in range(nz):
        target[ids[1] ^ i] = total[i * block : (i + 1) * block, :]


def finish_down_kernel(share, ids, own, oth, q_ref, kv_ref):
    first = jnp.where(ids[0] == 0, own[...], oth[...]).astype(f32)
    second = jnp.where(ids[0] == 0, oth[...], own[...]).astype(f32)
    rest = q_ref.shape[1] - share
    q_ref[:, :share] = first[:, :share]
    q_ref[:, share:] = second[:, :rest]
    kv_ref[...] = second[:, rest : rest + kv_ref.shape[1]]


def body(
    sizes,
    tokens,
    segments,
    gain_attn,
    w_qa,
    gain_q,
    w_kva,
    gain_kv,
    w_qb,
    w_kvb,
    w_o,
    gain_mlp,
    w_gate,
    w_up,
    w_down,
    cotangent,
):
    nt, nz, nc = sizes
    t, z, c = lax.axis_index("tensor"), lax.axis_index("dp"), lax.axis_index("ctx")
    ids = jnp.stack([t, z, c]).astype(jnp.int32)
    rows, width = tokens.shape[1:]
    half = rows // nt
    block = w_o.shape[0]
    length = nc * rows
    heads = w_qb.shape[1] // (NOPE + ROPE) // nc
    ff = w_gate.shape[1] // nz
    qrank, kvrank = w_qa.shape[1], w_kva.shape[1]
    w_kva = w_kva.T
    lat_width = -(-(qrank + kvrank) // LANES) * LANES
    line = nz == 4

    def turn_gain(value):
        return jnp.swapaxes(value.reshape(nz, nc, block), 0, 1).reshape(1, width)

    def swap(value):
        return exchange(value, "tensor", 1, nt)

    def along_ctx(value):
        if nc != 4:
            return [value] + [exchange(value, "ctx", k, nc) for k in range(1, nc)]
        cut = value.shape[0] // 2
        first, second = exchange(value, "ctx", 1, nc), exchange(value, "ctx", 2, nc)
        upper = exchange(second[:cut], "ctx", 1, nc)
        lower = exchange(first[cut:], "ctx", 2, nc)
        return [value, first, second, jnp.concatenate([upper, lower])]

    def back_ctx(parts):
        if nc != 4:
            return across(parts, "ctx", nc)
        cut = parts[0].shape[0] // 2
        upper = exchange(parts[3][:cut], "ctx", 1, nc).astype(f32)
        lower = exchange(parts[3][cut:], "ctx", 2, nc).astype(f32)
        first, second = parts[1].astype(f32), parts[2].astype(f32)
        first = jnp.concatenate([first[:cut], first[cut:] + lower]).astype(bf16)
        second = jnp.concatenate([second[:cut] + upper, second[cut:]]).astype(bf16)
        return [parts[0], exchange(first, "ctx", 1, nc), exchange(second, "ctx", 2, nc)]

    def gather_dp(value):
        if not line:
            return [value] + [exchange(value, "dp", k, nz) for k in range(1, nz)]
        first, second = exchange(value, "dp", 1, nz), exchange(value, "dp", 2, nz)
        near = lax.ppermute(value, "dp", [(1, 2), (2, 1)])
        far = lax.ppermute(second, "dp", [(1, 0), (2, 3)])
        return [value, first, second, jnp.where((z == 0) | (z == 3), far, near)]

    def scatter_dp(parts):
        if not line:
            return [parts[0]] + [exchange(parts[k], "dp", k, nz) for k in range(1, nz)]
        far = lax.ppermute(parts[3], "dp", [(0, 1), (3, 2)])
        first = exchange(parts[1], "dp", 1, nz)
        near = lax.ppermute(parts[3], "dp", [(1, 2), (2, 1)])
        second = (parts[2].astype(f32) + far.astype(f32)).astype(bf16)
        return [parts[0], first, exchange(second, "dp", 2, nz), near]

    def split_columns(values, axis, at, pieces):
        deep, wide = values[0].shape[0], values[0].shape[1] // pieces
        if pieces > 4:
            parts = jnp.stack(values).reshape(len(values), deep, pieces, wide)
            parts = jnp.moveaxis(parts, 2, 0)
            return [pick(parts, lax.axis_index(axis) ^ k) for k in range(pieces)]
        outs = [((len(values), deep, wide), values[0].dtype)] * pieces
        return plain(functools.partial(split_kernel, at, pieces, len(values)), ids, values, outs)

    def join_columns(parts, axis, at):
        pieces, (count, deep, wide) = len(parts), parts[0].shape
        if pieces > 4:
            stacked = jnp.stack(parts)
            index = lax.axis_index(axis)
            parts = [pick(stacked, index ^ j) for j in range(pieces)]
            return list(jnp.concatenate(parts, axis=2).astype(f32))
        outs = [((deep, pieces * wide), f32)] * count
        return plain(functools.partial(join_kernel, at, pieces), ids, parts, outs)

    def stack_blocks(parts, at):
        count = parts[0].shape[0]
        outs = [((count, len(parts)) + parts[0].shape[1:], parts[0].dtype)]
        return plain(functools.partial(stack_kernel, at, len(parts)), ids, parts, outs)[0]

    def across(parts, axis, size):
        return [parts[0]] + [exchange(parts[k], axis, k, size) for k in range(1, size)]

    def join_rows(own):
        outs = [((rows, width), bf16)]
        return plain(rows_kernel, ids, [own, swap(own)], outs)[0][None]

    def weight_parts(*values):
        return across(split_columns(values, "dp", 1, nz), "dp", nz)

    def gather_weights(parts):
        parts = stack_blocks(parts, 1).reshape(-1, ff)
        return lax.all_gather(parts, "ctx", axis=0, tiled=True)

    def scatter_weights(value):
        return lax.psum_scatter(value, "ctx", scatter_dimension=0, tiled=True)

    def weight_rows(value):
        parts = value.reshape(-1, nz, block, ff)
        parts = [lax.dynamic_index_in_dim(parts, z ^ k, axis=1, keepdims=False) for k in range(nz)]
        return join_columns(across(parts, "dp", nz), "dp", 1)

    def reduce_ctx(keep, give):
        parts = (keep + swap(give).astype(f32)).astype(bf16)
        return back_ctx([parts[k] for k in range(nc)])

    turned = jnp.asarray(turn_matrix(), f32)

    gain_in = gain_attn.astype(f32)[None]
    gain_query = gain_q.astype(f32)[None]
    gain_latent = gain_kv.astype(f32)[None]
    gain_middle = turn_gain(gain_mlp.astype(f32))

    spread_q = jnp.asarray(spread_queries(heads), bf16)
    spread_k = jnp.asarray(spread_keys(heads), bf16)
    own_qb = lax.dynamic_slice_in_dim(w_qb, c * heads * (NOPE + ROPE), heads * (NOPE + ROPE), axis=1)
    own_kvb = lax.dynamic_slice_in_dim(w_kvb, c * heads * (NOPE + VDIM), heads * (NOPE + VDIM), axis=1)
    wide_qb = dot(own_qb, spread_q, NN).astype(bf16)
    wide_kvb = jnp.concatenate(
        [
            dot(own_kvb, spread_k, NN).astype(bf16),
            jnp.asarray(spread_rope(heads), bf16),
            jnp.zeros((lat_width - qrank - kvrank, heads * 2 * LANES), bf16),
        ],
        axis=0,
    )

    half_of = lambda w, d: ((half, w), d)
    out_parts = across(split_columns([w_o], "ctx", 2, nc), "ctx", nc)
    down_parts = weight_parts(w_down)
    outs = plain(
        functools.partial(enter_kernel, sizes, block),
        ids,
        [
            tokens[0],
            cotangent[0],
            segments,
            jnp.asarray(frequencies(ROPE, 0)),
            gain_in,
            gain_query,
            gain_latent,
            w_qa,
            w_kva,
            turned,
        ],
        [
            half_of(ROPE, f32),
            half_of(ROPE, f32),
            half_of(width, bf16),
            half_of(lat_width, bf16),
            half_of(qrank, f32),
            half_of(kvrank, f32),
            half_of(width, bf16),
            half_of(width, bf16),
            half_of(width, bf16),
        ]
        + [half_of(nz * block, bf16)] * nc,
        [pltpu.VMEM((half, width), bf16)] * 2,
        flops=2 * half * width * (qrank + kvrank),
    )
    own_cos, own_sin, _, latents, q_latent, kv_latent, own_tokens, own_cotangent, grad_mlp = outs[:9]
    normed_parts = outs[9:]
    lat_parts = along_ctx(latents)

    out_parts[0] = after(out_parts[0], latents)
    own_out = stack_blocks(out_parts, 2)[0]
    down_parts[0] = after(down_parts[0], own_out, wide_qb, wide_kvb)
    down = gather_weights(down_parts)
    out_pieces = gather_dp(after(own_out, down_parts[1], down_parts[2], down_parts[3]))
    lat_parts[0] = after(lat_parts[0], out_pieces[1])
    lat_own = jnp.stack(lat_parts)
    lat_oth = swap(lat_own)
    pair_parts = weight_parts(after(w_gate, out_pieces[2]), w_up)
    o_own, o_oth, q_rot, keys, values, qn, kvn, cos_table, sin_table = attend(
        nt, ids, lat_own, lat_oth, after(wide_qb, out_pieces[2]), wide_kvb, segments
    )
    out_pieces[0] = after(out_pieces[0], o_own)
    full_out = plain(
        functools.partial(spread_kernel, heads, nz),
        ids,
        out_pieces,
        [((nc, nz, block, heads * LANES), bf16)],
    )[0].reshape(width, heads * LANES)
    keep, give = project_out(o_own, o_oth, full_out)
    pair_parts[0] = after(pair_parts[0], keep)
    pair = gather_weights(pair_parts)
    gm = gather_dp(after(grad_mlp, *pair_parts[1:]))
    attn = reduce_ctx(keep, give)
    resid, normed_mid = plain(
        functools.partial(middle_kernel, len(attn)),
        ids,
        attn + [own_tokens, gain_middle],
        [half_of(width, f32), half_of(width, bf16)],
    )
    nm = gather_dp(after(normed_mid, gm[1]))
    groups = [range(0, nz // 2), range(nz // 2, nz)]
    nm_all, gm_all, hidden, grad_gate, grad_up, grad_parts, mlp_parts = [], [], [], [], [], [], []
    for group in groups:
        nm_own = jnp.concatenate([nm[k] for k in group])
        gm_own = jnp.concatenate([gm[k] for k in group])
        if hidden:
            nm_own = after(nm_own, hidden[0])
        nm_oth, gm_oth = swap(nm_own), swap(gm_own)
        nm_all += [nm_own, nm_oth]
        gm_all += [gm_own, gm_oth]
        hid, gg, gu, gn_own, gn_oth, ml_own, ml_oth = feed_forward(
            nc, nm_own, nm_oth, gm_own, gm_oth, pair, down
        )
        hidden.append(hid)
        grad_gate.append(gg)
        grad_up.append(gu)
        for parts, own, oth in ((grad_parts, gn_own, gn_oth), (mlp_parts, ml_own, ml_oth)):
            total = (own.astype(f32) + swap(oth).astype(f32)).astype(bf16)
            parts += [total[i * half : (i + 1) * half] for i in range(len(group))]
    grad_normed = scatter_dp(grad_parts)
    gm_all[0] = after(gm_all[0], grad_normed[1])
    down_product = products(gm_all, [hidden], nc)
    down_product = scatter_weights(down_product)
    nm_all[0] = after(nm_all[0], grad_normed[3])
    pair_product = products(nm_all, [grad_gate, grad_up], nc)
    grad_normed[0] = after(grad_normed[0], pair_product)

    grad_resid, grad_attn, grad_gain_mlp = plain(
        functools.partial(back_middle_kernel, nz),
        ids,
        grad_normed + [resid, own_cotangent, gain_middle],
        [half_of(width, f32), half_of(width, bf16), ((1, width), f32)],
    )
    ga_parts = along_ctx(grad_attn)
    mlp_parts = scatter_dp([after(part, grad_attn) for part in mlp_parts])
    ga_own = jnp.stack(ga_parts)
    ga_oth = swap(ga_own)
    pair_product = scatter_weights(after(pair_product, ga_own))
    g_own, g_oth = project_heads(ga_own, ga_oth, full_out)
    grad_q, grad_kv = attend_back(
        nt, ids, q_rot, keys, values, o_own, o_oth, g_own, g_oth, cos_table, sin_table
    )
    mlp_parts[0] = after(mlp_parts[0], grad_q)
    layer_out = plain(
        functools.partial(leave_kernel, sizes, block, nz),
        ids,
        mlp_parts + [resid],
        [half_of(width, bf16)],
        [pltpu.VMEM((half, width), f32)],
    )[0]
    (grad_w_down,) = weight_rows(after(down_product, *mlp_parts))
    grad_lat = reduce_ctx(*grad_latent(sizes, ids, grad_q, grad_kv, wide_qb, wide_kvb))

    ups = grad_ups(qn, after(kvn, grad_lat[0]), grad_q, grad_kv)
    deep = ups.shape[0] // nz
    ups = ups.reshape(nz, deep, heads * LANES)
    ups = scatter_dp([pick(ups, z ^ k) for k in range(nz)])
    out_product = grad_out_weight(
        sizes, block, ids, ga_own, after(ga_oth, grad_lat[0], ups[0]), o_own, o_oth
    )
    grad_lat[0] = after(grad_lat[0], out_product)
    grad_lat, grad_gain_q, grad_gain_kv = plain(
        functools.partial(grad_enter_kernel, len(grad_lat)),
        ids,
        grad_lat + [q_latent, kv_latent, gain_query, gain_latent, own_cos, own_sin, turned],
        [half_of(lat_width, bf16), ((1, qrank), f32), ((1, KVRANK), f32)],
    )
    gl_parts = along_ctx(grad_lat)
    grad_tokens, grad_gain_attn = plain(
        functools.partial(grad_tokens_kernel, sizes, block),
        ids,
        [grad_lat, w_qa, w_kva, tokens[0], gain_in, grad_resid],
        [half_of(width, bf16), ((1, width), f32)],
        [pltpu.VMEM((half, width), f32)],
        flops=2 * half * width * (qrank + kvrank),
    )
    ups[0] = after(ups[0], grad_lat)
    own = sum(p.astype(f32) for p in ups).astype(bf16)
    ups = gather_dp(own)
    out_parts = scatter_dp([out_product[k] for k in range(nz)])
    gl_parts[0] = after(gl_parts[0], grad_tokens)
    gl_own = jnp.stack(gl_parts)
    gl_oth = swap(gl_own)

    xin_own = jnp.stack(across(normed_parts, "ctx", nc))
    xin_oth = swap(xin_own)
    share = lat_width // nt // LANES * LANES
    wide = lat_width - share
    parts = plain(
        functools.partial(grad_down_kernel, share),
        ids,
        [xin_own, xin_oth, gl_own, gl_oth],
        [((nz, block, wide), bf16)],
        flops=2 * length * nz * block * wide,
    )[0]
    ups[0] = after(ups[0], parts)
    ups = stack_blocks([piece[None] for piece in ups], 1).reshape(nz * deep, heads * LANES)
    ups = along_ctx(ups)
    out_parts[0] = after(out_parts[0], parts)
    own = sum(p.astype(f32) for p in out_parts).astype(bf16)
    out_parts = across([pick(own, c ^ k)[None] for k in range(nc)], "ctx", nc)
    own = scatter_dp([parts[k] for k in range(nz)])
    grad_w_gate, grad_w_up = weight_rows(after(pair_product, own[-1]))
    own = sum(p.astype(f32) for p in own).astype(bf16)
    grad_w_qa, grad_w_kva = plain(
        functools.partial(finish_down_kernel, share),
        ids,
        [own, swap(own)],
        [((block, qrank), f32), ((block, kvrank), f32)],
    )
    (grad_w_o,) = join_columns(out_parts, "ctx", 2)
    grad_w_qb, grad_w_kvb = plain(
        functools.partial(finish_ups_kernel, heads, nc),
        ids,
        [jnp.stack(ups)],
        [((qrank, nc * heads * (NOPE + ROPE)), f32), ((KVRANK, nc * heads * LANES), f32)],
    )
    layer_out = join_rows(layer_out)
    grad_tokens = join_rows(grad_tokens)

    turned_gain = jnp.swapaxes(grad_gain_mlp.reshape(nc, nz, block), 0, 1).reshape(1, width)
    gains = jnp.concatenate([grad_gain_attn, grad_gain_q, grad_gain_kv, turned_gain], axis=1)
    gains = gains.reshape(-1, LANES)
    for axis, size in (("tensor", nt), ("ctx", nc), ("dp", nz)):
        step = 1
        while step < size:
            gains = gains + exchange(gains, axis, step, size)
            step *= 2
    gains = gains.reshape(-1)
    ends = np.cumsum([width, qrank, KVRANK])
    grad_gain_attn, grad_gain_q, grad_gain_kv, grad_gain_mlp = jnp.split(gains, ends)
    return (
        layer_out,
        grad_tokens,
        grad_gain_attn,
        grad_w_qa,
        grad_gain_q,
        grad_w_kva,
        grad_gain_kv,
        grad_w_qb,
        grad_w_kvb,
        grad_w_o,
        grad_gain_mlp,
        grad_w_gate,
        grad_w_up,
        grad_w_down,
    )


def solution(mesh):
    placed = (
        P("dp", "ctx", None),
        P("dp", None),
        P(),
        P(),
        P(),
        P(),
        P(),
        P(None, "tensor"),
        P(None, "tensor"),
        P(("dp", "ctx"), "tensor"),
        P(),
        P(("dp", "ctx"), "tensor"),
        P(("dp", "ctx"), "tensor"),
        P(("dp", "ctx"), "tensor"),
        P("dp", "ctx", None),
    )
    sizes = tuple(mesh.shape[name] for name in ("tensor", "dp", "ctx"))
    return jax.shard_map(
        functools.partial(body, sizes),
        mesh=mesh,
        in_specs=placed,
        out_specs=(
            P("dp", "ctx", None),
            P("dp", "ctx", None),
            P(),
            P(("dp", "ctx"), None),
            P(),
            P(("dp", "ctx"), None),
            P(),
            P(None, "tensor"),
            P(None, "tensor"),
            P(("dp", "ctx"), "tensor"),
            P(),
            P(("dp", "ctx"), "tensor"),
            P(("dp", "ctx"), "tensor"),
            P(("dp", "ctx"), "tensor"),
        ),
        check_vma=False,
    )
```
